128 devices in a mesh: section: 2 (over z_lo), tensor: 2 (over core), dp: 32 (over y, z_hi, x).
Axes of the slice: x: 4, y: 4, z: 4 (z_hi: 2, z_lo: 2; z = z_hi * 2 + z_lo), core: 2. Of those that a mesh axis runs over, the one named last changes fastest.
Arguments:
- tokens: bfloat16 [2, 8192, 1024], P(None, ('tensor', 'dp')), may hold values from -6 to 6
- cotangent: bfloat16 [2, 8192, 1024], P(None, ('tensor', 'dp')), may hold values from -6 to 6
- doc_lengths: int32 [2, 4, 4], replicated, may hold values from 1 to 1792, 2048 in all within a row
- gains: float32 [2, 2, 1024], P('section'), may hold values from 0.5 to 1.5
- wqkv: bfloat16 [2, 1024, 3, 1024], P('section', None, None, 'tensor'), may hold values from -0.1875 to 0.1875
- wo: bfloat16 [2, 1024, 1024], P('section', 'tensor'), may hold values from -2 to 2
- wgu: bfloat16 [2, 1024, 2, 2816], P('section', None, None, 'tensor'), may hold values from -0.1875 to 0.1875
- wd: bfloat16 [2, 2816, 1024], P('section', 'tensor'), may hold values from -0.109375 to 0.109375
Outputs:
- acts: bfloat16 [2, 2, 8192, 1024], P('section', None, ('tensor', 'dp'))
- dins: float32 [2, 2, 8192, 1024], P('section', None, ('tensor', 'dp'))
- grad_qkv: float32 [2, 1024, 3, 1024], P('section', 'dp', None, 'tensor')
- grad_out_proj: float32 [2, 1024, 1024], P('section', ('tensor', 'dp'))
- grad_gate_up: float32 [2, 1024, 2, 2816], P('section', 'dp', None, 'tensor')
- grad_down: float32 [2, 2816, 1024], P('section', ('tensor', 'dp'))
- grad_gains: float32 [2, 2, 1024], P('section')
The draws below stay inside these ranges and needn't reach their ends.
Inputs may be any that keep to these rules, and one draw needn't show every extreme that they name: `doc_lengths`: in each sequence one document has exactly 1792 tokens.
All inputs are finite; a program needn't handle non-finite values.
Results may differ from the reference program's by a relative error of at most 0.04.
Values may be sent and summed in bfloat16 or wider, within the bound.
No kernel may reach another device: no remote copies, remote signals or barrier semaphores. Data moves between devices by JAX's collectives and lax.ppermute only.
A program may use at most 256 MiB of HBM per device.

```python
import math
import jax
import jax.numpy as jnp
import numpy as np
from jax import lax

D = 1024
HEADS = 16
HD = 64
FF = 2816
LEN = 2048
SPLIT = 8
DOCS = 4
SEQS = 2
GROUPS = 4
ROWS = 256
SUB = 128
TOT = 8192
N_TENSOR = 2


def shard_levels(stream_key, extent, shards, smallest, largest):
    def one(position, parts):
        heights = jax.random.uniform(jax.random.fold_in(jax.random.fold_in(stream_key, 6), position), (parts,), jnp.float32, smallest / len(shards), largest / len(shards))
        return jnp.repeat(jnp.exp(heights), extent[position] // parts).reshape((-1,) + (1,) * (len(extent) - position - 1))

    level = one(*shards[0])
    for cut in shards[1:]:
        level = level * one(*cut)
    return level


def profile(count, total, bound, lean):
    portions = [(1 << 20) // math.isqrt(grade ** lean) + 1 for grade in range(2, count + 1)]
    surplus, counts = total - bound - (count - 1), [1] * (count - 1)
    while surplus > 0:
        candidates = [i for i in range(count - 1) if counts[i] < bound]
        whole, left = sum([portions[i] for i in candidates]), surplus
        for i in candidates:
            extra = min(bound - counts[i], max(1, left * portions[i] // whole), surplus)
            counts[i] = counts[i] + extra
            surplus = surplus - extra
    return np.array([bound] + counts)


def ragged_sizes(rng, count, total, reach, lean):
    if count == 2:
        one = jax.random.randint(rng, (), max(1, total - reach), min(reach, total - 1) + 1)
        return jnp.stack([one, total - one])
    lengths = jnp.asarray(profile(count, total, reach, lean), jnp.int32)
    pairs = (count - 1) // 2
    giver, sink = lengths[1:1 + 2 * pairs:2], lengths[2:2 + 2 * pairs:2]
    margin = jnp.minimum(giver - 1, reach - sink)
    shifted = jax.random.randint(jax.random.fold_in(rng, 1), (pairs,), 0, 1 << 20) % (margin + 1)
    lengths = lengths.at[1:1 + 2 * pairs:2].set(giver - shifted).at[2:2 + 2 * pairs:2].set(sink + shifted)
    return lengths[jax.random.permutation(jax.random.fold_in(rng, 2), count)]


def gaussian(rng, shape, spread, limit, split=(), kind=jnp.bfloat16):
    values = spread * jax.random.normal(rng, shape, jnp.float32)
    if split:
        values = values * shard_levels(rng, shape, split, -0.22, 0.18)
    return jnp.clip(values, -limit, limit).astype(kind)


def setup_inputs(seed: int = 0) -> dict:
    seeds = jax.random.split(jax.random.key(seed), 9)
    tokens = gaussian(seeds[0], (SEQS, TOT, D), 1.0, 6.0, ((1, 64),))
    cotangent = gaussian(seeds[1], (SEQS, TOT, D), 1.0, 6.0, ((1, 64),))
    doc_lengths = jax.vmap(lambda own: ragged_sizes(own, DOCS, LEN, 7 * LEN // 8, 2))(jax.random.split(seeds[2], SEQS * GROUPS)).reshape((SEQS, GROUPS, DOCS)).astype(jnp.int32)
    gains = jnp.clip(1.0 + 0.1 * jax.random.normal(seeds[3], (2, 2, D), jnp.float32), 0.5, 1.5)
    wqkv = gaussian(seeds[4], (2, D, 3, D), D ** -0.5, 0.1875, ((0, 2), (3, 2)))
    wo = gaussian(seeds[5], (2, D, D), (max(D // 128, 1)) ** -0.5, 2.0, ((0, 2), (1, 2)))
    wgu = gaussian(seeds[6], (2, D, 2, FF), D ** -0.5, 0.1875, ((0, 2), (3, 2)))
    wd = gaussian(seeds[7], (2, FF, D), FF ** -0.5, 0.109375, ((0, 2), (1, 2)))
    return {"tokens": tokens, "cotangent": cotangent, "doc_lengths": doc_lengths, "gains": gains, "wqkv": wqkv, "wo": wo, "wgu": wgu, "wd": wd}


EPSILON = 1e-06
NEGATIVE = -1e+30
HIGHEST = lax.Precision.HIGHEST

@jax.custom_vjp
def low(v):
    return lax.optimization_barrier(v.astype(jnp.bfloat16)).astype(jnp.float32)

@jax.custom_vjp
def low_back(v):
    return v

def low_keep(v):
    return (low(v), None)

def low_pass(kept, grad):
    return (grad,)

def back_keep(v):
    return (v, None)

def back_low(kept, grad):
    return (low(grad),)
low.defvjp(low_keep, low_pass)
low_back.defvjp(back_keep, back_low)

def rms_scale(hidden):
    return lax.rsqrt(lax.optimization_barrier(jnp.mean(hidden * hidden, axis=-1, keepdims=True)) + EPSILON)

def rotary_tables(start, count):
    places = (start + jnp.arange(count, dtype=jnp.int32)).astype(jnp.float32)
    half = HD // 2
    freqs = 10000.0 ** (-jnp.arange(half, dtype=jnp.float32) / half)
    angles = places[:, None] * freqs[None, :]
    return (jnp.cos(angles)[:, None, :], jnp.sin(angles)[:, None, :])

def rotate(vectors, tables):
    cosine, sine = tables
    half = vectors.shape[-1] // 2
    first = vectors[..., :half]
    second = vectors[..., half:]
    return jnp.concatenate([first * cosine - second * sine, second * cosine + first * sine], axis=-1)

def block_forward(hidden, gain_pair, w_qkv, w_out, w_gu, w_down, visible, tables, value_first):
    normed = low(hidden * rms_scale(hidden) * gain_pair[0])
    projected = low_back(jnp.einsum('td,dcf->tcf', normed, w_qkv, precision=HIGHEST))
    queries = low(rotate(projected[:, 0].reshape(LEN, HEADS, HD), tables))
    keys_all = low(rotate(projected[:, 1].reshape(LEN, HEADS, HD), tables))
    values_raw = projected[:, 2]
    if value_first is None:
        values = low(values_raw)
    else:
        values = low(0.5 * values_raw + 0.5 * value_first)
    scores = low_back(jnp.einsum('qhd,khd->hqk', queries, keys_all, precision=HIGHEST) * HD ** (-0.5))
    scores = jnp.where(visible[None], scores, NEGATIVE)
    highest = lax.optimization_barrier(jnp.max(scores, axis=-1, keepdims=True))
    expd = jnp.exp(scores - highest)
    attend = expd / lax.optimization_barrier(jnp.sum(expd, axis=-1, keepdims=True))
    attended = jnp.einsum('hqk,khd->qhd', low(attend), values.reshape(LEN, HEADS, HD), precision=HIGHEST)
    attended = low_back(low(attended.reshape(LEN, D)))
    middle = hidden + low_back(jnp.dot(attended, w_out, precision=HIGHEST))
    normed_two = low(middle * rms_scale(middle) * gain_pair[1])
    gate_up = low_back(jnp.einsum('td,dcf->tcf', normed_two, w_gu, precision=HIGHEST))
    activated = low(jax.nn.silu(gate_up[:, 0]) * gate_up[:, 1])
    return (middle + low_back(jnp.dot(activated, w_down, precision=HIGHEST)), values)

def sequence_forward(params, item):
    gain_all, w_qkv, w_out, w_gu, w_down = params
    inputs, lens_row, probe = item
    ends = jnp.cumsum(lens_row, dtype=jnp.int32)
    places = jnp.arange(LEN, dtype=jnp.int32)
    docs = lax.optimization_barrier(jnp.sum((places[:, None] >= ends[None, :]).astype(jnp.int32), axis=1, dtype=jnp.int32))
    visible = (places[None, :] <= places[:, None]) & (docs[None, :] == docs[:, None])
    tables = rotary_tables(0, LEN)
    first_out, first_values = block_forward(inputs, gain_all[0], w_qkv[0], w_out[0], w_gu[0], w_down[0], visible, tables, None)
    handed = low(first_out)
    second_out, unused = block_forward(low_back(handed) + probe, gain_all[1], w_qkv[1], w_out[1], w_gu[1], w_down[1], visible, tables, low_back(first_values))
    return (second_out, handed)

def place_of_local():
    local = jnp.arange(LEN, dtype=jnp.int32)
    quarter = local // ROWS
    within = local % ROWS
    half = ROWS // 2
    block = jnp.where(within < half, quarter, 2 * SPLIT - 1 - quarter)
    return (block * half + within % half).astype(jnp.int32)

def local_of_place():
    places = jnp.arange(LEN, dtype=jnp.int32)
    half = ROWS // 2
    block = places // half
    offset = places % half
    quarter = jnp.where(block < SPLIT, block, 2 * SPLIT - 1 - block)
    within = jnp.where(block < SPLIT, offset, half + offset)
    return (quarter * ROWS + within).astype(jnp.int32)

def unpack(array):
    array = array.astype(jnp.float32).reshape(SEQS, N_TENSOR, GROUPS, SPLIT, SUB, D)
    array = array.transpose(0, 2, 3, 1, 4, 5).reshape(SEQS * GROUPS, LEN, D)
    return jnp.take(array, local_of_place(), axis=1)

def pack(array):
    array = jnp.take(array, place_of_local(), axis=1)
    array = array.reshape(SEQS, GROUPS, SPLIT, N_TENSOR, SUB, D).transpose(0, 3, 1, 2, 4, 5)
    return array.reshape(SEQS, TOT, D)

def reference(tokens, cotangent, doc_lengths, gains, wqkv, wo, wgu, wd):
    inputs = unpack(tokens)
    grad_top = unpack(cotangent)
    lens = doc_lengths.reshape(SEQS * GROUPS, DOCS)
    probe = jnp.zeros_like(inputs)
    params = (gains.astype(jnp.float32), wqkv.astype(jnp.float32), wo.astype(jnp.float32), wgu.astype(jnp.float32), wd.astype(jnp.float32))

    def forward(params, inputs, probe):

        def one_sequence(item):
            return sequence_forward(params, item)
        second, handed = lax.map(jax.checkpoint(one_sequence), (inputs, lens, probe))
        return (second, handed)
    result, pullback, handed = jax.vjp(forward, params, inputs, probe, has_aux=True)
    param_grads, grad_inputs, grad_probe = pullback(grad_top)
    acts = jnp.stack([pack(handed), pack(result)]).astype(jnp.bfloat16)
    dins = jnp.stack([pack(grad_inputs), pack(grad_probe)])
    return (acts, dins, param_grads[1], param_grads[2], param_grads[3], param_grads[4], param_grads[0])
```

```python
import functools

import jax
import jax.numpy as jnp
from jax import lax
from jax.experimental import pallas as pl
from jax.experimental.pallas import tpu as pltpu
from jax.sharding import PartitionSpec as P

HD = 64
LEN = 2048
RING = 4
BLOCK = 128
PAIR = 2 * HD
EPSILON = 1e-06
NEGATIVE = -1e30
KEYS = 256
QUERIES = 512
VMEM = 56 * 1024 * 1024
BF = jnp.bfloat16
F32 = jnp.float32


def along(kind, shift):
    pairs = []
    for index in range(32):
        y, z, x = index // 8, index // 4 % 2, index % 4
        if kind == "x":
            x = (x + shift) % 4
        elif kind == "y":
            y = (y + shift) % 4
        else:
            z = (z + shift) % 2
        pairs.append((index, y * 8 + z * 4 + x))
    return pairs


def moved(value, kind, shift):
    return lax.ppermute(value, "dp", along(kind, shift))


def swapped(value):
    return lax.ppermute(value, "tensor", [(0, 1), (1, 0)])


def rms_scale(hidden):
    return lax.rsqrt(jnp.mean(hidden * hidden, axis=-1, keepdims=True) + EPSILON)


def norm_backward(hidden, grad_normed, gain_row):
    scale_row = rms_scale(hidden)
    unit = hidden * scale_row
    weighted = grad_normed * gain_row
    grad_hidden = scale_row * (weighted - unit * jnp.mean(weighted * unit, axis=-1, keepdims=True))
    return (grad_hidden, jnp.sum(grad_normed * unit, axis=0))


def rotary_tables():
    places = jnp.arange(LEN, dtype=jnp.int32).astype(F32)
    half = HD // 2
    freqs = 10000.0 ** (-jnp.arange(half, dtype=F32) / half)
    angles = places[:, None] * freqs[None, :]
    return (jnp.tile(jnp.cos(angles), (1, 4)), jnp.tile(jnp.sin(angles), (1, 4)))


def low_lanes(shape):
    return lax.broadcasted_iota(jnp.int32, shape, 1) % HD < HD // 2


def turned(u, cosine, sine, sign):
    ahead = pltpu.roll(u, PAIR - HD // 2, 1)
    behind = pltpu.roll(u, HD // 2, 1)
    cross = jnp.where(low_lanes(u.shape), -sign * ahead, sign * behind)
    return u * cosine + cross * sine


def place_block(source, part):
    return (source, 4 + source, 15 - source, 11 - source)[part]


def project_kernel(x_ref, mix_ref, h_ref, gain_ref, w_ref, v1_ref, cos_ref, sin_ref,
                   m0, m1, m2, m3, n_ref, v_ref):
    step = pl.program_id(0)

    @pl.when(step == 0)
    def _():
        h = h_ref[...].astype(F32)
        n_ref[...] = (h * rms_scale(h) * gain_ref[...]).astype(BF)

    normed = n_ref[...]
    cosine, sine = cos_ref[...], sin_ref[...]
    query = jnp.dot(normed, w_ref[0], preferred_element_type=F32)
    query = (turned(query, cosine, sine, 1.0) * HD ** (-0.5)).astype(BF)
    key = jnp.dot(normed, w_ref[1], preferred_element_type=F32)
    key = turned(key, cosine, sine, 1.0).astype(BF)
    value = jnp.dot(normed, w_ref[2], preferred_element_type=F32)
    value = (mix_ref[0] * value + mix_ref[1] * v1_ref[0].astype(F32)).astype(BF)
    v_ref[0] = value
    for index, out in enumerate((m0, m1, m2, m3)):
        @pl.when(step == index)
        def _():
            out[0] = query
            out[1] = key
            out[2] = value


def project(x_index, mix, hidden, gain, w_qkv, value_first, cosine, sine):
    rows, width = hidden.shape
    message = jax.ShapeDtypeStruct((3, rows, PAIR), BF)
    whole = lambda *shape: pl.BlockSpec(shape, lambda i, x: (0,) * len(shape))
    return pl.pallas_call(
        project_kernel,
        grid_spec=pltpu.PrefetchScalarGridSpec(
            num_scalar_prefetch=1,
            grid=(RING,),
            in_specs=[
                pl.BlockSpec(memory_space=pltpu.SMEM),
                whole(rows, width),
                whole(1, width),
                pl.BlockSpec((3, width, PAIR), lambda i, x: (0, 0, (i + x[0]) % RING)),
                pl.BlockSpec((1, rows, PAIR), lambda i, x: (i, 0, 0)),
                whole(rows, PAIR),
                whole(rows, PAIR),
            ],
            out_specs=[whole(3, rows, PAIR)] * 4
            + [whole(rows, width), pl.BlockSpec((1, rows, PAIR), lambda i, x: (i, 0, 0))],
        ),
        out_shape=[message] * 4
        + [jax.ShapeDtypeStruct((rows, width), BF), jax.ShapeDtypeStruct((RING, rows, PAIR), BF)],
        compiler_params=pltpu.CompilerParams(vmem_limit_bytes=VMEM),
        cost_estimate=pl.CostEstimate(
            flops=2 * rows * width * 12 * PAIR, bytes_accessed=8 * 1024 * 1024, transcendentals=0
        ),
        name="project",
    )(x_index, mix, hidden, gain, w_qkv, value_first, cosine, sine)


def first_visible(ends_ref, places):
    start = jnp.zeros_like(places)
    for index in range(4):
        start = jnp.where(places >= ends_ref[index], ends_ref[index], start)
    return start


def attend_kernel(x_ref, ends_ref, m0, m1, m2, m3, o0, o1, o2, o3, lse_ref, out_t, keys, query_t,
                  value_t, acc):
    x = x_ref[0]
    lanes = lax.broadcasted_iota(jnp.int32, (BLOCK, PAIR), 1)
    for shift, message in enumerate((m0, m1, m2, m3)):
        source = lax.rem(x + RING - shift, RING)
        for part in range(4):
            at = pl.ds(pl.multiple_of(place_block(source, part) * BLOCK, BLOCK), BLOCK)
            inside = slice(part * BLOCK, (part + 1) * BLOCK)
            block = message[1, inside, :]
            keys[0, at, :] = jnp.where(lanes < HD, block, jnp.zeros_like(block))
            keys[1, at, :] = jnp.where(lanes < HD, jnp.zeros_like(block), block)
            query_t[:, at] = message[0, inside, :].T
            value_t[:, at] = message[2, inside, :].T

    def one_query_block(qi, _):
        q_at = pl.ds(pl.multiple_of(qi * QUERIES, QUERIES), QUERIES)
        places = qi * QUERIES + lax.broadcasted_iota(jnp.int32, (1, QUERIES), 1)
        start = first_visible(ends_ref, places)
        acc[...] = jnp.zeros_like(acc)

        def one_key_block(kj, carry):
            k_at = pl.ds(pl.multiple_of(kj * KEYS, KEYS), KEYS)
            key_places = kj * KEYS + lax.broadcasted_iota(jnp.int32, (KEYS, QUERIES), 0)
            visible = (key_places <= places) & (key_places >= start)
            after = []
            for head in range(2):
                highest, total = carry[head]
                scores = jnp.dot(keys[head, k_at, :], query_t[:, q_at], preferred_element_type=F32)
                scores = jnp.where(visible, scores, NEGATIVE)
                higher = jnp.maximum(highest, jnp.max(scores, axis=0, keepdims=True))
                shrink = jnp.exp(highest - higher)
                weight = jnp.exp(scores - higher)
                total = total * shrink + jnp.sum(weight, axis=0, keepdims=True)
                part = slice(head * HD, (head + 1) * HD)
                acc[part, :] = acc[part, :] * shrink + jnp.dot(
                    value_t[part, k_at], weight.astype(BF), preferred_element_type=F32
                )
                after.append((higher, total))
            return tuple(after)

        begin = (jnp.full((1, QUERIES), NEGATIVE, F32), jnp.zeros((1, QUERIES), F32))
        done = lax.fori_loop(0, (qi + 1) * (QUERIES // KEYS), one_key_block, (begin, begin))
        for head in range(2):
            highest, total = done[head]
            part = slice(head * HD, (head + 1) * HD)
            out_t[part, q_at] = acc[part, :] / total
            lse_ref[head : head + 1, q_at] = highest + jnp.log(total)
        return 0

    lax.fori_loop(0, LEN // QUERIES, one_query_block, 0)
    for shift, out in enumerate((o0, o1, o2, o3)):
        source = lax.rem(x + RING - shift, RING)
        for part in range(4):
            at = pl.ds(pl.multiple_of(place_block(source, part) * BLOCK, BLOCK), BLOCK)
            out[part * BLOCK : (part + 1) * BLOCK, :] = out_t[:, at].T.astype(BF)


def attend(x_index, ends, messages):
    rows = messages[0].shape[1]
    smem = pl.BlockSpec(memory_space=pltpu.SMEM)
    vmem = pl.BlockSpec(memory_space=pltpu.VMEM)
    return pl.pallas_call(
        attend_kernel,
        in_specs=[smem, smem] + [vmem] * 4,
        out_specs=[vmem] * 6,
        out_shape=[jax.ShapeDtypeStruct((rows, PAIR), BF)] * 4
        + [jax.ShapeDtypeStruct((2, LEN), F32), jax.ShapeDtypeStruct((PAIR, LEN), F32)],
        scratch_shapes=[
            pltpu.VMEM((2, LEN, PAIR), BF),
            pltpu.VMEM((PAIR, LEN), BF),
            pltpu.VMEM((PAIR, LEN), BF),
            pltpu.VMEM((PAIR, QUERIES), F32),
        ],
        compiler_params=pltpu.CompilerParams(vmem_limit_bytes=VMEM),
        cost_estimate=pl.CostEstimate(
            flops=8 * LEN * LEN * HD, bytes_accessed=4 * 1024 * 1024, transcendentals=LEN * LEN
        ),
        name="attend",
    )(x_index, ends, *messages)


def attend_back_kernel(x_ref, ends_ref, mix_ref, m0, m1, m2, m3, d0, d1, d2, d3, lse_ref, out_t,
                       dv1_ref, cos_ref, sin_ref, g0, g1, g2, g3, keys, values, queries, grads,
                       key_t, query_t, grad_t, delta, grad_k, grad_v, grad_q_t):
    x = x_ref[0]
    lanes = lax.broadcasted_iota(jnp.int32, (BLOCK, PAIR), 1)
    for shift, (message, arrived) in enumerate(((m0, d0), (m1, d1), (m2, d2), (m3, d3))):
        source = lax.rem(x + RING - shift, RING)
        for part in range(4):
            at = pl.ds(pl.multiple_of(place_block(source, part) * BLOCK, BLOCK), BLOCK)
            inside = slice(part * BLOCK, (part + 1) * BLOCK)
            query, key, value = message[0, inside, :], message[1, inside, :], message[2, inside, :]
            grad = arrived[inside, :]
            zero = jnp.zeros_like(query)
            for both, block in ((keys, key), (values, value), (queries, query), (grads, grad)):
                both[0, at, :] = jnp.where(lanes < HD, block, zero)
                both[1, at, :] = jnp.where(lanes < HD, zero, block)
            key_t[:, at] = key.T
            query_t[:, at] = query.T
            turned_grad = grad.T
            grad_t[:, at] = turned_grad
            product = out_t[:, at] * turned_grad.astype(F32)
            delta[0:1, at] = jnp.sum(product[:HD], axis=0, keepdims=True)
            delta[1:2, at] = jnp.sum(product[HD:], axis=0, keepdims=True)
    grad_k[...] = jnp.zeros_like(grad_k)
    grad_v[...] = jnp.zeros_like(grad_v)
    grad_q_t[...] = jnp.zeros_like(grad_q_t)

    def one_query_block(qi, _):
        q_at = pl.ds(pl.multiple_of(qi * QUERIES, QUERIES), QUERIES)
        places = qi * QUERIES + lax.broadcasted_iota(jnp.int32, (1, QUERIES), 1)
        start = first_visible(ends_ref, places)

        def one_key_block(kj, carry):
            k_at = pl.ds(pl.multiple_of(kj * KEYS, KEYS), KEYS)
            key_places = kj * KEYS + lax.broadcasted_iota(jnp.int32, (KEYS, QUERIES), 0)
            visible = (key_places <= places) & (key_places >= start)
            for head in range(2):
                part = slice(head * HD, (head + 1) * HD)
                scores = jnp.dot(keys[head, k_at, :], query_t[:, q_at], preferred_element_type=F32)
                scores = jnp.where(visible, scores, NEGATIVE)
                weight = jnp.exp(scores - lse_ref[head : head + 1, q_at])
                grad_w = jnp.dot(values[head, k_at, :], grad_t[:, q_at], preferred_element_type=F32)
                grad_s = (weight * (grad_w - delta[head : head + 1, q_at])).astype(BF)
                grad_v[k_at, :] += jnp.dot(
                    weight.astype(BF), grads[head, q_at, :], preferred_element_type=F32
                )
                grad_k[k_at, :] += jnp.dot(grad_s, queries[head, q_at, :], preferred_element_type=F32)
                grad_q_t[part, q_at] += jnp.dot(
                    key_t[part, k_at], grad_s, preferred_element_type=F32
                )
            return carry

        return lax.fori_loop(0, (qi + 1) * (QUERIES // KEYS), one_key_block, 0)

    lax.fori_loop(0, LEN // QUERIES, one_query_block, 0)
    for shift, out in enumerate((g0, g1, g2, g3)):
        source = lax.rem(x + RING - shift, RING)
        for part in range(4):
            at = pl.ds(pl.multiple_of(place_block(source, part) * BLOCK, BLOCK), BLOCK)
            inside = slice(part * BLOCK, (part + 1) * BLOCK)
            cosine, sine = cos_ref[at, :], sin_ref[at, :]
            grad_q = grad_q_t[:, at].T * HD ** (-0.5)
            out[0, inside, :] = turned(grad_q, cosine, sine, -1.0).astype(BF)
            out[1, inside, :] = turned(grad_k[at, :], cosine, sine, -1.0).astype(BF)
            out[2, inside, :] = (
                mix_ref[0] * grad_v[at, :] + mix_ref[1] * dv1_ref[shift, inside, :].astype(F32)
            ).astype(BF)


def attend_back(x_index, ends, mix, messages, arrived, lse, out_t, dv1, cosine, sine):
    rows = messages[0].shape[1]
    smem = pl.BlockSpec(memory_space=pltpu.SMEM)
    vmem = pl.BlockSpec(memory_space=pltpu.VMEM)
    return pl.pallas_call(
        attend_back_kernel,
        in_specs=[smem] * 3 + [vmem] * 13,
        out_specs=[vmem] * 4,
        out_shape=[jax.ShapeDtypeStruct((3, rows, PAIR), BF)] * 4,
        scratch_shapes=[pltpu.VMEM((2, LEN, PAIR), BF)] * 4
        + [pltpu.VMEM((PAIR, LEN), BF)] * 3
        + [
            pltpu.VMEM((2, LEN), F32),
            pltpu.VMEM((LEN, PAIR), F32),
            pltpu.VMEM((LEN, PAIR), F32),
            pltpu.VMEM((PAIR, LEN), F32),
        ],
        compiler_params=pltpu.CompilerParams(vmem_limit_bytes=VMEM),
        cost_estimate=pl.CostEstimate(
            flops=20 * LEN * LEN * HD, bytes_accessed=8 * 1024 * 1024, transcendentals=LEN * LEN
        ),
        name="attend_back",
    )(x_index, ends, mix, *messages, *arrived, lse, out_t, dv1, cosine, sine)


def out_and_back(values, sign):
    return [values[0]] + [moved(values[shift], "x", sign * shift) for shift in range(1, RING)]


def per_device(tokens, cotangent, doc_lengths, gains, wqkv, wo, wgu, wd):
    first = lax.axis_index("section") == 0
    tensor = lax.axis_index("tensor")
    position = lax.axis_index("dp")
    y, z, x = position // 8, position // 4 % 2, position % 4
    x_index = x.astype(jnp.int32).reshape(1)
    width = tokens.shape[2]

    def held_and_got(pair):
        keep = lax.dynamic_index_in_dim(pair, z, 0, keepdims=False)
        send = lax.dynamic_index_in_dim(pair, 1 - z, 0, keepdims=False)
        got = moved(send.astype(BF), "z", 1).astype(pair.dtype)
        return jnp.where(z == 0, jnp.stack([keep, got]), jnp.stack([got, keep]))

    def both_cores(rows):
        other = swapped(rows)
        return jnp.where(
            tensor == 0, jnp.concatenate([rows, other]), jnp.concatenate([other, rows])
        )

    def own_half(full):
        half = full.shape[0] // 2
        return lax.dynamic_slice_in_dim(full, tensor * half, half, 0)

    lens = lax.dynamic_slice(doc_lengths, (z, y, 0), (1, 1, 4))
    ends = jnp.cumsum(lens.reshape(4), dtype=jnp.int32)
    cosine, sine = rotary_tables()
    blocks = [place_block(x, part) for part in range(4)]
    own_cos, own_sin = [
        jnp.concatenate([lax.dynamic_slice_in_dim(table, b * BLOCK, BLOCK, 0) for b in blocks])
        for table in (cosine, sine)
    ]
    w_qkv = jnp.transpose(wqkv[0], (1, 0, 2))
    w_out = jnp.concatenate(
        [lax.dynamic_slice_in_dim(wo[0], (x + k) % 4 * PAIR, PAIR, 0) for k in range(RING)]
    )
    w_gate, w_up = wgu[0, :, 0], wgu[0, :, 1]
    w_down = wd[0]
    gain_one, gain_two = gains[0, 0:1], gains[0, 1:2]
    mix = jnp.where(first, jnp.array([1.0, 0.0], F32), jnp.array([0.5, 0.5], F32))
    mix_back = jnp.where(first, jnp.array([1.0, 1.0], F32), jnp.array([0.5, 0.0], F32))

    def forward(hidden, value_first):
        *messages, normed, value = project(
            x_index, mix, hidden, gain_one, w_qkv, value_first, own_cos, own_sin
        )
        messages = out_and_back(messages, 1)
        *outs, lse, out_t = attend(x_index, ends, messages)
        attended = jnp.concatenate(out_and_back(outs, -1), axis=1)
        branch = jnp.dot(attended, w_out, preferred_element_type=F32).astype(BF)
        middle = hidden.astype(F32) + (branch.astype(F32) + swapped(branch).astype(F32))
        normed_two = (middle * rms_scale(middle) * gain_two).astype(BF)
        gate = jnp.dot(normed_two, w_gate, preferred_element_type=F32)
        up = jnp.dot(normed_two, w_up, preferred_element_type=F32)
        activated = (jax.nn.silu(gate) * up).astype(BF)
        feed = jnp.dot(activated, w_down, preferred_element_type=F32).astype(BF)
        result = middle + (feed.astype(F32) + swapped(feed).astype(F32))
        saved = (hidden, normed, messages, lse, out_t, attended, middle, normed_two, gate, up, activated)
        return (result.astype(BF), value, saved)

    def backward(grad_out, grad_value_first, saved):
        hidden, normed, messages, lse, out_t, attended, middle, normed_two, gate, up, activated = saved
        hidden = hidden.astype(F32)
        grad_feed = grad_out.astype(BF)
        grad_act = jnp.einsum("td,fd->tf", grad_feed, w_down, preferred_element_type=F32)
        sigma = jax.nn.sigmoid(gate)
        grad_gate = (grad_act * up * sigma * (1.0 + gate * (1.0 - sigma))).astype(BF)
        grad_up = (grad_act * gate * sigma).astype(BF)
        part = (
            jnp.einsum("tf,df->td", grad_gate, w_gate, preferred_element_type=F32)
            + jnp.einsum("tf,df->td", grad_up, w_up, preferred_element_type=F32)
        ).astype(BF)
        grad_normed_two = part.astype(F32) + swapped(part).astype(F32)
        grad_mid, gain_grad_two = norm_backward(middle, grad_normed_two, gain_two)
        grad_middle = grad_out.astype(F32) + grad_mid
        grad_branch = grad_middle.astype(BF)
        grad_attended = jnp.einsum("td,fd->tf", grad_branch, w_out, preferred_element_type=F32)
        grad_attended = grad_attended.astype(BF)
        arrived = out_and_back([grad_attended[:, k * PAIR : (k + 1) * PAIR] for k in range(RING)], 1)
        grads = attend_back(
            x_index, ends, mix_back, messages, arrived, lse, out_t, grad_value_first, cosine, sine
        )
        grad_value_send = jnp.stack([grad[2] for grad in grads])
        grads = out_and_back(grads, -1)
        grad_proj = [
            jnp.concatenate([grads[k][c] for k in range(RING)], axis=1) for c in range(3)
        ]
        w_rel = [
            jnp.concatenate(
                [
                    lax.dynamic_slice_in_dim(w_qkv[c], (x + k) % 4 * PAIR, PAIR, 1)
                    for k in range(RING)
                ],
                axis=1,
            )
            for c in range(3)
        ]
        part = sum(
            jnp.einsum("tf,df->td", grad_proj[c], w_rel[c], preferred_element_type=F32)
            for c in range(3)
        ).astype(BF)
        grad_normed = part.astype(F32) + swapped(part).astype(F32)
        grad_in, gain_grad_one = norm_backward(hidden, grad_normed, gain_one)
        grad_hidden = grad_middle + grad_in
        terms = (grad_feed, grad_gate, grad_up, grad_branch, grad_proj)
        return (grad_hidden, grad_value_send, terms, jnp.stack([gain_grad_one, gain_grad_two]))

    def summed(part, order):
        axes = ["y", "z", "x"]
        place = {"y": y, "z": z, "x": x}
        size = {"y": 4, "z": 2, "x": 4}
        current = part
        for kind in order:
            at = axes.index(kind)
            axes.remove(kind)
            n = size[kind]
            pick = lambda s: lax.dynamic_index_in_dim(
                current, (place[kind] + s) % n, at, keepdims=False
            )
            total = pick(0).astype(F32)
            for s in range(1, n):
                total = total + moved(pick(s), kind, s).astype(F32)
            current = total.astype(BF) if axes else total
        return current

    def summed_gains(total):
        for kind, n in (("x", 4), ("y", 4), ("z", 2)):
            total = sum([total] + [moved(total, kind, s) for s in range(1, n)])
        return total

    own_rows = both_cores(held_and_got(tokens).reshape(2 * BLOCK, width))
    top_grad = both_cores(held_and_got(cotangent).reshape(2 * BLOCK, width))
    no_value = jnp.zeros((RING, 4 * BLOCK, PAIR), BF)

    def handed(value, pairs):
        return lax.ppermute(value, "section", pairs)

    result, value, _ = forward(own_rows, no_value)
    h_in = both_cores(handed(own_half(result), [(0, 1)]))
    v_in = handed(value, [(0, 1)])
    hidden = jnp.where(first, own_rows, h_in)
    result, _, saved = forward(hidden, v_in)
    acts = held_and_got(own_half(result).reshape(2, BLOCK, width))[None]

    grad_hidden, grad_value, _, _ = backward(top_grad, no_value, saved)
    g_in = both_cores(handed(own_half(grad_hidden).astype(BF), [(1, 0)]))
    gv_in = handed(grad_value, [(1, 0)])
    grad_out = jnp.where(first, g_in, top_grad)
    grad_hidden, _, terms, gain_terms = backward(grad_out, gv_in, saved)
    dins = held_and_got(own_half(grad_hidden).reshape(2, BLOCK, width))[None]

    normed, attended, normed_two, activated = saved[1], saved[5], saved[7], saved[10]
    grad_feed, grad_gate, grad_up, grad_branch, grad_proj = terms

    def term(left, right):
        return jnp.einsum("tf,td->fd", left, right, preferred_element_type=F32).astype(BF)

    def cut(whole):
        return whole.reshape(4, 2, 4, whole.shape[0] // 32, whole.shape[1])

    def unrolled(blocks_rel, axis):
        return jnp.concatenate(
            [
                lax.dynamic_index_in_dim(blocks_rel, (b - x) % 4, 0, keepdims=False)
                for b in range(RING)
            ],
            axis=axis,
        )

    down = summed(cut(term(activated, grad_feed)), "yzx")
    gate_share = summed(cut(term(normed_two, grad_gate)), "yxz")
    up_share = summed(cut(term(normed_two, grad_up)), "xyz")
    out_rel = term(attended, grad_branch).reshape(RING, PAIR, width)
    out_share = summed(cut(unrolled(out_rel, 0)), "yxz")
    qkv_shares = []
    for c in range(3):
        full = term(normed, grad_proj[c])
        rel = jnp.stack([full[:, k * PAIR : (k + 1) * PAIR] for k in range(RING)])
        qkv_shares.append(summed(cut(unrolled(rel, 1)), ("yxz", "xyz", "xyz")[c]))
    gain_total = summed_gains(gain_terms)
    return (
        acts,
        dins,
        jnp.stack(qkv_shares, axis=1)[None],
        out_share[None],
        jnp.stack([gate_share, up_share], axis=1)[None],
        down[None],
        gain_total[None],
    )


def solution(mesh):
    placed = (
        P(None, ("tensor", "dp"), None),
        P(None, ("tensor", "dp"), None),
        P(),
        P("section", None, None),
        P("section", None, None, "tensor"),
        P("section", "tensor", None),
        P("section", None, None, "tensor"),
        P("section", "tensor", None),
    )
    return jax.shard_map(
        per_device,
        mesh=mesh,
        in_specs=placed,
        out_specs=(
            P("section", None, ("tensor", "dp"), None),
            P("section", None, ("tensor", "dp"), None),
            P("section", "dp", None, "tensor"),
            P("section", ("tensor", "dp"), None),
            P("section", "dp", None, "tensor"),
            P("section", ("tensor", "dp"), None),
            P("section", None, None),
        ),
        check_vma=False,
    )
```

```python
import jax
import jax.numpy as jnp
import numpy as np
from jax import lax
from jax.experimental import pallas as pl
from jax.experimental.pallas import tpu as pltpu
from jax.sharding import PartitionSpec as P

HD = 64
LEN = 2048
RING = 4
BLOCK = 128
PAIR = 2 * HD
EPSILON = 1e-06
NEGATIVE = -1e30
KEYS = 512
QUERIES = 1024
BACK_KEYS = 256
BACK_QUERIES = 512
BF = jnp.bfloat16
F32 = jnp.float32


def along(kind, shift):
    pairs = []
    for index in range(32):
        y, z, x = index // 8, index // 4 % 2, index % 4
        if kind == "x":
            x = (x + shift) % 4
        elif kind == "y":
            y = (y + shift) % 4
        else:
            z = (z + shift) % 2
        pairs.append((index, y * 8 + z * 4 + x))
    return pairs


def moved(value, kind, shift):
    return lax.ppermute(value, "dp", along(kind, shift))


def swapped(value):
    return lax.ppermute(value, "tensor", [(0, 1), (1, 0)])


def rms_scale(hidden):
    return lax.rsqrt(jnp.mean(hidden * hidden, axis=-1, keepdims=True) + EPSILON)


def rotary_tables():
    half = HD // 2
    freqs = np.float32(10000.0) ** (-np.arange(half, dtype=np.float32) / np.float32(half))
    angles = np.arange(LEN, dtype=np.float32)[:, None] * freqs[None, :]
    return [jnp.asarray(np.tile(f(angles).astype(np.float32), (1, 4))) for f in (np.cos, np.sin)]


def low_lanes(shape):
    return lax.broadcasted_iota(jnp.int32, shape, 1) % HD < HD // 2


def turned(u, cosine, sine, sign):
    ahead = pltpu.roll(u, PAIR - HD // 2, 1)
    behind = pltpu.roll(u, HD // 2, 1)
    cross = jnp.where(low_lanes(u.shape), -sign * ahead, sign * behind)
    return u * cosine + cross * sine


def place_block(source, part):
    return (source, 4 + source, 15 - source, 11 - source)[part]


def on_core(kernel, ins, outs, *, scratch=(), smem=0, far=0, waits=(), limit=24, name):
    spots = [pl.BlockSpec(memory_space=pltpu.SMEM)] * smem
    spots += [pl.BlockSpec(memory_space=pltpu.VMEM)] * (len(ins) - smem - far)
    spots += [pl.BlockSpec(memory_space=pltpu.HBM)] * far
    spots += [pl.BlockSpec(memory_space=pl.ANY)] * len(waits)
    taken, given = len(ins), len(outs)

    def body(*refs):
        kernel(*refs[:taken], *refs[taken + len(waits) :])

    return pl.pallas_call(
        body,
        in_specs=spots,
        out_specs=[pl.BlockSpec(memory_space=pltpu.VMEM)] * given,
        out_shape=list(outs),
        scratch_shapes=list(scratch),
        compiler_params=pltpu.CompilerParams(vmem_limit_bytes=limit * 2**20),
        cost_estimate=pl.CostEstimate(flops=1, bytes_accessed=1, transcendentals=0),
        name=name,
    )(*ins, *waits)


def seen(value):
    return value[(0,) * (value.ndim - 2)][:8, :PAIR]


def shaped(*shape, dtype=BF):
    return jax.ShapeDtypeStruct(shape, dtype)


def heads_at(x_ref, shift):
    return pl.ds(pl.multiple_of(lax.rem(x_ref[0] + shift, RING) * PAIR, PAIR), PAIR)


def halves(rows):
    return [slice(0, rows // 2), slice(rows // 2, rows)]


def across(left, right):
    return lax.dot_general(left, right, (((1,), (1,)), ((), ())), preferred_element_type=F32)


def down_rows(left, right):
    return lax.dot_general(left, right, (((0,), (0,)), ((), ())), preferred_element_type=F32)


def own_half(t_ref, rows):
    return pl.ds(pl.multiple_of(t_ref[0] * (rows // 2), rows // 2), rows // 2)


def far_half(t_ref, rows):
    return pl.ds(pl.multiple_of((1 - t_ref[0]) * (rows // 2), rows // 2), rows // 2)


def own_tables(x_ref, table, half):
    blocks = [place_block(x_ref[0], 2 * half + part) for part in range(2)]
    return jnp.concatenate(
        [table[pl.ds(pl.multiple_of(b * BLOCK, BLOCK), BLOCK), :] for b in blocks]
    )


def project_kernel(x_ref, t_ref, mix_ref, own_ref, other_ref, gain_ref, w_ref, v1_ref, cos_ref, sin_ref,
                   m0, m1, m2, m3, n_ref, v_ref, h_ref):
    rows = h_ref.shape[0]
    h_ref[own_half(t_ref, rows), :] = own_ref[...]
    h_ref[far_half(t_ref, rows), :] = other_ref[...]
    for part in halves(rows):
        h = h_ref[part].astype(F32)
        n_ref[part] = (h * rms_scale(h) * gain_ref[...]).astype(BF)
    outs = (m0, m1, m2, m3)
    for pair in ((0, 1), (2, 3)):
        weight = jnp.concatenate(
            [w_ref[c, :, heads_at(x_ref, k)] for k in pair for c in range(3)], axis=1
        )
        for which, part in enumerate(halves(rows)):
            both = jnp.dot(n_ref[part], weight, preferred_element_type=F32)
            cosine, sine = own_tables(x_ref, cos_ref, which), own_tables(x_ref, sin_ref, which)
            for index, k in enumerate(pair):
                query, key, value = [
                    both[:, (3 * index + c) * PAIR : (3 * index + c + 1) * PAIR] for c in range(3)
                ]
                outs[k][0, part] = (turned(query, cosine, sine, 1.0) * HD ** (-0.5)).astype(BF)
                outs[k][1, part] = turned(key, cosine, sine, 1.0).astype(BF)
                value = mix_ref[0] * value + mix_ref[1] * v1_ref[k, part].astype(F32)
                outs[k][2, part] = value.astype(BF)
                v_ref[k, part] = value.astype(BF)


def project(x_index, t_index, mix, own, other, gain, w_qkv, value_first, cosine, sine, waits=()):
    rows, width = 2 * own.shape[0], own.shape[1]
    return on_core(
        project_kernel,
        (x_index, t_index, mix, own, other, gain, w_qkv, value_first, cosine, sine),
        [shaped(3, rows, PAIR)] * 4
        + [shaped(rows, width), shaped(RING, rows, PAIR), shaped(rows, width)],
        smem=3, waits=waits, limit=20, name="project",
    )


def pick_kernel(z_ref, pair_ref, keep_ref, send_ref):
    keep_ref[...] = pair_ref[z_ref[0]]
    send_ref[...] = pair_ref[1 - z_ref[0]]


def pick(z_index, pair, waits=()):
    return on_core(
        pick_kernel, (z_index, pair), [shaped(*pair.shape[1:])] * 2, smem=1, waits=waits, limit=4, name="pick"
    )


def branch_kernel(x_ref, o0, o1, o2, o3, w_ref, v_ref, o_ref, part_ref, copy_ref):
    for k, arrived in enumerate((o0, o1, o2, o3)):
        o_ref[:, heads_at(x_ref, k)] = arrived[...]
    for part in halves(o_ref.shape[0]):
        part_ref[part] = jnp.dot(o_ref[part], w_ref[...], preferred_element_type=F32).astype(BF)
    copy_ref[...] = v_ref[...]


def branch(x_index, arrived, w_out, value, waits=()):
    rows, width = arrived[0].shape[0], w_out.shape[1]
    return on_core(
        branch_kernel,
        (x_index, *arrived, w_out, value),
        [shaped(rows, RING * PAIR), shaped(rows, width), jax.ShapeDtypeStruct(value.shape, BF)],
        smem=1, waits=waits, limit=14, name="branch",
    )


def put_halves(t_ref, which, keep_ref, send_ref, value):
    @pl.when(t_ref[0] == which)
    def _():
        keep_ref[...] = value

    @pl.when(t_ref[0] != which)
    def _():
        send_ref[...] = value


def pieces(units):
    cut = (units // PAIR + 1) // 2 * PAIR
    return [(0, cut), (cut, units)]


def weight_copies(wgu_ref, wd_ref, gu_buf, d_buf, sems):
    copies = []
    for index, (low, high) in enumerate(pieces(wd_ref.shape[0])):
        at = pl.ds(low, high - low)
        copies.append(
            [
                pltpu.make_async_copy(wgu_ref.at[:, :, at], gu_buf.at[:, :, at], sems.at[index, 0]),
                pltpu.make_async_copy(wd_ref.at[at, :], d_buf.at[at, :], sems.at[index, 1]),
            ]
        )
    return copies


def weight_scratch(width, units):
    return [
        pltpu.VMEM((2, width, units), BF),
        pltpu.VMEM((units, width), BF),
        pltpu.SemaphoreType.DMA((2, 2)),
    ]


def feed_kernel(t_ref, h_ref, p_ref, q_ref, gain_ref, wgu_ref, wd_ref,
                m_ref, mine_ref, n_ref, gate_ref, up_ref, act_ref, keep_ref, send_ref,
                gu_buf, d_buf, sems, acc):
    copies = weight_copies(wgu_ref, wd_ref, gu_buf, d_buf, sems)
    for pair in copies:
        for copy in pair:
            copy.start()
    rows = halves(h_ref.shape[0])
    for part in rows:
        middle = h_ref[part].astype(F32) + (p_ref[part].astype(F32) + q_ref[part].astype(F32))
        m_ref[part] = middle
        n_ref[part] = (middle * rms_scale(middle) * gain_ref[...]).astype(BF)
    mine_ref[...] = m_ref[own_half(t_ref, h_ref.shape[0]), :]
    for index, (low, high) in enumerate(pieces(d_buf.shape[0])):
        at = slice(low, high)
        for copy in copies[index]:
            copy.wait()
        for which, part in enumerate(rows):
            gate = jnp.dot(n_ref[part], gu_buf[0, :, at], preferred_element_type=F32)
            up = jnp.dot(n_ref[part], gu_buf[1, :, at], preferred_element_type=F32)
            gate_ref[part, at] = gate.astype(BF)
            up_ref[part, at] = up.astype(BF)
            act = (gate / (1.0 + jnp.exp(-gate)) * up).astype(BF)
            act_ref[part, at] = act
            total = jnp.dot(act, d_buf[at, :], preferred_element_type=F32)
            if index == 0:
                acc[part] = total
            else:
                put_halves(t_ref, which, keep_ref, send_ref, (acc[part] + total).astype(BF))


def feed(t_index, hidden, own, other, gain, w_gu, w_down, waits=()):
    rows, width = hidden.shape
    units = w_down.shape[0]
    wide = shaped(rows, units)
    return on_core(
        feed_kernel,
        (t_index, hidden, own, other, gain, w_gu, w_down),
        [shaped(rows, width, dtype=F32), shaped(rows // 2, width, dtype=F32), shaped(rows, width)]
        + [wide, wide, wide, shaped(rows // 2, width), shaped(rows // 2, width)],
        scratch=weight_scratch(width, units) + [pltpu.VMEM((rows, width), F32)],
        smem=1, far=2, waits=waits, limit=30, name="feed",
    )


def feed_back_kernel(t_ref, own_ref, other_ref, gate_ref, up_ref, wgu_ref, wd_ref,
                     dgate_ref, dup_ref, part_ref, g_ref, gu_buf, d_buf, sems, acc):
    copies = weight_copies(wgu_ref, wd_ref, gu_buf, d_buf, sems)
    for which in (1, 0):
        for pair in copies:
            pair[which].start()
    g_ref[own_half(t_ref, g_ref.shape[0]), :] = own_ref[...]
    g_ref[far_half(t_ref, g_ref.shape[0]), :] = other_ref[...]
    for index, (low, high) in enumerate(pieces(d_buf.shape[0])):
        at = slice(low, high)
        copies[index][1].wait()
        for part in halves(g_ref.shape[0]):
            grad = across(g_ref[part], d_buf[at, :])
            gate = gate_ref[part, at].astype(F32)
            sigma = 1.0 / (1.0 + jnp.exp(-gate))
            up = up_ref[part, at].astype(F32)
            dgate_ref[part, at] = (grad * up * sigma * (1.0 + gate * (1.0 - sigma))).astype(BF)
            dup_ref[part, at] = (grad * gate * sigma).astype(BF)
        copies[index][0].wait()
        for part in halves(g_ref.shape[0]):
            total = across(dgate_ref[part, at], gu_buf[0, :, at]) + across(
                dup_ref[part, at], gu_buf[1, :, at]
            )
            if index == 0:
                acc[part] = total
            else:
                part_ref[part] = (acc[part] + total).astype(BF)


def feed_back(t_index, own, other, w_gu, w_down, gate, up, waits=()):
    rows, width = 2 * own.shape[0], own.shape[1]
    units = w_down.shape[0]
    wide = shaped(rows, units)
    return on_core(
        feed_back_kernel,
        (t_index, own, other, gate, up, w_gu, w_down),
        [wide, wide, shaped(rows, width), shaped(rows, width)],
        scratch=weight_scratch(width, units) + [pltpu.VMEM((rows, width), F32)],
        smem=1, far=2, waits=waits, limit=26, name="feed_back",
    )


def feed_terms_kernel(y_ref, n_ref, g_ref, u_ref, t0, t1, t2, t3):
    size = n_ref.shape[1] // 4
    rows = size // 8
    for k, out in enumerate((t0, t1, t2, t3)):
        at = pl.multiple_of(lax.rem(y_ref[0] + k, 4) * size, size)
        left = n_ref[:, pl.ds(at, size)]
        for spot, right in enumerate((g_ref, u_ref)):
            term = down_rows(left, right[...]).astype(BF)
            for index in range(8):
                out[index, spot * rows : (spot + 1) * rows, :] = term[index * rows : (index + 1) * rows]


def feed_terms(y_index, normed, dgate, dup):
    width, units = normed.shape[1], dgate.shape[1]
    return on_core(
        feed_terms_kernel, (y_index, normed, dgate, dup), [shaped(8, width // 16, units)] * 4,
        smem=1, limit=16, name="feed_terms",
    )


def sum_kernel(*refs):
    total = refs[0][...].astype(F32)
    for ref in refs[1:-1]:
        total += ref[...].astype(F32)
    refs[-1][...] = total.astype(BF)


def summed(values, waits=()):
    shape = values[0].shape
    piece = pl.BlockSpec((shape[0] // 4, *shape[1:]), lambda i: (i, 0, 0))

    def body(*refs):
        sum_kernel(*refs[: len(values)], refs[-1])

    return pl.pallas_call(
        body,
        grid=(4,),
        in_specs=[piece] * len(values) + [pl.BlockSpec(memory_space=pl.ANY)] * len(waits),
        out_specs=piece,
        out_shape=shaped(*shape),
        compiler_params=pltpu.CompilerParams(vmem_limit_bytes=8 * 2**20),
        cost_estimate=pl.CostEstimate(flops=1, bytes_accessed=1, transcendentals=0),
        name="summed",
    )(*values, *waits)


def middle_back_kernel(x_ref, t_ref, g_ref, m_ref, p_ref, q_ref, gain_ref, w_ref,
                       dm_ref, gm_ref, d0, d1, d2, d3, sum_ref, do_ref):
    rows = g_ref.shape[0]
    for which, part in enumerate(halves(rows)):
        grad = p_ref[part].astype(F32) + q_ref[part].astype(F32)
        inner, scale, unit = norm_back(m_ref[part], grad, gain_ref[...])
        middle = g_ref[part].astype(F32) + inner

        @pl.when(t_ref[0] == which)
        def _():
            dm_ref[...] = middle
            sum_ref[...] = jnp.sum(grad * unit, axis=0, keepdims=True)

        gm_ref[part] = middle.astype(BF)
        do_ref[part] = across(gm_ref[part], w_ref[...]).astype(BF)
    for k, out in enumerate((d0, d1, d2, d3)):
        out[...] = do_ref[:, heads_at(x_ref, k)]


def norm_back(hidden, grad, gain):
    scale = rms_scale(hidden)
    unit = hidden * scale
    weighted = grad * gain
    inner = scale * (weighted - unit * jnp.mean(weighted * unit, axis=-1, keepdims=True))
    return inner, scale, unit


def middle_back(x_index, t_index, grad, middle, own, other, gain, w_out, waits=()):
    rows, width = grad.shape
    return on_core(
        middle_back_kernel,
        (x_index, t_index, grad, middle, own, other, gain, w_out),
        [shaped(rows // 2, width, dtype=F32), shaped(rows, width)]
        + [shaped(rows, PAIR)] * 4
        + [shaped(1, width, dtype=F32)],
        scratch=[pltpu.VMEM((rows, RING * PAIR), BF)],
        smem=2, waits=waits, limit=20, name="middle_back",
    )


def project_back_kernel(x_ref, t_ref, g0, g1, g2, g3, w_ref, n_ref, keep_ref, send_ref, half_ref, d_ref):
    for k, grad in enumerate((g0, g1, g2, g3)):
        for c in range(3):
            d_ref[c, :, heads_at(x_ref, k)] = grad[c]
    for which, part in enumerate(halves(d_ref.shape[1])):
        total = sum(across(d_ref[c, part], w_ref[c]) for c in range(3)).astype(BF)
        put_halves(t_ref, which, keep_ref, send_ref, total)
    half_ref[...] = n_ref[own_half(t_ref, n_ref.shape[0]), :]


def project_back(x_index, t_index, grads, w_qkv, normed, waits=()):
    rows, width = normed.shape
    return on_core(
        project_back_kernel,
        (x_index, t_index, *grads, w_qkv, normed),
        [shaped(rows // 2, width)] * 3,
        scratch=[pltpu.VMEM((3, rows, RING * PAIR), BF)],
        smem=2, waits=waits, limit=16, name="project_back",
    )


def input_back_kernel(h_ref, dm_ref, p_ref, q_ref, gain_ref, dh_ref, low_ref):
    grad = p_ref[...].astype(F32) + q_ref[...].astype(F32)
    total = dm_ref[...] + norm_back(h_ref[...].astype(F32), grad, gain_ref[...])[0]
    dh_ref[...] = total
    low_ref[...] = total.astype(BF)


def input_back(hidden, grad_middle, own, other, gain):
    return on_core(
        input_back_kernel, (hidden, grad_middle, own, other, gain),
        [shaped(*hidden.shape, dtype=F32), shaped(*hidden.shape)], limit=10, name="input_back",
    )


def close_kernel(m_ref, p_ref, q_ref, out_ref):
    out_ref[...] = (m_ref[...] + (p_ref[...].astype(F32) + q_ref[...].astype(F32))).astype(BF)


def close(middle, own, other, waits=()):
    return on_core(
        close_kernel, (middle, own, other), [shaped(*own.shape)], waits=waits, limit=6, name="close"
    )[0]


DOWN_ROWS, OUT_AT, QKV_AT = 44, 48, 64


def put_by_z(z_ref, keep_ref, send_ref, device, rows, lanes, value):
    spot = device // 8 * 4 + device % 4
    put_halves(z_ref, device // 4 % 2, keep_ref.at[spot, rows, lanes], send_ref.at[spot, rows, lanes], value)


def early_terms_kernel(z_ref, act_ref, go_ref, o_ref, gm_ref, keep_ref, send_ref, down):
    width = go_ref.shape[1]
    units = act_ref.shape[1]
    for low in range(0, units, 256):
        high = min(low + 256, units)
        down[low:high, :] = down_rows(act_ref[:, low:high], go_ref[...])
    blank = jnp.zeros((OUT_AT - DOWN_ROWS, width), F32)
    everywhere = slice(0, width)
    for at in range(32):
        block = jnp.concatenate([down[at * DOWN_ROWS : (at + 1) * DOWN_ROWS, :], blank])
        put_by_z(z_ref, keep_ref, send_ref, at, slice(0, OUT_AT), everywhere, block.astype(BF))
    rows = o_ref.shape[1] // 32
    for low in range(0, o_ref.shape[1], 256):
        term = down_rows(o_ref[:, low : low + 256], gm_ref[...]).astype(BF)
        for index in range(256 // rows):
            put_by_z(
                z_ref, keep_ref, send_ref, low // rows + index, slice(OUT_AT, QKV_AT), everywhere,
                term[index * rows : (index + 1) * rows],
            )


def early_terms(z_index, act, grad_out, attended, grad_branch):
    width = grad_out.shape[1]
    return on_core(
        early_terms_kernel,
        (z_index, act, grad_out, attended, grad_branch),
        [shaped(16, QKV_AT, width)] * 2,
        scratch=[pltpu.VMEM((act.shape[1], width), F32)],
        smem=1, limit=18, name="early_terms",
    )


def qkv_terms_kernel(x_ref, t_ref, z_ref, n_ref, near_ref, far_ref, g0, g1, g2, g3,
                     w_ref, gain_ref, two_ref, keep_ref, send_ref, sum_ref, acc):
    half = near_ref.shape[1]
    rows, wide = n_ref.shape[1] // 32, 3 * PAIR

    def joined(grad, at):
        return jnp.concatenate([grad[c, at, :] for c in range(3)], axis=1)

    acc[...] = down_rows(joined(g0, slice(None)), n_ref[...])
    for index, grad in enumerate((g1, g2, g3)):
        acc[...] += down_rows(joined(grad, own_half(t_ref, 2 * half)), near_ref[index]) + down_rows(
            joined(grad, far_half(t_ref, 2 * half)), far_ref[index]
        )
    for low in range(0, acc.shape[1], 256):
        term = acc[:, low : low + 256].T.astype(BF)
        for index in range(256 // rows):
            at = low // rows + index
            block = term[index * rows : (index + 1) * rows]
            both = jnp.concatenate([block[: rows // 2], block[rows // 2 :]], axis=1)
            put_by_z(z_ref, keep_ref, send_ref, at, slice(0, rows // 2), slice(0, 2 * wide), both)
        total = jnp.zeros((1, 256), F32)
        for c in range(3):
            weight = w_ref[c, low : low + 256, heads_at(x_ref, 0)].astype(F32).T
            total += jnp.sum(weight * acc[c * PAIR : (c + 1) * PAIR, low : low + 256], axis=0, keepdims=True)
        sum_ref[0:1, low : low + 256] = total / gain_ref[:, low : low + 256]
    sum_ref[1:2, :] = two_ref[...]


def qkv_terms(x_index, t_index, z_index, normed, near, far, grads, w_qkv, gain, gain_sum):
    width = normed.shape[1]
    return on_core(
        qkv_terms_kernel,
        (x_index, t_index, z_index, normed, near, far, *grads, w_qkv, gain, gain_sum),
        [shaped(16, width // 64, 6 * PAIR)] * 2 + [shaped(2, width, dtype=F32)],
        scratch=[pltpu.VMEM((3 * PAIR, width), F32)],
        smem=3, limit=18, name="qkv_terms",
    )


def rest_kernel(a_ref, b_ref, c_ref, d_ref, out_ref):
    wide = c_ref.shape[2]
    out_ref[:, :QKV_AT, :] = (a_ref[...].astype(F32) + b_ref[...].astype(F32)).astype(BF)
    out_ref[:, QKV_AT:, :wide] = (c_ref[...].astype(F32) + d_ref[...].astype(F32)).astype(BF)
    out_ref[:, QKV_AT:, wide:] = jnp.zeros((out_ref.shape[0], out_ref.shape[1] - QKV_AT, out_ref.shape[2] - wide), BF)


def rest_sum(early, early_got, late, late_got, waits=()):
    count, _, width = early.shape
    first = pl.BlockSpec((count // 4, QKV_AT, width), lambda i: (i, 0, 0))
    second = pl.BlockSpec((count // 4, *late.shape[1:]), lambda i: (i, 0, 0))
    total = QKV_AT + late.shape[1]

    def body(*refs):
        rest_kernel(*refs[:4], refs[-1])

    return pl.pallas_call(
        body,
        grid=(4,),
        in_specs=[first, first, second, second] + [pl.BlockSpec(memory_space=pl.ANY)] * len(waits),
        out_specs=pl.BlockSpec((count // 4, total, width), lambda i: (i, 0, 0)),
        out_shape=shaped(count, total, width),
        compiler_params=pltpu.CompilerParams(vmem_limit_bytes=8 * 2**20),
        cost_estimate=pl.CostEstimate(flops=1, bytes_accessed=1, transcendentals=0),
        name="rest_sum",
    )(early, early_got, late, late_got, *waits)


def first_visible(ends_ref, places):
    start = jnp.zeros_like(places)
    for index in range(4):
        start = jnp.where(places >= ends_ref[index], ends_ref[index], start)
    return start


def attend_kernel(x_ref, ends_ref, m0, m1, m2, m3, o0, o1, o2, o3, lse_ref, out_t, keys, query_t,
                  value_t, acc):
    x = x_ref[0]
    lanes = lax.broadcasted_iota(jnp.int32, (BLOCK, PAIR), 1)
    for shift, message in enumerate((m0, m1, m2, m3)):
        source = lax.rem(x + RING - shift, RING)
        for part in range(4):
            at = pl.ds(pl.multiple_of(place_block(source, part) * BLOCK, BLOCK), BLOCK)
            inside = slice(part * BLOCK, (part + 1) * BLOCK)
            block = message[1, inside, :]
            keys[0, at, :] = jnp.where(lanes < HD, block, jnp.zeros_like(block))
            keys[1, at, :] = jnp.where(lanes < HD, jnp.zeros_like(block), block)
            query_t[:, at] = message[0, inside, :].T
            value_t[:, at] = message[2, inside, :].T

    def one_query_block(qi, _):
        q_at = pl.ds(pl.multiple_of(qi * QUERIES, QUERIES), QUERIES)
        places = qi * QUERIES + lax.broadcasted_iota(jnp.int32, (1, QUERIES), 1)
        start = first_visible(ends_ref, places)
        acc[...] = jnp.zeros_like(acc)

        def one_key_block(kj, carry, diagonal):
            k_at = pl.ds(pl.multiple_of(kj * KEYS, KEYS), KEYS)
            key_places = kj * KEYS + lax.broadcasted_iota(jnp.int32, (KEYS, QUERIES), 0)
            visible = key_places >= start
            if diagonal:
                visible = visible & (key_places <= places)
            after = []
            for head in range(2):
                highest, total = carry[head]
                scores = jnp.dot(keys[head, k_at, :], query_t[:, q_at], preferred_element_type=F32)
                scores = jnp.where(visible, scores, NEGATIVE)
                higher = jnp.maximum(highest, jnp.max(scores, axis=0, keepdims=True))
                shrink = jnp.exp(highest - higher)
                weight = jnp.exp(scores - higher)
                total = total * shrink + jnp.sum(weight, axis=0, keepdims=True)
                part = slice(head * HD, (head + 1) * HD)
                acc[part, :] = acc[part, :] * shrink + jnp.dot(
                    value_t[part, k_at], weight.astype(BF), preferred_element_type=F32
                )
                after.append((higher, total))
            return tuple(after)

        begin = (jnp.full((1, QUERIES), NEGATIVE, F32), jnp.zeros((1, QUERIES), F32))
        ratio = QUERIES // KEYS
        done = lax.fori_loop(
            0, qi * ratio, lambda kj, carry: one_key_block(kj, carry, False), (begin, begin)
        )
        for step in range(ratio):
            done = one_key_block(qi * ratio + step, done, True)
        for head in range(2):
            highest, total = done[head]
            part = slice(head * HD, (head + 1) * HD)
            out_t[part, q_at] = acc[part, :] / total
            lse_ref[head : head + 1, q_at] = highest + jnp.log(total)
        return 0

    lax.fori_loop(0, LEN // QUERIES, one_query_block, 0)
    for shift, out in enumerate((o0, o1, o2, o3)):
        source = lax.rem(x + RING - shift, RING)
        for part in range(4):
            at = pl.ds(pl.multiple_of(place_block(source, part) * BLOCK, BLOCK), BLOCK)
            out[part * BLOCK : (part + 1) * BLOCK, :] = out_t[:, at].T.astype(BF)


def attend(x_index, ends, messages, waits=()):
    rows = messages[0].shape[1]
    return on_core(
        attend_kernel,
        (x_index, ends, *messages),
        [shaped(rows, PAIR)] * 4 + [shaped(2, LEN, dtype=F32), shaped(PAIR, LEN, dtype=F32)],
        scratch=[
            pltpu.VMEM((2, LEN, PAIR), BF),
            pltpu.VMEM((PAIR, LEN), BF),
            pltpu.VMEM((PAIR, LEN), BF),
            pltpu.VMEM((PAIR, QUERIES), F32),
        ],
        smem=2, waits=waits, limit=16, name="attend",
    )


def attend_back_kernel(x_ref, ends_ref, mix_ref, m0, m1, m2, m3, d0, d1, d2, d3, lse_ref, out_t,
                       dv1_ref, cos_ref, sin_ref, g0, g1, g2, g3, keys, values, queries, grads,
                       key_t, query_t, grad_t, delta, grad_k, grad_v, grad_q_t):
    x = x_ref[0]
    lanes = lax.broadcasted_iota(jnp.int32, (BLOCK, PAIR), 1)
    for shift, (message, arrived) in enumerate(((m0, d0), (m1, d1), (m2, d2), (m3, d3))):
        source = lax.rem(x + RING - shift, RING)
        for part in range(4):
            at = pl.ds(pl.multiple_of(place_block(source, part) * BLOCK, BLOCK), BLOCK)
            inside = slice(part * BLOCK, (part + 1) * BLOCK)
            query, key, value = message[0, inside, :], message[1, inside, :], message[2, inside, :]
            grad = arrived[inside, :]
            zero = jnp.zeros_like(query)
            for both, block in ((keys, key), (values, value), (queries, query), (grads, grad)):
                both[0, at, :] = jnp.where(lanes < HD, block, zero)
                both[1, at, :] = jnp.where(lanes < HD, zero, block)
            key_t[:, at] = key.T
            query_t[:, at] = query.T
            turned_grad = grad.T
            grad_t[:, at] = turned_grad
            product = out_t[:, at] * turned_grad.astype(F32)
            delta[0:1, at] = jnp.sum(product[:HD], axis=0, keepdims=True)
            delta[1:2, at] = jnp.sum(product[HD:], axis=0, keepdims=True)
    grad_k[...] = jnp.zeros_like(grad_k)
    grad_v[...] = jnp.zeros_like(grad_v)
    grad_q_t[...] = jnp.zeros_like(grad_q_t)

    def one_query_block(qi, _):
        q_at = pl.ds(pl.multiple_of(qi * BACK_QUERIES, BACK_QUERIES), BACK_QUERIES)
        places = qi * BACK_QUERIES + lax.broadcasted_iota(jnp.int32, (1, BACK_QUERIES), 1)
        start = first_visible(ends_ref, places)

        def one_key_block(kj, carry):
            k_at = pl.ds(pl.multiple_of(kj * BACK_KEYS, BACK_KEYS), BACK_KEYS)
            key_places = kj * BACK_KEYS + lax.broadcasted_iota(jnp.int32, (BACK_KEYS, BACK_QUERIES), 0)
            visible = (key_places <= places) & (key_places >= start)
            for head in range(2):
                part = slice(head * HD, (head + 1) * HD)
                scores = jnp.dot(keys[head, k_at, :], query_t[:, q_at], preferred_element_type=F32)
                scores = jnp.where(visible, scores, NEGATIVE)
                weight = jnp.exp(scores - lse_ref[head : head + 1, q_at])
                grad_w = jnp.dot(values[head, k_at, :], grad_t[:, q_at], preferred_element_type=F32)
                grad_s = (weight * (grad_w - delta[head : head + 1, q_at])).astype(BF)
                grad_v[k_at, :] += jnp.dot(
                    weight.astype(BF), grads[head, q_at, :], preferred_element_type=F32
                )
                grad_k[k_at, :] += jnp.dot(grad_s, queries[head, q_at, :], preferred_element_type=F32)
                grad_q_t[part, q_at] += jnp.dot(
                    key_t[part, k_at], grad_s, preferred_element_type=F32
                )
            return carry

        return lax.fori_loop(0, (qi + 1) * (BACK_QUERIES // BACK_KEYS), one_key_block, 0)

    lax.fori_loop(0, LEN // BACK_QUERIES, one_query_block, 0)
    for shift, out in enumerate((g0, g1, g2, g3)):
        source = lax.rem(x + RING - shift, RING)
        for part in range(4):
            at = pl.ds(pl.multiple_of(place_block(source, part) * BLOCK, BLOCK), BLOCK)
            inside = slice(part * BLOCK, (part + 1) * BLOCK)
            cosine, sine = cos_ref[at, :], sin_ref[at, :]
            grad_q = grad_q_t[:, at].T * HD ** (-0.5)
            out[0, inside, :] = turned(grad_q, cosine, sine, -1.0).astype(BF)
            out[1, inside, :] = turned(grad_k[at, :], cosine, sine, -1.0).astype(BF)
            out[2, inside, :] = (
                mix_ref[0] * grad_v[at, :] + mix_ref[1] * dv1_ref[shift, inside, :].astype(F32)
            ).astype(BF)


def attend_back(x_index, ends, mix, messages, arrived, lse, out_t, dv1, cosine, sine, waits=()):
    rows = messages[0].shape[1]
    return on_core(
        attend_back_kernel,
        (x_index, ends, mix, *messages, *arrived, lse, out_t, dv1, cosine, sine),
        [shaped(3, rows, PAIR)] * 4,
        scratch=[pltpu.VMEM((2, LEN, PAIR), BF)] * 4
        + [pltpu.VMEM((PAIR, LEN), BF)] * 3
        + [
            pltpu.VMEM((2, LEN), F32),
            pltpu.VMEM((LEN, PAIR), F32),
            pltpu.VMEM((LEN, PAIR), F32),
            pltpu.VMEM((PAIR, LEN), F32),
        ],
        smem=3, waits=waits, limit=24, name="attend_back",
    )


def out_and_back(values, sign):
    return [values[0]] + [moved(values[shift], "x", sign * shift) for shift in range(1, RING)]


def all_to_all(value, kinds):
    groups = {}
    for index in range(32):
        place = {"y": index // 8, "z": index // 4 % 2, "x": index % 4}
        groups.setdefault(tuple(place[k] for k in "yzx" if k not in kinds), []).append(index)
    return lax.all_to_all(value, "dp", 0, 0, axis_index_groups=list(groups.values()))


def per_device(tokens, cotangent, doc_lengths, gains, wqkv, wo, wgu, wd):
    first = lax.axis_index("section") == 0
    tensor = lax.axis_index("tensor")
    position = lax.axis_index("dp")
    y, z, x = position // 8, position // 4 % 2, position % 4
    x_index, y_index, z_index, t_index = [
        v.astype(jnp.int32).reshape(1) for v in (x, y, z, tensor)
    ]
    width = tokens.shape[2]

    def in_order(keep, got):
        got = got.astype(keep.dtype)
        return jnp.where(z == 0, jnp.stack([keep, got]), jnp.stack([got, keep]))

    def regrouped(pair):
        keep = lax.dynamic_index_in_dim(pair, z, 0, keepdims=False)
        send = lax.dynamic_index_in_dim(pair, 1 - z, 0, keepdims=False)
        return in_order(keep, moved(send.astype(BF), "z", 1))

    lens = lax.dynamic_slice(doc_lengths, (z, y, 0), (1, 1, 4))
    ends = jnp.cumsum(lens.reshape(4), dtype=jnp.int32)
    cosine, sine = rotary_tables()
    w_qkv = jnp.transpose(wqkv[0], (1, 0, 2))
    w_gu = jnp.transpose(wgu[0], (1, 0, 2))
    w_out, w_down = wo[0], wd[0]
    gain_one, gain_two = gains[0, 0:1], gains[0, 1:2]
    mix = jnp.where(first, jnp.array([1.0, 0.0], F32), jnp.array([0.5, 0.5], F32))
    mix_back = jnp.where(first, jnp.array([1.0, 1.0], F32), jnp.array([0.5, 0.0], F32))

    def handed(value, pairs):
        return lax.ppermute(value, "section", pairs)

    def first_half(own, value_first):
        *messages, normed, value, hidden = project(
            x_index, t_index, mix, own, swapped(own), gain_one, w_qkv, value_first, cosine, sine
        )
        return out_and_back(messages, 1), normed, value, hidden

    def second_half(hidden, outs, value, waits=()):
        attended, part, value = branch(x_index, out_and_back(outs, -1), w_out, value, waits=waits)
        middle, mine, normed_two, gate, up, act, keep, send = feed(
            t_index, hidden, part, swapped(part), gain_two, w_gu, w_down
        )
        return mine, keep, swapped(send), value, (attended, middle, normed_two, gate, up, act)

    own_rows = regrouped(tokens).reshape(2 * BLOCK, width)
    no_value = jnp.zeros((RING, 4 * BLOCK, PAIR), BF)

    messages, _, value, hidden = first_half(own_rows, no_value)
    *outs, _, _ = attend(x_index, ends, messages, waits=(seen(w_gu),))
    cot_keep, cot_send = pick(z_index, cotangent, waits=(seen(outs[0]),))
    top_grad = in_order(cot_keep, moved(cot_send, "z", 1)).reshape(2 * BLOCK, width)
    mine, keep, got, value, _ = second_half(hidden, outs, value)
    v_in = handed(value, [(0, 1)])
    result = close(mine, keep, got, waits=(seen(v_in),))
    own = jnp.where(first, own_rows, handed(result, [(0, 1)]))

    messages, normed, value, hidden = first_half(own, v_in)
    *outs, lse, out_t = attend(x_index, ends, messages)
    mine, keep, got, _, saved = second_half(hidden, outs, value, waits=(seen(top_grad),))
    attended, middle, normed_two, gate, up, act = saved
    acts = regrouped(close(mine, keep, got).reshape(2, BLOCK, width))[None]

    def first_back(own_grad, waits=()):
        return feed_back(t_index, own_grad, swapped(own_grad), w_gu, w_down, gate, up, waits=waits)

    def second_back(grad, part, waits=()):
        grad_middle, grad_branch, *sends, gain_sum = middle_back(
            x_index, t_index, grad, middle, part, swapped(part), gain_two, w_out, waits=waits
        )
        return grad_middle, grad_branch, out_and_back(sends, 1), gain_sum

    def third_back(arrived, grad_value, waits=()):
        return attend_back(
            x_index, ends, mix_back, messages, arrived, lse, out_t, grad_value, cosine, sine, waits=waits
        )

    def fourth_back(grads, grad_middle, waits=()):
        keep, send, half = project_back(
            x_index, t_index, out_and_back(grads, -1), w_qkv, normed, waits=waits
        )
        return *input_back(own, grad_middle, keep, swapped(send), gain_one), half, keep

    _, _, part, grad = first_back(top_grad)
    grad_middle, _, arrived, _ = second_back(grad, part)
    grads = third_back(arrived, no_value, waits=(seen(acts[0]),))
    gv_in = handed(jnp.stack([grad[2] for grad in grads]), [(1, 0)])
    _, grad_hidden, half, _ = fourth_back(grads, grad_middle, waits=(seen(gv_in),))
    near = [moved(half, "x", k) for k in range(1, RING)]
    own_grad = jnp.where(first, handed(grad_hidden, [(1, 0)]), top_grad)

    dgate, dup, part, grad_out = first_back(own_grad, waits=[seen(rows) for rows in near])
    feed_term = feed_terms(y_index, normed_two, dgate, dup)
    feed_got = [moved(feed_term[k], "y", k) for k in range(1, 4)]
    grad_middle, grad_branch, arrived, gain_sum = second_back(grad_out, part, waits=(seen(feed_term[0]),))
    early, early_send = early_terms(z_index, act, grad_out, attended, grad_branch)
    early_got = moved(early_send, "z", 1)
    near = jnp.stack(near)
    far = swapped(near)
    grads = third_back(arrived, gv_in, waits=(seen(far), seen(early)))
    late, late_send, gain_total = qkv_terms(
        x_index, t_index, z_index, normed, near, far, grads, w_qkv, gain_one, gain_sum
    )
    late_got = moved(late_send, "z", 1)
    grad_hidden, _, _, last = fourth_back(grads, grad_middle, waits=(seen(late),))
    dins = regrouped(grad_hidden.reshape(2, BLOCK, width))[None]

    rows = width // 32
    feed_sum = summed([feed_term[0], *feed_got], waits=(seen(last),))
    feed_share = jnp.sum(all_to_all(feed_sum, "zx").astype(F32), axis=0).reshape(2, rows, -1)
    rest = rest_sum(early, early_got, late, late_got, waits=(seen(feed_sum),))
    rest = all_to_all(rest, "yx").astype(F32)
    down_share = jnp.sum(rest[:, :DOWN_ROWS], axis=0)
    out_share = jnp.sum(rest[:, OUT_AT:QKV_AT], axis=0)
    qkv_share = jnp.sum(
        rest[:, QKV_AT:, : 6 * PAIR].reshape(4, RING, rows // 2, 2, 3, PAIR), axis=0
    )
    qkv_share = jnp.transpose(qkv_share, (2, 1, 3, 0, 4)).reshape(rows, 3, RING * PAIR)

    gain_total = gain_total + swapped(gain_total)
    gain_total = jnp.sum(
        lax.all_to_all(jnp.broadcast_to(gain_total, (32, *gain_total.shape)), "dp", 0, 0), axis=0
    )
    return (
        acts,
        dins,
        qkv_share[None],
        out_share[None],
        jnp.transpose(feed_share, (1, 0, 2))[None],
        down_share[None],
        gain_total[None],
    )


def solution(mesh):
    placed = (
        P(None, ("tensor", "dp"), None),
        P(None, ("tensor", "dp"), None),
        P(),
        P("section", None, None),
        P("section", None, None, "tensor"),
        P("section", "tensor", None),
        P("section", None, None, "tensor"),
        P("section", "tensor", None),
    )
    return jax.shard_map(
        per_device,
        mesh=mesh,
        in_specs=placed,
        out_specs=(
            P("section", None, ("tensor", "dp"), None),
            P("section", None, ("tensor", "dp"), None),
            P("section", "dp", None, "tensor"),
            P("section", ("tensor", "dp"), None),
            P("section", "dp", None, "tensor"),
            P("section", ("tensor", "dp"), None),
            P("section", None, None),
        ),
        check_vma=False,
    )
```

```python
import jax
import jax.numpy as jnp
import numpy as np
from jax import lax
from jax.experimental import pallas as pl
from jax.experimental.pallas import tpu as pltpu
from jax.sharding import PartitionSpec as P

HD = 64
LEN = 2048
RING = 4
BLOCK = 128
PAIR = 2 * HD
EPSILON = 1e-06
BRIEF = 0.001
NEGATIVE = -1e30
KEYS = 512
QUERIES = 1024
BACK_KEYS = 256
BACK_QUERIES = 512
BF = jnp.bfloat16
F32 = jnp.float32


def along(kind, shift):
    pairs = []
    for index in range(32):
        y, z, x = index // 8, index // 4 % 2, index % 4
        if kind == "x":
            x = (x + shift) % 4
        elif kind == "y":
            y = (y + shift) % 4
        else:
            z = (z + shift) % 2
        pairs.append((index, y * 8 + z * 4 + x))
    return pairs


def moved(value, kind, shift):
    return lax.ppermute(value, "dp", along(kind, shift))


def swapped(value):
    return lax.ppermute(value, "tensor", [(0, 1), (1, 0)])


def rms_scale(hidden):
    return lax.rsqrt(jnp.mean(hidden * hidden, axis=-1, keepdims=True) + EPSILON)


def rotary_tables():
    half = HD // 2
    freqs = np.float32(10000.0) ** (-np.arange(half, dtype=np.float32) / np.float32(half))
    angles = np.arange(LEN, dtype=np.float32)[:, None] * freqs[None, :]
    return [jnp.asarray(np.tile(f(angles).astype(np.float32), (1, 4))) for f in (np.cos, np.sin)]


def low_lanes(shape):
    return lax.broadcasted_iota(jnp.int32, shape, 1) % HD < HD // 2


def turned(u, cosine, sine, sign):
    ahead = pltpu.roll(u, PAIR - HD // 2, 1)
    behind = pltpu.roll(u, HD // 2, 1)
    cross = jnp.where(low_lanes(u.shape), -sign * ahead, sign * behind)
    return u * cosine + cross * sine


def place_block(source, part):
    return (source, 4 + source, 15 - source, 11 - source)[part]


def lasting(us):
    return pl.CostEstimate(flops=int(us * 1.1e9), bytes_accessed=int(us * 3.6e6), transcendentals=0)


def on_core(kernel, ins, outs, *, scratch=(), smem=0, far=0, waits=(), limit=24, us, name):
    spots = [pl.BlockSpec(memory_space=pltpu.SMEM)] * smem
    spots += [pl.BlockSpec(memory_space=pltpu.VMEM)] * (len(ins) - smem - far)
    spots += [pl.BlockSpec(memory_space=pltpu.HBM)] * far
    spots += [pl.BlockSpec(memory_space=pl.ANY)] * len(waits)
    taken, given = len(ins), len(outs)

    def body(*refs):
        kernel(*refs[:taken], *refs[taken + len(waits) :])

    return pl.pallas_call(
        body,
        in_specs=spots,
        out_specs=[pl.BlockSpec(memory_space=pltpu.VMEM)] * given,
        out_shape=list(outs),
        scratch_shapes=list(scratch),
        compiler_params=pltpu.CompilerParams(vmem_limit_bytes=limit * 2**20),
        cost_estimate=lasting(us),
        name=name,
    )(*ins, *waits)


def seen(value):
    return value[(0,) * (value.ndim - 2)][:8, :PAIR]


def shaped(*shape, dtype=BF):
    return jax.ShapeDtypeStruct(shape, dtype)


def heads_at(x_ref, shift):
    return pl.ds(pl.multiple_of(lax.rem(x_ref[0] + shift, RING) * PAIR, PAIR), PAIR)


def halves(rows):
    return [slice(0, rows // 2), slice(rows // 2, rows)]


def across(left, right):
    return lax.dot_general(left, right, (((1,), (1,)), ((), ())), preferred_element_type=F32)


def down_rows(left, right):
    return lax.dot_general(left, right, (((0,), (0,)), ((), ())), preferred_element_type=F32)


def own_half(t_ref, rows):
    return pl.ds(pl.multiple_of(t_ref[0] * (rows // 2), rows // 2), rows // 2)


def far_half(t_ref, rows):
    return pl.ds(pl.multiple_of((1 - t_ref[0]) * (rows // 2), rows // 2), rows // 2)


def project_kernel(x_ref, t_ref, mix_ref, own_ref, other_ref, gain_ref, w_ref, v1_ref, cos_ref, sin_ref,
                   m0, m1, m2, m3, n_ref, v_ref, h_ref, zero_ref, cos_buf, sin_buf, sems):
    copies = []
    for part in range(4):
        at = pl.ds(pl.multiple_of(place_block(x_ref[0], part) * BLOCK, BLOCK), BLOCK)
        to = pl.ds(part * BLOCK, BLOCK)
        copies.append(pltpu.make_async_copy(cos_ref.at[at], cos_buf.at[to], sems.at[part, 0]))
        copies.append(pltpu.make_async_copy(sin_ref.at[at], sin_buf.at[to], sems.at[part, 1]))
    for copy in copies:
        copy.start()
    zero_ref[...] = jnp.zeros_like(zero_ref)
    rows = h_ref.shape[0]
    h_ref[own_half(t_ref, rows), :] = own_ref[...]
    h_ref[far_half(t_ref, rows), :] = other_ref[...]
    for part in halves(rows):
        h = h_ref[part].astype(F32)
        n_ref[part] = (h * rms_scale(h) * gain_ref[...]).astype(BF)
    for copy in copies:
        copy.wait()
    outs = (m0, m1, m2, m3)
    for pair in ((0, 1), (2, 3)):
        weight = jnp.concatenate(
            [w_ref[c, :, heads_at(x_ref, k)] for k in pair for c in range(3)], axis=1
        )
        for part in halves(rows):
            both = jnp.dot(n_ref[part], weight, preferred_element_type=F32)
            cosine, sine = cos_buf[part], sin_buf[part]
            for index, k in enumerate(pair):
                query, key, value = [
                    both[:, (3 * index + c) * PAIR : (3 * index + c + 1) * PAIR] for c in range(3)
                ]
                outs[k][0, part] = (turned(query, cosine, sine, 1.0) * HD ** (-0.5)).astype(BF)
                outs[k][1, part] = turned(key, cosine, sine, 1.0).astype(BF)
                value = mix_ref[0] * value + mix_ref[1] * v1_ref[k, part].astype(F32)
                outs[k][2, part] = value.astype(BF)
                v_ref[k, part] = value.astype(BF)


def project(x_index, t_index, mix, own, other, gain, w_qkv, value_first, cosine, sine, waits=()):
    rows, width = 2 * own.shape[0], own.shape[1]
    return on_core(
        project_kernel,
        (x_index, t_index, mix, own, other, gain, w_qkv, value_first, cosine, sine),
        [shaped(3, rows, PAIR)] * 4
        + [shaped(rows, width), shaped(RING, rows, PAIR), shaped(rows, width), shaped(8, PAIR)],
        scratch=[pltpu.VMEM((rows, PAIR), F32)] * 2 + [pltpu.SemaphoreType.DMA((4, 2))],
        smem=3, far=2, waits=waits, limit=5, us=3, name="project",
    )


def pick_kernel(z_ref, pair_ref, keep_ref, send_ref):
    keep_ref[...] = pair_ref[z_ref[0]]
    send_ref[...] = pair_ref[1 - z_ref[0]]


def pick(z_index, pair, waits=()):
    return on_core(
        pick_kernel, (z_index, pair), [shaped(*pair.shape[1:])] * 2, smem=1, waits=waits, limit=4, us=0.6, name="pick"
    )


def branch_kernel(x_ref, o0, o1, o2, o3, w_ref, v_ref, o_ref, part_ref, copy_ref):
    for k, arrived in enumerate((o0, o1, o2, o3)):
        o_ref[:, heads_at(x_ref, k)] = arrived[...]
    for part in halves(o_ref.shape[0]):
        part_ref[part] = jnp.dot(o_ref[part], w_ref[...], preferred_element_type=F32).astype(BF)
    copy_ref[...] = v_ref[...]


def branch(x_index, arrived, w_out, value, waits=()):
    rows, width = arrived[0].shape[0], w_out.shape[1]
    return on_core(
        branch_kernel,
        (x_index, *arrived, w_out, value),
        [shaped(rows, RING * PAIR), shaped(rows, width), jax.ShapeDtypeStruct(value.shape, BF)],
        smem=1, waits=waits, limit=4, us=1, name="branch",
    )


def put_halves(t_ref, which, keep_ref, send_ref, value):
    @pl.when(t_ref[0] == which)
    def _():
        keep_ref[...] = value

    @pl.when(t_ref[0] != which)
    def _():
        send_ref[...] = value


def pieces(units):
    cut = (units // PAIR + 1) // 2 * PAIR
    return [(0, cut), (cut, units)]


def weight_copies(wgu_ref, wd_ref, gu_buf, d_buf, sems):
    copies = []
    for index, (low, high) in enumerate(pieces(wd_ref.shape[0])):
        at = pl.ds(low, high - low)
        copies.append(
            [
                pltpu.make_async_copy(wgu_ref.at[:, :, at], gu_buf.at[:, :, at], sems.at[index, 0]),
                pltpu.make_async_copy(wd_ref.at[at, :], d_buf.at[at, :], sems.at[index, 1]),
            ]
        )
    return copies


def weight_scratch(width, units):
    return [
        pltpu.VMEM((2, width, units), BF),
        pltpu.VMEM((units, width), BF),
        pltpu.SemaphoreType.DMA((2, 2)),
    ]


def feed_kernel(t_ref, h_ref, p_ref, q_ref, gain_ref, wgu_ref, wd_ref,
                mine_ref, keep_ref, send_ref, n_ref, *rest):
    *saved, gu_buf, d_buf, sems, acc = rest
    copies = weight_copies(wgu_ref, wd_ref, gu_buf, d_buf, sems)
    for pair in copies:
        for copy in pair:
            copy.start()
    rows = halves(h_ref.shape[0])
    for which, part in enumerate(rows):
        middle = h_ref[part].astype(F32) + (p_ref[part].astype(F32) + q_ref[part].astype(F32))
        if saved:
            saved[0][part] = middle
        n_ref[part] = (middle * rms_scale(middle) * gain_ref[...]).astype(BF)

        @pl.when(t_ref[0] == which)
        def _():
            mine_ref[...] = middle

    for index, (low, high) in enumerate(pieces(d_buf.shape[0])):
        at = slice(low, high)
        for copy in copies[index]:
            copy.wait()
        for which, part in enumerate(rows):
            gate = jnp.dot(n_ref[part], gu_buf[0, :, at], preferred_element_type=F32)
            up = jnp.dot(n_ref[part], gu_buf[1, :, at], preferred_element_type=F32)
            act = (gate / (1.0 + jnp.exp(-gate)) * up).astype(BF)
            if saved:
                saved[1][part, at] = gate.astype(BF)
                saved[2][part, at] = up.astype(BF)
                saved[3][part, at] = act
            total = jnp.dot(act, d_buf[at, :], preferred_element_type=F32)
            if index == 0:
                acc[part] = total
            else:
                put_halves(t_ref, which, keep_ref, send_ref, (acc[part] + total).astype(BF))


def feed(t_index, hidden, own, other, gain, w_gu, w_down, save, waits=()):
    rows, width = hidden.shape
    units = w_down.shape[0]
    wide, half = shaped(rows, units), shaped(rows // 2, width)
    outs = [shaped(rows // 2, width, dtype=F32), half, half, shaped(rows, width)]
    if save:
        outs += [shaped(rows, width, dtype=F32), wide, wide, wide]
    return on_core(
        feed_kernel,
        (t_index, hidden, own, other, gain, w_gu, w_down),
        outs,
        scratch=weight_scratch(width, units) + [pltpu.VMEM((rows, width), F32)],
        smem=1, far=2, waits=waits, limit=14, us=7, name="feed",
    )


def feed_back_kernel(t_ref, own_ref, other_ref, gate_ref, up_ref, wgu_ref, wd_ref,
                     dgate_ref, dup_ref, part_ref, g_ref, gu_buf, d_buf, sems, acc):
    copies = weight_copies(wgu_ref, wd_ref, gu_buf, d_buf, sems)
    for which in (1, 0):
        for pair in copies:
            pair[which].start()
    g_ref[own_half(t_ref, g_ref.shape[0]), :] = own_ref[...]
    g_ref[far_half(t_ref, g_ref.shape[0]), :] = other_ref[...]
    for index, (low, high) in enumerate(pieces(d_buf.shape[0])):
        at = slice(low, high)
        copies[index][1].wait()
        for part in halves(g_ref.shape[0]):
            grad = across(g_ref[part], d_buf[at, :])
            gate = gate_ref[part, at].astype(F32)
            sigma = 1.0 / (1.0 + jnp.exp(-gate))
            up = up_ref[part, at].astype(F32)
            dgate_ref[part, at] = (grad * up * sigma * (1.0 + gate * (1.0 - sigma))).astype(BF)
            dup_ref[part, at] = (grad * gate * sigma).astype(BF)
        copies[index][0].wait()
        for part in halves(g_ref.shape[0]):
            total = across(dgate_ref[part, at], gu_buf[0, :, at]) + across(
                dup_ref[part, at], gu_buf[1, :, at]
            )
            if index == 0:
                acc[part] = total
            else:
                part_ref[part] = (acc[part] + total).astype(BF)


def feed_back(t_index, own, other, w_gu, w_down, gate, up, waits=(), us=7):
    rows, width = 2 * own.shape[0], own.shape[1]
    units = w_down.shape[0]
    wide = shaped(rows, units)
    return on_core(
        feed_back_kernel,
        (t_index, own, other, gate, up, w_gu, w_down),
        [wide, wide, shaped(rows, width), shaped(rows, width)],
        scratch=weight_scratch(width, units) + [pltpu.VMEM((rows, width), F32)],
        smem=1, far=2, waits=waits, limit=15, us=us, name="feed_back",
    )


def feed_terms_kernel(n_ref, g_ref, u_ref, out_ref):
    rows = n_ref.shape[1] // 32
    for low in range(0, n_ref.shape[1], 256):
        left = n_ref[:, low : low + 256]
        for spot, right in enumerate((g_ref, u_ref)):
            term = down_rows(left, right[...]).astype(BF)
            for index in range(256 // rows):
                out_ref[low // rows + index, spot * rows : (spot + 1) * rows, :] = term[
                    index * rows : (index + 1) * rows
                ]


def feed_terms(normed, dgate, dup, waits=()):
    width, units = normed.shape[1], dgate.shape[1]
    return on_core(
        feed_terms_kernel, (normed, dgate, dup), [shaped(32, width // 16, units)],
        waits=waits, limit=8, us=BRIEF, name="feed_terms",
    )[0]


def sum_kernel(*refs):
    total = refs[0][...].astype(F32)
    for ref in refs[1:-1]:
        total += ref[...].astype(F32)
    refs[-1][...] = total.astype(BF)


def summed(values, waits=()):
    shape = values[0].shape
    piece = pl.BlockSpec((shape[0] // 4, *shape[1:]), lambda i: (i, 0, 0))

    def body(*refs):
        sum_kernel(*refs[: len(values)], refs[-1])

    return pl.pallas_call(
        body,
        grid=(4,),
        in_specs=[piece] * len(values) + [pl.BlockSpec(memory_space=pl.ANY)] * len(waits),
        out_specs=piece,
        out_shape=shaped(*shape),
        compiler_params=pltpu.CompilerParams(vmem_limit_bytes=8 * 2**20),
        cost_estimate=lasting(BRIEF),
        name="summed",
    )(*values, *waits)


def middle_back_kernel(x_ref, t_ref, g_ref, m_ref, p_ref, q_ref, gain_ref, w_ref,
                       dm_ref, gm_ref, d0, d1, d2, d3, sum_ref, do_ref):
    rows = g_ref.shape[0]
    for which, part in enumerate(halves(rows)):
        grad = p_ref[part].astype(F32) + q_ref[part].astype(F32)
        inner, scale, unit = norm_back(m_ref[part], grad, gain_ref[...])
        middle = g_ref[part].astype(F32) + inner

        @pl.when(t_ref[0] == which)
        def _():
            dm_ref[...] = middle
            sum_ref[...] = jnp.sum(grad * unit, axis=0, keepdims=True)

        gm_ref[part] = middle.astype(BF)
        do_ref[part] = across(gm_ref[part], w_ref[...]).astype(BF)
    for k, out in enumerate((d0, d1, d2, d3)):
        out[...] = do_ref[:, heads_at(x_ref, k)]


def norm_back(hidden, grad, gain):
    scale = rms_scale(hidden)
    unit = hidden * scale
    weighted = grad * gain
    inner = scale * (weighted - unit * jnp.mean(weighted * unit, axis=-1, keepdims=True))
    return inner, scale, unit


def middle_back(x_index, t_index, grad, middle, own, other, gain, w_out, waits=(), us=2.3):
    rows, width = grad.shape
    return on_core(
        middle_back_kernel,
        (x_index, t_index, grad, middle, own, other, gain, w_out),
        [shaped(rows // 2, width, dtype=F32), shaped(rows, width)]
        + [shaped(rows, PAIR)] * 4
        + [shaped(1, width, dtype=F32)],
        scratch=[pltpu.VMEM((rows, RING * PAIR), BF)],
        smem=2, waits=waits, limit=8, us=us, name="middle_back",
    )


def project_back_kernel(x_ref, t_ref, g0, g1, g2, g3, w_ref, keep_ref, send_ref, d_ref):
    for k, grad in enumerate((g0, g1, g2, g3)):
        for c in range(3):
            d_ref[c, :, heads_at(x_ref, k)] = grad[c]
    for which, part in enumerate(halves(d_ref.shape[1])):
        total = sum(across(d_ref[c, part], w_ref[c]) for c in range(3)).astype(BF)
        put_halves(t_ref, which, keep_ref, send_ref, total)


def project_back(x_index, t_index, grads, w_qkv, waits=(), us=2.2):
    rows, width = grads[0].shape[1], w_qkv.shape[1]
    return on_core(
        project_back_kernel,
        (x_index, t_index, *grads, w_qkv),
        [shaped(rows // 2, width)] * 2,
        scratch=[pltpu.VMEM((3, rows, RING * PAIR), BF)],
        smem=2, waits=waits, limit=5, us=us, name="project_back",
    )


def input_back_kernel(t_ref, h_ref, dm_ref, p_ref, q_ref, gain_ref, n_ref, dh_ref, low_ref, half_ref):
    grad = p_ref[...].astype(F32) + q_ref[...].astype(F32)
    total = dm_ref[...] + norm_back(h_ref[...].astype(F32), grad, gain_ref[...])[0]
    dh_ref[...] = total
    low_ref[...] = total.astype(BF)
    half_ref[...] = n_ref[own_half(t_ref, n_ref.shape[0]), :]


def input_back(t_index, hidden, grad_middle, own, other, gain, normed, us=1.5):
    return on_core(
        input_back_kernel, (t_index, hidden, grad_middle, own, other, gain, normed),
        [shaped(*hidden.shape, dtype=F32), shaped(*hidden.shape), shaped(*hidden.shape)],
        smem=1, limit=5, us=us, name="input_back",
    )


def close_kernel(m_ref, p_ref, q_ref, out_ref):
    out_ref[...] = (m_ref[...] + (p_ref[...].astype(F32) + q_ref[...].astype(F32))).astype(BF)


def close(middle, own, other, waits=()):
    return on_core(
        close_kernel, (middle, own, other), [shaped(*own.shape)], waits=waits, limit=4, us=0.7, name="close"
    )[0]


DOWN_ROWS, OUT_AT, QKV_AT = 44, 48, 64


def put_by_z(z_ref, keep_ref, send_ref, device, rows, lanes, value):
    spot = device // 8 * 4 + device % 4
    put_halves(z_ref, device // 4 % 2, keep_ref.at[spot, rows, lanes], send_ref.at[spot, rows, lanes], value)


def early_terms_kernel(z_ref, act_ref, go_ref, o_ref, gm_ref, keep_ref, send_ref, down):
    width = go_ref.shape[1]
    units = act_ref.shape[1]
    for low in range(0, units, 256):
        high = min(low + 256, units)
        down[low:high, :] = down_rows(act_ref[:, low:high], go_ref[...])
    blank = jnp.zeros((OUT_AT - DOWN_ROWS, width), F32)
    everywhere = slice(0, width)
    for at in range(32):
        block = jnp.concatenate([down[at * DOWN_ROWS : (at + 1) * DOWN_ROWS, :], blank])
        put_by_z(z_ref, keep_ref, send_ref, at, slice(0, OUT_AT), everywhere, block.astype(BF))
    rows = o_ref.shape[1] // 32
    for low in range(0, o_ref.shape[1], 256):
        term = down_rows(o_ref[:, low : low + 256], gm_ref[...]).astype(BF)
        for index in range(256 // rows):
            put_by_z(
                z_ref, keep_ref, send_ref, low // rows + index, slice(OUT_AT, QKV_AT), everywhere,
                term[index * rows : (index + 1) * rows],
            )


def early_terms(z_index, act, grad_out, attended, grad_branch):
    width = grad_out.shape[1]
    return on_core(
        early_terms_kernel,
        (z_index, act, grad_out, attended, grad_branch),
        [shaped(16, QKV_AT, width)] * 2,
        scratch=[pltpu.VMEM((act.shape[1], width), F32)],
        smem=1, limit=9, us=BRIEF, name="early_terms",
    )


def qkv_terms_kernel(x_ref, t_ref, z_ref, n_ref, near_ref, far_ref, g0, g1, g2, g3,
                     w_ref, gain_ref, two_ref, keep_ref, send_ref, acc):
    half = near_ref.shape[1]
    rows, wide = n_ref.shape[1] // 32, 3 * PAIR

    def joined(grad, at):
        return jnp.concatenate([grad[c, at, :] for c in range(3)], axis=1)

    acc[...] = down_rows(joined(g0, slice(None)), n_ref[...])
    for shift, grad in ((1, g1), (2, g2), (3, g3)):
        source = lax.rem(x_ref[0] + RING - shift, RING)
        acc[...] += down_rows(joined(grad, own_half(t_ref, 2 * half)), near_ref[source]) + down_rows(
            joined(grad, far_half(t_ref, 2 * half)), far_ref[source]
        )
    sums = []
    for low in range(0, acc.shape[1], 256):
        term = acc[:, low : low + 256].T.astype(BF)
        for index in range(256 // rows):
            at = low // rows + index
            block = term[index * rows : (index + 1) * rows]
            both = jnp.concatenate([block[: rows // 2], block[rows // 2 :]], axis=1)
            put_by_z(z_ref, keep_ref, send_ref, at, slice(0, rows // 2), slice(0, 2 * wide), both)
        total = jnp.zeros((1, 256), F32)
        for c in range(3):
            weight = w_ref[c, low : low + 256, heads_at(x_ref, 0)].astype(F32).T
            total += jnp.sum(weight * acc[c * PAIR : (c + 1) * PAIR, low : low + 256], axis=0, keepdims=True)
        sums.append(total / gain_ref[:, low : low + 256])
    sums += [two_ref[:, low : low + 256] for low in range(0, acc.shape[1], 256)]
    sums = jnp.concatenate(sums)
    high = sums.astype(BF)
    sums = jnp.concatenate([high, (sums - high.astype(F32)).astype(BF)])
    for out in (keep_ref, send_ref):
        out[:, :, 2 * wide :] = jnp.broadcast_to(sums[None], (out.shape[0], *sums.shape))


def qkv_terms(x_index, t_index, z_index, normed, near, far, grads, w_qkv, gain, gain_sum):
    width = normed.shape[1]
    return on_core(
        qkv_terms_kernel,
        (x_index, t_index, z_index, normed, near, far, *grads, w_qkv, gain, gain_sum),
        [shaped(16, width // 64, width)] * 2,
        scratch=[pltpu.VMEM((3 * PAIR, width), F32)],
        smem=3, limit=6, us=BRIEF, name="qkv_terms",
    )


def rest_kernel(a_ref, b_ref, c_ref, d_ref, out_ref):
    rows, lanes = c_ref.shape[1] // 2, 6 * PAIR
    out_ref[:, :QKV_AT, :] = (a_ref[...].astype(F32) + b_ref[...].astype(F32)).astype(BF)
    late = c_ref[...].astype(F32) + d_ref[...].astype(F32)
    out_ref[:, QKV_AT:, :lanes] = late[:, :, :lanes].astype(BF)
    sums = late[:, :rows, lanes:] + late[:, rows:, lanes:]
    high = sums.astype(BF)
    out_ref[:, QKV_AT : QKV_AT + rows, lanes:] = high
    out_ref[:, QKV_AT + rows :, lanes:] = (sums - high.astype(F32)).astype(BF)


def finish_kernel(rest_ref, down_ref, out_ref, qkv_ref, gain_ref):
    count, total, width = rest_ref.shape
    wide, rows = 3 * PAIR, total - QKV_AT

    def added(low, high):
        value = rest_ref[0, low:high, :].astype(F32)
        for source in range(1, count):
            value += rest_ref[source, low:high, :].astype(F32)
        return value

    down_ref[...] = added(0, OUT_AT)[:DOWN_ROWS]
    out_ref[...] = added(OUT_AT, QKV_AT)
    gains = jnp.zeros((rows, width - 2 * wide), F32)
    for x in range(RING):
        value = rest_ref[x, QKV_AT:, :].astype(F32)
        for source in range(x + RING, count, RING):
            value += rest_ref[source, QKV_AT:, :].astype(F32)
        for half in range(2):
            for c in range(3):
                low = half * wide + c * PAIR
                qkv_ref[c, half * rows : (half + 1) * rows, x * PAIR : (x + 1) * PAIR] = value[
                    :, low : low + PAIR
                ]
        gains += value[:, 2 * wide :]
    gains = gains[: rows // 2] + gains[rows // 2 :]
    for index in range(rows // 2):
        low = index % 4 * 256
        gain_ref[index // 4 : index // 4 + 1, low : low + 256] = gains[index : index + 1]


def finish(rest):
    width = rest.shape[2]
    rows = 2 * (rest.shape[1] - QKV_AT)
    return on_core(
        finish_kernel,
        (rest,),
        [
            shaped(DOWN_ROWS, width, dtype=F32),
            shaped(QKV_AT - OUT_AT, width, dtype=F32),
            shaped(3, rows, RING * PAIR, dtype=F32),
            shaped(2, width, dtype=F32),
        ],
        limit=4, us=BRIEF, name="finish",
    )


def rest_sum(early, early_got, late, late_got, waits=()):
    count, _, width = early.shape
    first = pl.BlockSpec((count // 4, QKV_AT, width), lambda i: (i, 0, 0))
    second = pl.BlockSpec((count // 4, *late.shape[1:]), lambda i: (i, 0, 0))
    total = QKV_AT + late.shape[1]

    def body(*refs):
        rest_kernel(*refs[:4], refs[-1])

    return pl.pallas_call(
        body,
        grid=(4,),
        in_specs=[first, first, second, second] + [pl.BlockSpec(memory_space=pl.ANY)] * len(waits),
        out_specs=pl.BlockSpec((count // 4, total, width), lambda i: (i, 0, 0)),
        out_shape=shaped(count, total, width),
        compiler_params=pltpu.CompilerParams(vmem_limit_bytes=8 * 2**20),
        cost_estimate=lasting(BRIEF),
        name="rest_sum",
    )(early, early_got, late, late_got, *waits)


def first_visible(ends_ref, places):
    start = jnp.zeros_like(places)
    for index in range(4):
        start = jnp.where(places >= ends_ref[index], ends_ref[index], start)
    return start


def attend_kernel(x_ref, ends_ref, m0, m1, m2, m3, o0, o1, o2, o3, lse_ref, out_t, keys, query_t,
                  value_t, acc):
    x = x_ref[0]
    lanes = lax.broadcasted_iota(jnp.int32, (BLOCK, PAIR), 1)
    for shift, message in enumerate((m0, m1, m2, m3)):
        source = lax.rem(x + RING - shift, RING)
        for part in range(4):
            at = pl.ds(pl.multiple_of(place_block(source, part) * BLOCK, BLOCK), BLOCK)
            inside = slice(part * BLOCK, (part + 1) * BLOCK)
            block = message[1, inside, :]
            keys[0, at, :] = jnp.where(lanes < HD, block, jnp.zeros_like(block))
            keys[1, at, :] = jnp.where(lanes < HD, jnp.zeros_like(block), block)
            query_t[:, at] = message[0, inside, :].T
            value_t[:, at] = message[2, inside, :].T

    def one_query_block(qi, _):
        q_at = pl.ds(pl.multiple_of(qi * QUERIES, QUERIES), QUERIES)
        places = qi * QUERIES + lax.broadcasted_iota(jnp.int32, (1, QUERIES), 1)
        start = first_visible(ends_ref, places)
        acc[...] = jnp.zeros_like(acc)

        def one_key_block(kj, carry, diagonal):
            k_at = pl.ds(pl.multiple_of(kj * KEYS, KEYS), KEYS)
            key_places = kj * KEYS + lax.broadcasted_iota(jnp.int32, (KEYS, QUERIES), 0)
            visible = key_places >= start
            if diagonal:
                visible = visible & (key_places <= places)
            after = []
            for head in range(2):
                highest, total = carry[head]
                scores = jnp.dot(keys[head, k_at, :], query_t[:, q_at], preferred_element_type=F32)
                scores = jnp.where(visible, scores, NEGATIVE)
                higher = jnp.maximum(highest, jnp.max(scores, axis=0, keepdims=True))
                shrink = jnp.exp(highest - higher)
                weight = jnp.exp(scores - higher)
                total = total * shrink + jnp.sum(weight, axis=0, keepdims=True)
                part = slice(head * HD, (head + 1) * HD)
                acc[part, :] = acc[part, :] * shrink + jnp.dot(
                    value_t[part, k_at], weight.astype(BF), preferred_element_type=F32
                )
                after.append((higher, total))
            return tuple(after)

        begin = (jnp.full((1, QUERIES), NEGATIVE, F32), jnp.zeros((1, QUERIES), F32))
        ratio = QUERIES // KEYS
        done = lax.fori_loop(
            0, qi * ratio, lambda kj, carry: one_key_block(kj, carry, False), (begin, begin)
        )
        for step in range(ratio):
            done = one_key_block(qi * ratio + step, done, True)
        for head in range(2):
            highest, total = done[head]
            part = slice(head * HD, (head + 1) * HD)
            out_t[part, q_at] = acc[part, :] / total
            lse_ref[head : head + 1, q_at] = highest + jnp.log(total)
        return 0

    lax.fori_loop(0, LEN // QUERIES, one_query_block, 0)
    for shift, out in enumerate((o0, o1, o2, o3)):
        source = lax.rem(x + RING - shift, RING)
        for part in range(4):
            at = pl.ds(pl.multiple_of(place_block(source, part) * BLOCK, BLOCK), BLOCK)
            out[part * BLOCK : (part + 1) * BLOCK, :] = out_t[:, at].T.astype(BF)


def attend(x_index, ends, messages, waits=()):
    rows = messages[0].shape[1]
    return on_core(
        attend_kernel,
        (x_index, ends, *messages),
        [shaped(rows, PAIR)] * 4 + [shaped(2, LEN, dtype=F32), shaped(PAIR, LEN, dtype=F32)],
        scratch=[
            pltpu.VMEM((2, LEN, PAIR), BF),
            pltpu.VMEM((PAIR, LEN), BF),
            pltpu.VMEM((PAIR, LEN), BF),
            pltpu.VMEM((PAIR, QUERIES), F32),
        ],
        smem=2, waits=waits, limit=12, us=13, name="attend",
    )


def attend_back_kernel(x_ref, ends_ref, mix_ref, m0, m1, m2, m3, d0, d1, d2, d3, lse_ref, out_t,
                       dv1_ref, cos_ref, sin_ref, g0, g1, g2, g3, dv_ref, keys, values, queries, grads,
                       key_t, query_t, grad_t, delta, grad_k, grad_v, grad_q_t):
    x = x_ref[0]
    lanes = lax.broadcasted_iota(jnp.int32, (BLOCK, PAIR), 1)
    for shift, (message, arrived) in enumerate(((m0, d0), (m1, d1), (m2, d2), (m3, d3))):
        source = lax.rem(x + RING - shift, RING)
        for part in range(4):
            at = pl.ds(pl.multiple_of(place_block(source, part) * BLOCK, BLOCK), BLOCK)
            inside = slice(part * BLOCK, (part + 1) * BLOCK)
            query, key, value = message[0, inside, :], message[1, inside, :], message[2, inside, :]
            grad = arrived[inside, :]
            zero = jnp.zeros_like(query)
            for both, block in ((keys, key), (values, value), (queries, query), (grads, grad)):
                both[0, at, :] = jnp.where(lanes < HD, block, zero)
                both[1, at, :] = jnp.where(lanes < HD, zero, block)
            key_t[:, at] = key.T
            query_t[:, at] = query.T
            turned_grad = grad.T
            grad_t[:, at] = turned_grad
            product = out_t[:, at] * turned_grad.astype(F32)
            delta[0:1, at] = jnp.sum(product[:HD], axis=0, keepdims=True)
            delta[1:2, at] = jnp.sum(product[HD:], axis=0, keepdims=True)
    grad_k[...] = jnp.zeros_like(grad_k)
    grad_v[...] = jnp.zeros_like(grad_v)
    grad_q_t[...] = jnp.zeros_like(grad_q_t)

    def one_query_block(qi, _):
        q_at = pl.ds(pl.multiple_of(qi * BACK_QUERIES, BACK_QUERIES), BACK_QUERIES)
        places = qi * BACK_QUERIES + lax.broadcasted_iota(jnp.int32, (1, BACK_QUERIES), 1)
        start = first_visible(ends_ref, places)

        def one_key_block(kj, carry):
            k_at = pl.ds(pl.multiple_of(kj * BACK_KEYS, BACK_KEYS), BACK_KEYS)
            key_places = kj * BACK_KEYS + lax.broadcasted_iota(jnp.int32, (BACK_KEYS, BACK_QUERIES), 0)
            visible = (key_places <= places) & (key_places >= start)
            for head in range(2):
                part = slice(head * HD, (head + 1) * HD)
                scores = jnp.dot(keys[head, k_at, :], query_t[:, q_at], preferred_element_type=F32)
                scores = jnp.where(visible, scores, NEGATIVE)
                weight = jnp.exp(scores - lse_ref[head : head + 1, q_at])
                grad_w = jnp.dot(values[head, k_at, :], grad_t[:, q_at], preferred_element_type=F32)
                grad_s = (weight * (grad_w - delta[head : head + 1, q_at])).astype(BF)
                grad_v[k_at, :] += jnp.dot(
                    weight.astype(BF), grads[head, q_at, :], preferred_element_type=F32
                )
                grad_k[k_at, :] += jnp.dot(grad_s, queries[head, q_at, :], preferred_element_type=F32)
                grad_q_t[part, q_at] += jnp.dot(
                    key_t[part, k_at], grad_s, preferred_element_type=F32
                )
            return carry

        return lax.fori_loop(0, (qi + 1) * (BACK_QUERIES // BACK_KEYS), one_key_block, 0)

    lax.fori_loop(0, LEN // BACK_QUERIES, one_query_block, 0)
    for shift, out in enumerate((g0, g1, g2, g3)):
        source = lax.rem(x + RING - shift, RING)
        for part in range(4):
            at = pl.ds(pl.multiple_of(place_block(source, part) * BLOCK, BLOCK), BLOCK)
            inside = slice(part * BLOCK, (part + 1) * BLOCK)
            cosine, sine = cos_ref[at, :], sin_ref[at, :]
            grad_q = grad_q_t[:, at].T * HD ** (-0.5)
            out[0, inside, :] = turned(grad_q, cosine, sine, -1.0).astype(BF)
            out[1, inside, :] = turned(grad_k[at, :], cosine, sine, -1.0).astype(BF)
            grad_value = mix_ref[0] * grad_v[at, :] + mix_ref[1] * dv1_ref[shift, inside, :].astype(F32)
            out[2, inside, :] = grad_value.astype(BF)
            dv_ref[shift, inside, :] = grad_value.astype(BF)


def attend_back(x_index, ends, mix, messages, arrived, lse, out_t, dv1, cosine, sine, waits=(), us=20):
    rows = messages[0].shape[1]
    return on_core(
        attend_back_kernel,
        (x_index, ends, mix, *messages, *arrived, lse, out_t, dv1, cosine, sine),
        [shaped(3, rows, PAIR)] * 4 + [shaped(RING, rows, PAIR)],
        scratch=[pltpu.VMEM((2, LEN, PAIR), BF)] * 4
        + [pltpu.VMEM((PAIR, LEN), BF)] * 3
        + [
            pltpu.VMEM((2, LEN), F32),
            pltpu.VMEM((LEN, PAIR), F32),
            pltpu.VMEM((LEN, PAIR), F32),
            pltpu.VMEM((PAIR, LEN), F32),
        ],
        smem=3, waits=waits, limit=13, us=us, name="attend_back",
    )


def out_and_back(values, sign):
    return [values[0]] + [moved(values[shift], "x", sign * shift) for shift in range(1, RING)]


def groups(kinds):
    found = {}
    for index in range(32):
        place = {"y": index // 8, "z": index // 4 % 2, "x": index % 4}
        found.setdefault(tuple(place[k] for k in "yzx" if k not in kinds), []).append(index)
    return list(found.values())


def all_to_all(value, kinds):
    return lax.all_to_all(value, "dp", 0, 0, axis_index_groups=groups(kinds))


def per_device(tokens, cotangent, doc_lengths, gains, wqkv, wo, wgu, wd):
    first = lax.axis_index("section") == 0
    tensor = lax.axis_index("tensor")
    position = lax.axis_index("dp")
    y, z, x = position // 8, position // 4 % 2, position % 4
    x_index, z_index, t_index = [v.astype(jnp.int32).reshape(1) for v in (x, z, tensor)]
    width = tokens.shape[2]

    def in_order(keep, got):
        got = got.astype(keep.dtype)
        return jnp.where(z == 0, jnp.stack([keep, got]), jnp.stack([got, keep]))

    def regrouped(pair):
        keep = lax.dynamic_index_in_dim(pair, z, 0, keepdims=False)
        send = lax.dynamic_index_in_dim(pair, 1 - z, 0, keepdims=False)
        return in_order(keep, moved(send.astype(BF), "z", 1))

    lens = lax.dynamic_slice(doc_lengths, (z, y, 0), (1, 1, 4))
    ends = jnp.cumsum(lens.reshape(4), dtype=jnp.int32)
    cosine, sine = rotary_tables()
    w_qkv = jnp.transpose(wqkv[0], (1, 0, 2))
    w_out, w_down = wo[0], wd[0]
    gain_one, gain_two = gains[0, 0:1], gains[0, 1:2]
    mix = jnp.where(first, jnp.array([1.0, 0.0], F32), jnp.array([0.5, 0.5], F32))
    mix_back = jnp.where(first, jnp.array([1.0, 1.0], F32), jnp.array([0.5, 0.0], F32))

    def handed(value, pairs):
        return lax.ppermute(value, "section", pairs)

    def first_half(own, value_first):
        *messages, normed, value, hidden, zero = project(
            x_index, t_index, mix, own, swapped(own), gain_one, w_qkv, value_first, cosine, sine
        )
        return out_and_back(messages, 1), normed, value, hidden, zero

    def second_half(hidden, outs, value, save, waits=()):
        attended, part, value = branch(x_index, out_and_back(outs, -1), w_out, value, waits=waits)
        mine, keep, send, normed_two, *more = feed(
            t_index, hidden, part, swapped(part), gain_two, w_gu, w_down, save
        )
        return mine, keep, swapped(send), value, (attended, normed_two, *more)

    own_rows = regrouped(tokens).reshape(2 * BLOCK, width)
    no_value = jnp.zeros((RING, 4 * BLOCK, PAIR), BF)

    messages, _, value, hidden, zero = first_half(own_rows, no_value)
    w_gu = jnp.transpose(wgu[0] + zero[0, 0], (1, 0, 2))
    *outs, _, _ = attend(x_index, ends, messages, waits=(seen(w_gu),))
    cot_keep, cot_send = pick(z_index, cotangent, waits=(seen(outs[0]),))
    top_grad = in_order(cot_keep, moved(cot_send, "z", 1)).reshape(2 * BLOCK, width)
    mine, keep, got, value, _ = second_half(hidden, outs, value, False)
    v_in = handed(value, [(0, 1)])
    result = close(mine, keep, got, waits=(seen(v_in),))
    own = jnp.where(first, own_rows, handed(result, [(0, 1)]))

    messages, normed, value, hidden, _ = first_half(own, v_in)
    *outs, lse, out_t = attend(x_index, ends, messages)
    mine, keep, got, _, saved = second_half(hidden, outs, value, True, waits=(seen(top_grad),))
    attended, normed_two, middle, gate, up, act = saved
    def first_back(own_grad, us=7):
        return feed_back(t_index, own_grad, swapped(own_grad), w_gu, w_down, gate, up, us=us)

    def second_back(grad, part, waits=(), us=2.3):
        grad_middle, grad_branch, *sends, gain_sum = middle_back(
            x_index, t_index, grad, middle, part, swapped(part), gain_two, w_out, waits=waits, us=us
        )
        return grad_middle, grad_branch, out_and_back(sends, 1), gain_sum

    def third_back(arrived, grad_value, waits=(), us=20):
        return attend_back(
            x_index, ends, mix_back, messages, arrived, lse, out_t, grad_value, cosine, sine, waits=waits, us=us
        )

    def fourth_back(grads, grad_middle, waits=(), us=2):
        keep, send = project_back(
            x_index, t_index, out_and_back(grads, -1), w_qkv, waits=waits, us=us
        )
        return *input_back(
            t_index, own, grad_middle, keep, swapped(send), gain_one, normed, us=us
        ), keep

    _, _, part, grad = first_back(top_grad)
    grad_middle, _, arrived, _ = second_back(grad, part)
    *grads, grad_value = third_back(arrived, no_value)
    result = close(mine, keep, got, waits=(seen(grad_value),))
    acts = regrouped(result.reshape(2, BLOCK, width))[None]
    gv_in = handed(grad_value, [(1, 0)])
    _, grad_hidden, half, _ = fourth_back(
        grads, grad_middle, waits=(seen(gv_in), seen(acts[0, 0]))
    )
    near = lax.all_gather(half, "dp", axis_index_groups=groups("x"))
    own_grad = jnp.where(first, handed(grad_hidden, [(1, 0)]), top_grad)

    dgate, dup, part, grad_out = first_back(own_grad, us=BRIEF)
    grad_middle, grad_branch, arrived, gain_sum = second_back(grad_out, part, us=BRIEF)
    feed_term = feed_terms(normed_two, dgate, dup, waits=(seen(grad_branch),))
    feed_sum = lax.psum_scatter(
        feed_term, "dp", scatter_dimension=0, axis_index_groups=groups("y"), tiled=True
    )
    early, early_send = early_terms(z_index, act, grad_out, attended, grad_branch)
    early_got = moved(early_send, "z", 1)
    far = swapped(near)
    *grads, _ = third_back(arrived, gv_in, waits=(seen(far), seen(early), seen(feed_term)), us=BRIEF)
    late, late_send = qkv_terms(
        x_index, t_index, z_index, normed, near, far, grads, w_qkv, gain_one, gain_sum
    )
    late_got = moved(late_send, "z", 1)
    grad_hidden, _, _, last = fourth_back(grads, grad_middle, waits=(seen(late),), us=BRIEF)
    rest = rest_sum(early, early_got, late, late_got, waits=(seen(last),))
    dins = regrouped(grad_hidden.reshape(2, BLOCK, width))[None]
    feed_sum = summed([feed_sum], waits=(seen(rest), seen(dins[0, 0])))
    feed_share = jnp.sum(all_to_all(feed_sum, "zx").astype(F32), axis=0)
    feed_share = feed_share.reshape(2, width // 32, -1)
    down_share, out_share, qkv_share, gain_total = finish(all_to_all(rest, "yx"))
    return (
        acts,
        dins,
        jnp.transpose(qkv_share, (1, 0, 2))[None],
        out_share[None],
        jnp.transpose(feed_share, (1, 0, 2))[None],
        down_share[None],
        (gain_total + swapped(gain_total))[None],
    )


def solution(mesh):
    placed = (
        P(None, ("tensor", "dp"), None),
        P(None, ("tensor", "dp"), None),
        P(),
        P("section", None, None),
        P("section", None, None, "tensor"),
        P("section", "tensor", None),
        P("section", None, None, "tensor"),
        P("section", "tensor", None),
    )
    return jax.shard_map(
        per_device,
        mesh=mesh,
        in_specs=placed,
        out_specs=(
            P("section", None, ("tensor", "dp"), None),
            P("section", None, ("tensor", "dp"), None),
            P("section", "dp", None, "tensor"),
            P("section", ("tensor", "dp"), None),
            P("section", "dp", None, "tensor"),
            P("section", ("tensor", "dp"), None),
            P("section", None, None),
        ),
        check_vma=False,
    )
```

```python
import jax
import jax.numpy as jnp
import numpy as np
from jax import lax
from jax.experimental import pallas as pl
from jax.experimental.pallas import tpu as pltpu
from jax.sharding import PartitionSpec as P

HD = 64
LEN = 2048
RING = 4
BLOCK = 128
PAIR = 2 * HD
EPSILON = 1e-06
BRIEF = 0.001
NEGATIVE = -1e30
KEYS = 512
BACK_KEYS = 256
BF = jnp.bfloat16
F32 = jnp.float32


def along(kind, shift):
    pairs = []
    for index in range(32):
        y, z, x = index // 8, index // 4 % 2, index % 4
        if kind == "x":
            x = (x + shift) % 4
        elif kind == "y":
            y = (y + shift) % 4
        else:
            z = (z + shift) % 2
        pairs.append((index, y * 8 + z * 4 + x))
    return pairs


def moved(value, kind, shift):
    return lax.ppermute(value, "dp", along(kind, shift))


def swapped(value):
    return lax.ppermute(value, "tensor", [(0, 1), (1, 0)])


def rms_scale(hidden):
    return lax.rsqrt(jnp.mean(hidden * hidden, axis=-1, keepdims=True) + EPSILON)


def rotary_tables():
    half = HD // 2
    freqs = np.float32(10000.0) ** (-np.arange(half, dtype=np.float32) / np.float32(half))
    angles = np.arange(LEN, dtype=np.float32)[:, None] * freqs[None, :]
    return [jnp.asarray(np.tile(f(angles).astype(np.float32), (1, 4))) for f in (np.cos, np.sin)]


def low_lanes(shape):
    return lax.broadcasted_iota(jnp.int32, shape, 1) % HD < HD // 2


def turned(u, cosine, sine, sign):
    ahead = pltpu.roll(u, PAIR - HD // 2, 1)
    behind = pltpu.roll(u, HD // 2, 1)
    cross = jnp.where(low_lanes(u.shape), -sign * ahead, sign * behind)
    return u * cosine + cross * sine


def place_block(source, part):
    return (source, 4 + source, 15 - source, 11 - source)[part]


def lasting(us):
    return pl.CostEstimate(flops=int(us * 1.1e9), bytes_accessed=int(us * 3.6e6), transcendentals=0)


def on_core(kernel, ins, outs, *, scratch=(), smem=0, far=0, waits=(), limit=24, us, name):
    spots = [pl.BlockSpec(memory_space=pltpu.SMEM)] * smem
    spots += [pl.BlockSpec(memory_space=pltpu.VMEM)] * (len(ins) - smem - far)
    spots += [pl.BlockSpec(memory_space=pltpu.HBM)] * far
    spots += [pl.BlockSpec(memory_space=pl.ANY)] * len(waits)
    taken, given = len(ins), len(outs)

    def body(*refs):
        kernel(*refs[:taken], *refs[taken + len(waits) :])

    return pl.pallas_call(
        body,
        in_specs=spots,
        out_specs=[pl.BlockSpec(memory_space=pltpu.VMEM)] * given,
        out_shape=list(outs),
        scratch_shapes=list(scratch),
        compiler_params=pltpu.CompilerParams(vmem_limit_bytes=limit * 2**20),
        cost_estimate=lasting(us),
        name=name,
    )(*ins, *waits)


def seen(value):
    return value[(0,) * (value.ndim - 2)][:8, :PAIR]


def shaped(*shape, dtype=BF):
    return jax.ShapeDtypeStruct(shape, dtype)


def heads_at(x_ref, shift):
    return pl.ds(pl.multiple_of(lax.rem(x_ref[0] + shift, RING) * PAIR, PAIR), PAIR)


def halves(rows):
    return [slice(0, rows // 2), slice(rows // 2, rows)]


def across(left, right):
    return lax.dot_general(left, right, (((1,), (1,)), ((), ())), preferred_element_type=F32)


def down_rows(left, right):
    return lax.dot_general(left, right, (((0,), (0,)), ((), ())), preferred_element_type=F32)


def own_half(t_ref, rows):
    return pl.ds(pl.multiple_of(t_ref[0] * (rows // 2), rows // 2), rows // 2)


def far_half(t_ref, rows):
    return pl.ds(pl.multiple_of((1 - t_ref[0]) * (rows // 2), rows // 2), rows // 2)


def project_kernel(x_ref, t_ref, mix_ref, own_ref, other_ref, gain_ref, w_ref, v1_ref, cos_ref, sin_ref,
                   m0, m1, m2, m3, n_ref, v_ref, h_ref, zero_ref, cos_buf, sin_buf, sems):
    copies = []
    for part in range(4):
        at = pl.ds(pl.multiple_of(place_block(x_ref[0], part) * BLOCK, BLOCK), BLOCK)
        to = pl.ds(part * BLOCK, BLOCK)
        copies.append(pltpu.make_async_copy(cos_ref.at[at], cos_buf.at[to], sems.at[part, 0]))
        copies.append(pltpu.make_async_copy(sin_ref.at[at], sin_buf.at[to], sems.at[part, 1]))
    for copy in copies:
        copy.start()
    zero_ref[...] = jnp.zeros_like(zero_ref)
    rows = h_ref.shape[0]
    h_ref[own_half(t_ref, rows), :] = own_ref[...]
    h_ref[far_half(t_ref, rows), :] = other_ref[...]
    for part in halves(rows):
        h = h_ref[part].astype(F32)
        n_ref[part] = (h * rms_scale(h) * gain_ref[...]).astype(BF)
    for copy in copies:
        copy.wait()
    outs = (m0, m1, m2, m3)
    for pair in ((0, 1), (2, 3)):
        weight = jnp.concatenate(
            [w_ref[c, :, heads_at(x_ref, k)] for k in pair for c in range(3)], axis=1
        )
        for part in halves(rows):
            both = jnp.dot(n_ref[part], weight, preferred_element_type=F32)
            cosine, sine = cos_buf[part], sin_buf[part]
            for index, k in enumerate(pair):
                query, key, value = [
                    both[:, (3 * index + c) * PAIR : (3 * index + c + 1) * PAIR] for c in range(3)
                ]
                outs[k][0, part] = (turned(query, cosine, sine, 1.0) * HD ** (-0.5)).astype(BF)
                outs[k][1, part] = turned(key, cosine, sine, 1.0).astype(BF)
                value = mix_ref[0] * value + mix_ref[1] * v1_ref[k, part].astype(F32)
                outs[k][2, part] = value.astype(BF)
                v_ref[k, part] = value.astype(BF)


def project(x_index, t_index, mix, own, other, gain, w_qkv, value_first, cosine, sine, waits=()):
    rows, width = 2 * own.shape[0], own.shape[1]
    return on_core(
        project_kernel,
        (x_index, t_index, mix, own, other, gain, w_qkv, value_first, cosine, sine),
        [shaped(3, rows, PAIR)] * 4
        + [shaped(rows, width), shaped(RING, rows, PAIR), shaped(rows, width), shaped(8, PAIR)],
        scratch=[pltpu.VMEM((rows, PAIR), F32)] * 2 + [pltpu.SemaphoreType.DMA((4, 2))],
        smem=3, far=2, waits=waits, limit=5, us=3, name="project",
    )


def pick_kernel(z_ref, pair_ref, keep_ref, send_ref):
    keep_ref[...] = pair_ref[z_ref[0]]
    send_ref[...] = pair_ref[1 - z_ref[0]]


def pick(z_index, pair, waits=()):
    return on_core(
        pick_kernel, (z_index, pair), [shaped(*pair.shape[1:])] * 2, smem=1, waits=waits, limit=4, us=0.6, name="pick"
    )


def branch_kernel(x_ref, o0, o1, o2, o3, w_ref, v_ref, o_ref, part_ref, copy_ref):
    for k, arrived in enumerate((o0, o1, o2, o3)):
        o_ref[:, heads_at(x_ref, k)] = arrived[...]
    for part in halves(o_ref.shape[0]):
        part_ref[part] = jnp.dot(o_ref[part], w_ref[...], preferred_element_type=F32).astype(BF)
    copy_ref[...] = v_ref[...]


def branch(x_index, arrived, w_out, value, waits=()):
    rows, width = arrived[0].shape[0], w_out.shape[1]
    return on_core(
        branch_kernel,
        (x_index, *arrived, w_out, value),
        [shaped(rows, RING * PAIR), shaped(rows, width), jax.ShapeDtypeStruct(value.shape, BF)],
        smem=1, waits=waits, limit=4, us=1, name="branch",
    )


def put_halves(t_ref, which, keep_ref, send_ref, value):
    @pl.when(t_ref[0] == which)
    def _():
        keep_ref[...] = value

    @pl.when(t_ref[0] != which)
    def _():
        send_ref[...] = value


def pieces(units):
    cut = (units // PAIR + 1) // 2 * PAIR
    return [(0, cut), (cut, units)]


def weight_copies(wgu_ref, wd_ref, gu_buf, d_buf, sems):
    copies = []
    for index, (low, high) in enumerate(pieces(wd_ref.shape[0])):
        at = pl.ds(low, high - low)
        copies.append(
            [
                pltpu.make_async_copy(wgu_ref.at[:, :, at], gu_buf.at[:, :, at], sems.at[index, 0]),
                pltpu.make_async_copy(wd_ref.at[at, :], d_buf.at[at, :], sems.at[index, 1]),
            ]
        )
    return copies


def weight_scratch(width, units):
    return [
        pltpu.VMEM((2, width, units), BF),
        pltpu.VMEM((units, width), BF),
        pltpu.SemaphoreType.DMA((2, 2)),
    ]


def feed_kernel(t_ref, h_ref, p_ref, q_ref, gain_ref, wgu_ref, wd_ref,
                mine_ref, keep_ref, send_ref, n_ref, *rest):
    *saved, gu_buf, d_buf, sems, acc = rest
    copies = weight_copies(wgu_ref, wd_ref, gu_buf, d_buf, sems)
    for pair in copies:
        for copy in pair:
            copy.start()
    rows = halves(h_ref.shape[0])
    for which, part in enumerate(rows):
        middle = h_ref[part].astype(F32) + (p_ref[part].astype(F32) + q_ref[part].astype(F32))
        if saved:
            saved[0][part] = middle
        n_ref[part] = (middle * rms_scale(middle) * gain_ref[...]).astype(BF)

        @pl.when(t_ref[0] == which)
        def _():
            mine_ref[...] = middle

    for index, (low, high) in enumerate(pieces(d_buf.shape[0])):
        at = slice(low, high)
        for copy in copies[index]:
            copy.wait()
        for which, part in enumerate(rows):
            gate = jnp.dot(n_ref[part], gu_buf[0, :, at], preferred_element_type=F32)
            up = jnp.dot(n_ref[part], gu_buf[1, :, at], preferred_element_type=F32)
            act = (gate / (1.0 + jnp.exp(-gate)) * up).astype(BF)
            if saved:
                saved[1][part, at] = gate.astype(BF)
                saved[2][part, at] = up.astype(BF)
                saved[3][part, at] = act
            total = jnp.dot(act, d_buf[at, :], preferred_element_type=F32)
            if index == 0:
                acc[part] = total
            else:
                put_halves(t_ref, which, keep_ref, send_ref, (acc[part] + total).astype(BF))


def feed(t_index, hidden, own, other, gain, w_gu, w_down, save, waits=()):
    rows, width = hidden.shape
    units = w_down.shape[0]
    wide, half = shaped(rows, units), shaped(rows // 2, width)
    outs = [shaped(rows // 2, width, dtype=F32), half, half, shaped(rows, width)]
    if save:
        outs += [shaped(rows, width, dtype=F32), wide, wide, wide]
    return on_core(
        feed_kernel,
        (t_index, hidden, own, other, gain, w_gu, w_down),
        outs,
        scratch=weight_scratch(width, units) + [pltpu.VMEM((rows, width), F32)],
        smem=1, far=2, waits=waits, limit=14, us=7, name="feed",
    )


def feed_back_kernel(t_ref, own_ref, other_ref, gate_ref, up_ref, wgu_ref, wd_ref,
                     dgate_ref, dup_ref, part_ref, g_ref, gu_buf, d_buf, sems, acc):
    copies = weight_copies(wgu_ref, wd_ref, gu_buf, d_buf, sems)
    for which in (1, 0):
        for pair in copies:
            pair[which].start()
    g_ref[own_half(t_ref, g_ref.shape[0]), :] = own_ref[...]
    g_ref[far_half(t_ref, g_ref.shape[0]), :] = other_ref[...]
    for index, (low, high) in enumerate(pieces(d_buf.shape[0])):
        at = slice(low, high)
        copies[index][1].wait()
        for part in halves(g_ref.shape[0]):
            grad = across(g_ref[part], d_buf[at, :])
            gate = gate_ref[part, at].astype(F32)
            sigma = 1.0 / (1.0 + jnp.exp(-gate))
            up = up_ref[part, at].astype(F32)
            dgate_ref[part, at] = (grad * up * sigma * (1.0 + gate * (1.0 - sigma))).astype(BF)
            dup_ref[part, at] = (grad * gate * sigma).astype(BF)
        copies[index][0].wait()
        for part in halves(g_ref.shape[0]):
            total = across(dgate_ref[part, at], gu_buf[0, :, at]) + across(
                dup_ref[part, at], gu_buf[1, :, at]
            )
            if index == 0:
                acc[part] = total
            else:
                part_ref[part] = (acc[part] + total).astype(BF)


def feed_back(t_index, own, other, w_gu, w_down, gate, up, waits=(), us=7):
    rows, width = 2 * own.shape[0], own.shape[1]
    units = w_down.shape[0]
    wide = shaped(rows, units)
    return on_core(
        feed_back_kernel,
        (t_index, own, other, gate, up, w_gu, w_down),
        [wide, wide, shaped(rows, width), shaped(rows, width)],
        scratch=weight_scratch(width, units) + [pltpu.VMEM((rows, width), F32)],
        smem=1, far=2, waits=waits, limit=15, us=us, name="feed_back",
    )


def feed_terms_kernel(n_ref, g_ref, u_ref, out_ref):
    rows = n_ref.shape[1] // 32
    for low in range(0, n_ref.shape[1], 256):
        left = n_ref[:, low : low + 256]
        for spot, right in enumerate((g_ref, u_ref)):
            term = down_rows(left, right[...]).astype(BF)
            for index in range(256 // rows):
                out_ref[low // rows + index, spot * rows : (spot + 1) * rows, :] = term[
                    index * rows : (index + 1) * rows
                ]


def feed_terms(normed, dgate, dup, waits=()):
    width, units = normed.shape[1], dgate.shape[1]
    return on_core(
        feed_terms_kernel, (normed, dgate, dup), [shaped(32, width // 16, units)],
        waits=waits, limit=8, us=BRIEF, name="feed_terms",
    )[0]


def sum_kernel(*refs):
    total = refs[0][...].astype(F32)
    for ref in refs[1:-1]:
        total += ref[...].astype(F32)
    refs[-1][...] = total.astype(BF)


def summed(values, waits=()):
    shape = values[0].shape
    piece = pl.BlockSpec((shape[0] // 4, *shape[1:]), lambda i: (i, 0, 0))

    def body(*refs):
        sum_kernel(*refs[: len(values)], refs[-1])

    return pl.pallas_call(
        body,
        grid=(4,),
        in_specs=[piece] * len(values) + [pl.BlockSpec(memory_space=pl.ANY)] * len(waits),
        out_specs=piece,
        out_shape=shaped(*shape),
        compiler_params=pltpu.CompilerParams(vmem_limit_bytes=8 * 2**20),
        cost_estimate=lasting(BRIEF),
        name="summed",
    )(*values, *waits)


def middle_back_kernel(x_ref, t_ref, g_ref, m_ref, p_ref, q_ref, gain_ref, w_ref,
                       dm_ref, gm_ref, d0, d1, d2, d3, sum_ref, do_ref):
    rows = g_ref.shape[0]
    for which, part in enumerate(halves(rows)):
        grad = p_ref[part].astype(F32) + q_ref[part].astype(F32)
        inner, scale, unit = norm_back(m_ref[part], grad, gain_ref[...])
        middle = g_ref[part].astype(F32) + inner

        @pl.when(t_ref[0] == which)
        def _():
            dm_ref[...] = middle
            sum_ref[...] = jnp.sum(grad * unit, axis=0, keepdims=True)

        gm_ref[part] = middle.astype(BF)
        do_ref[part] = across(gm_ref[part], w_ref[...]).astype(BF)
    for k, out in enumerate((d0, d1, d2, d3)):
        out[...] = do_ref[:, heads_at(x_ref, k)]


def norm_back(hidden, grad, gain):
    scale = rms_scale(hidden)
    unit = hidden * scale
    weighted = grad * gain
    inner = scale * (weighted - unit * jnp.mean(weighted * unit, axis=-1, keepdims=True))
    return inner, scale, unit


def middle_back(x_index, t_index, grad, middle, own, other, gain, w_out, waits=(), us=2.3):
    rows, width = grad.shape
    return on_core(
        middle_back_kernel,
        (x_index, t_index, grad, middle, own, other, gain, w_out),
        [shaped(rows // 2, width, dtype=F32), shaped(rows, width)]
        + [shaped(rows, PAIR)] * 4
        + [shaped(1, width, dtype=F32)],
        scratch=[pltpu.VMEM((rows, RING * PAIR), BF)],
        smem=2, waits=waits, limit=8, us=us, name="middle_back",
    )


def project_back_kernel(x_ref, t_ref, g0, g1, g2, g3, w_ref, keep_ref, send_ref, d_ref):
    for k, grad in enumerate((g0, g1, g2, g3)):
        for c in range(3):
            d_ref[c, :, heads_at(x_ref, k)] = grad[c]
    for which, part in enumerate(halves(d_ref.shape[1])):
        total = sum(across(d_ref[c, part], w_ref[c]) for c in range(3)).astype(BF)
        put_halves(t_ref, which, keep_ref, send_ref, total)


def project_back(x_index, t_index, grads, w_qkv, waits=(), us=2.2):
    rows, width = grads[0].shape[1], w_qkv.shape[1]
    return on_core(
        project_back_kernel,
        (x_index, t_index, *grads, w_qkv),
        [shaped(rows // 2, width)] * 2,
        scratch=[pltpu.VMEM((3, rows, RING * PAIR), BF)],
        smem=2, waits=waits, limit=5, us=us, name="project_back",
    )


def input_back_kernel(t_ref, h_ref, dm_ref, p_ref, q_ref, gain_ref, n_ref, dh_ref, low_ref, half_ref):
    grad = p_ref[...].astype(F32) + q_ref[...].astype(F32)
    total = dm_ref[...] + norm_back(h_ref[...].astype(F32), grad, gain_ref[...])[0]
    dh_ref[...] = total
    low_ref[...] = total.astype(BF)
    half_ref[...] = n_ref[own_half(t_ref, n_ref.shape[0]), :]


def input_back(t_index, hidden, grad_middle, own, other, gain, normed, us=1.5):
    return on_core(
        input_back_kernel, (t_index, hidden, grad_middle, own, other, gain, normed),
        [shaped(*hidden.shape, dtype=F32), shaped(*hidden.shape), shaped(*hidden.shape)],
        smem=1, limit=5, us=us, name="input_back",
    )


def close_kernel(m_ref, p_ref, q_ref, out_ref):
    out_ref[...] = (m_ref[...] + (p_ref[...].astype(F32) + q_ref[...].astype(F32))).astype(BF)


def close(middle, own, other, waits=()):
    return on_core(
        close_kernel, (middle, own, other), [shaped(*own.shape)], waits=waits, limit=4, us=0.7, name="close"
    )[0]


DOWN_ROWS, OUT_AT, QKV_AT = 44, 48, 64


def put_by_z(z_ref, keep_ref, send_ref, device, rows, lanes, value):
    spot = device // 8 * 4 + device % 4
    put_halves(z_ref, device // 4 % 2, keep_ref.at[spot, rows, lanes], send_ref.at[spot, rows, lanes], value)


def early_terms_kernel(z_ref, act_ref, go_ref, o_ref, gm_ref, keep_ref, send_ref, down):
    width = go_ref.shape[1]
    units = act_ref.shape[1]
    for low in range(0, units, 256):
        high = min(low + 256, units)
        down[low:high, :] = down_rows(act_ref[:, low:high], go_ref[...])
    blank = jnp.zeros((OUT_AT - DOWN_ROWS, width), F32)
    everywhere = slice(0, width)
    for at in range(32):
        block = jnp.concatenate([down[at * DOWN_ROWS : (at + 1) * DOWN_ROWS, :], blank])
        put_by_z(z_ref, keep_ref, send_ref, at, slice(0, OUT_AT), everywhere, block.astype(BF))
    rows = o_ref.shape[1] // 32
    for low in range(0, o_ref.shape[1], 256):
        term = down_rows(o_ref[:, low : low + 256], gm_ref[...]).astype(BF)
        for index in range(256 // rows):
            put_by_z(
                z_ref, keep_ref, send_ref, low // rows + index, slice(OUT_AT, QKV_AT), everywhere,
                term[index * rows : (index + 1) * rows],
            )


def early_terms(z_index, act, grad_out, attended, grad_branch):
    width = grad_out.shape[1]
    return on_core(
        early_terms_kernel,
        (z_index, act, grad_out, attended, grad_branch),
        [shaped(16, QKV_AT, width)] * 2,
        scratch=[pltpu.VMEM((act.shape[1], width), F32)],
        smem=1, limit=9, us=BRIEF, name="early_terms",
    )


def qkv_terms_kernel(x_ref, t_ref, z_ref, n_ref, near_ref, far_ref, g0, g1, g2, g3,
                     w_ref, gain_ref, two_ref, keep_ref, send_ref, acc):
    half = near_ref.shape[1]
    rows, wide = n_ref.shape[1] // 32, 3 * PAIR

    def joined(grad, at):
        return jnp.concatenate([grad[c, at, :] for c in range(3)], axis=1)

    acc[...] = down_rows(joined(g0, slice(None)), n_ref[...])
    for shift, grad in ((1, g1), (2, g2), (3, g3)):
        source = lax.rem(x_ref[0] + RING - shift, RING)
        acc[...] += down_rows(joined(grad, own_half(t_ref, 2 * half)), near_ref[source]) + down_rows(
            joined(grad, far_half(t_ref, 2 * half)), far_ref[source]
        )
    sums = []
    for low in range(0, acc.shape[1], 256):
        term = acc[:, low : low + 256].T.astype(BF)
        for index in range(256 // rows):
            at = low // rows + index
            block = term[index * rows : (index + 1) * rows]
            both = jnp.concatenate([block[: rows // 2], block[rows // 2 :]], axis=1)
            put_by_z(z_ref, keep_ref, send_ref, at, slice(0, rows // 2), slice(0, 2 * wide), both)
        total = jnp.zeros((1, 256), F32)
        for c in range(3):
            weight = w_ref[c, low : low + 256, heads_at(x_ref, 0)].astype(F32).T
            total += jnp.sum(weight * acc[c * PAIR : (c + 1) * PAIR, low : low + 256], axis=0, keepdims=True)
        sums.append(total / gain_ref[:, low : low + 256])
    sums += [two_ref[:, low : low + 256] for low in range(0, acc.shape[1], 256)]
    sums = jnp.concatenate(sums)
    high = sums.astype(BF)
    sums = jnp.concatenate([high, (sums - high.astype(F32)).astype(BF)])
    for out in (keep_ref, send_ref):
        out[:, :, 2 * wide :] = jnp.broadcast_to(sums[None], (out.shape[0], *sums.shape))


def qkv_terms(x_index, t_index, z_index, normed, near, far, grads, w_qkv, gain, gain_sum):
    width = normed.shape[1]
    return on_core(
        qkv_terms_kernel,
        (x_index, t_index, z_index, normed, near, far, *grads, w_qkv, gain, gain_sum),
        [shaped(16, width // 64, width)] * 2,
        scratch=[pltpu.VMEM((3 * PAIR, width), F32)],
        smem=3, limit=6, us=BRIEF, name="qkv_terms",
    )


def rest_kernel(a_ref, b_ref, c_ref, d_ref, out_ref):
    rows, lanes = c_ref.shape[1] // 2, 6 * PAIR
    out_ref[:, :QKV_AT, :] = (a_ref[...].astype(F32) + b_ref[...].astype(F32)).astype(BF)
    late = c_ref[...].astype(F32) + d_ref[...].astype(F32)
    out_ref[:, QKV_AT:, :lanes] = late[:, :, :lanes].astype(BF)
    sums = late[:, :rows, lanes:] + late[:, rows:, lanes:]
    high = sums.astype(BF)
    out_ref[:, QKV_AT : QKV_AT + rows, lanes:] = high
    out_ref[:, QKV_AT + rows :, lanes:] = (sums - high.astype(F32)).astype(BF)


def finish_kernel(rest_ref, down_ref, out_ref, qkv_ref, gain_ref):
    count, total, width = rest_ref.shape
    wide, rows = 3 * PAIR, total - QKV_AT

    def added(low, high):
        value = rest_ref[0, low:high, :].astype(F32)
        for source in range(1, count):
            value += rest_ref[source, low:high, :].astype(F32)
        return value

    down_ref[...] = added(0, OUT_AT)[:DOWN_ROWS]
    out_ref[...] = added(OUT_AT, QKV_AT)
    gains = jnp.zeros((rows, width - 2 * wide), F32)
    for x in range(RING):
        value = rest_ref[x, QKV_AT:, :].astype(F32)
        for source in range(x + RING, count, RING):
            value += rest_ref[source, QKV_AT:, :].astype(F32)
        for half in range(2):
            for c in range(3):
                low = half * wide + c * PAIR
                qkv_ref[c, half * rows : (half + 1) * rows, x * PAIR : (x + 1) * PAIR] = value[
                    :, low : low + PAIR
                ]
        gains += value[:, 2 * wide :]
    gains = gains[: rows // 2] + gains[rows // 2 :]
    for index in range(rows // 2):
        low = index % 4 * 256
        gain_ref[index // 4 : index // 4 + 1, low : low + 256] = gains[index : index + 1]


def finish(rest):
    width = rest.shape[2]
    rows = 2 * (rest.shape[1] - QKV_AT)
    return on_core(
        finish_kernel,
        (rest,),
        [
            shaped(DOWN_ROWS, width, dtype=F32),
            shaped(QKV_AT - OUT_AT, width, dtype=F32),
            shaped(3, rows, RING * PAIR, dtype=F32),
            shaped(2, width, dtype=F32),
        ],
        limit=4, us=BRIEF, name="finish",
    )


def rest_sum(early, early_got, late, late_got, waits=()):
    count, _, width = early.shape
    first = pl.BlockSpec((count // 4, QKV_AT, width), lambda i: (i, 0, 0))
    second = pl.BlockSpec((count // 4, *late.shape[1:]), lambda i: (i, 0, 0))
    total = QKV_AT + late.shape[1]

    def body(*refs):
        rest_kernel(*refs[:4], refs[-1])

    return pl.pallas_call(
        body,
        grid=(4,),
        in_specs=[first, first, second, second] + [pl.BlockSpec(memory_space=pl.ANY)] * len(waits),
        out_specs=pl.BlockSpec((count // 4, total, width), lambda i: (i, 0, 0)),
        out_shape=shaped(count, total, width),
        compiler_params=pltpu.CompilerParams(vmem_limit_bytes=8 * 2**20),
        cost_estimate=lasting(BRIEF),
        name="rest_sum",
    )(early, early_got, late, late_got, *waits)


def first_visible(ends_ref, places):
    start = jnp.zeros_like(places)
    for index in range(4):
        start = jnp.where(places >= ends_ref[index], ends_ref[index], start)
    return start


def attend_kernel(x_ref, ends_ref, m0, m1, m2, m3, o0, o1, o2, o3, lse_ref, out_t, keys, query_t,
                  value_t, totals):
    x = x_ref[0]
    lanes = lax.broadcasted_iota(jnp.int32, (BLOCK, PAIR), 1)
    for shift, message in enumerate((m0, m1, m2, m3)):
        source = lax.rem(x + RING - shift, RING)
        for part in range(4):
            at = pl.ds(pl.multiple_of(place_block(source, part) * BLOCK, BLOCK), BLOCK)
            inside = slice(part * BLOCK, (part + 1) * BLOCK)
            block = message[1, inside, :]
            keys[0, at, :] = jnp.where(lanes < HD, block, jnp.zeros_like(block))
            keys[1, at, :] = jnp.where(lanes < HD, jnp.zeros_like(block), block)
            query_t[:, at] = message[0, inside, :].T
            value_t[:, at] = message[2, inside, :].T

    places = lax.broadcasted_iota(jnp.int32, (1, LEN), 1)
    start = first_visible(ends_ref, places)
    out_t[...] = jnp.zeros_like(out_t)
    lse_ref[...] = jnp.full_like(lse_ref, NEGATIVE)
    totals[...] = jnp.zeros_like(totals)
    for low in range(0, LEN, KEYS):
        k_at, q_at = slice(low, low + KEYS), slice(low, LEN)
        key_places = low + lax.broadcasted_iota(jnp.int32, (KEYS, LEN - low), 0)
        visible = (key_places >= start[:, q_at]) & (key_places <= places[:, q_at])
        for head in range(2):
            row, part = slice(head, head + 1), slice(head * HD, (head + 1) * HD)
            scores = jnp.dot(keys[head, k_at, :], query_t[:, q_at], preferred_element_type=F32)
            scores = jnp.where(visible, scores, NEGATIVE)
            highest = lse_ref[row, q_at]
            higher = jnp.maximum(highest, jnp.max(scores, axis=0, keepdims=True))
            shrink = jnp.exp(highest - higher)
            weight = jnp.exp(scores - higher)
            lse_ref[row, q_at] = higher
            totals[row, q_at] = totals[row, q_at] * shrink + jnp.sum(weight, axis=0, keepdims=True)
            out_t[part, q_at] = out_t[part, q_at] * shrink + jnp.dot(
                value_t[part, k_at], weight.astype(BF), preferred_element_type=F32
            )
    for head in range(2):
        row, part = slice(head, head + 1), slice(head * HD, (head + 1) * HD)
        out_t[part, :] = out_t[part, :] / totals[row, :]
        lse_ref[row, :] = lse_ref[row, :] + jnp.log(totals[row, :])
    for shift, out in enumerate((o0, o1, o2, o3)):
        source = lax.rem(x + RING - shift, RING)
        for part in range(4):
            at = pl.ds(pl.multiple_of(place_block(source, part) * BLOCK, BLOCK), BLOCK)
            out[part * BLOCK : (part + 1) * BLOCK, :] = out_t[:, at].T.astype(BF)


def attend(x_index, ends, messages, waits=()):
    rows = messages[0].shape[1]
    return on_core(
        attend_kernel,
        (x_index, ends, *messages),
        [shaped(rows, PAIR)] * 4 + [shaped(2, LEN, dtype=F32), shaped(PAIR, LEN, dtype=F32)],
        scratch=[
            pltpu.VMEM((2, LEN, PAIR), BF),
            pltpu.VMEM((PAIR, LEN), BF),
            pltpu.VMEM((PAIR, LEN), BF),
            pltpu.VMEM((2, LEN), F32),
        ],
        smem=2, waits=waits, limit=12, us=11, name="attend",
    )


def attend_back_kernel(x_ref, ends_ref, mix_ref, m0, m1, m2, m3, d0, d1, d2, d3, lse_ref, out_t,
                       dv1_ref, cos_ref, sin_ref, g0, g1, g2, g3, dv_ref, keys, values, queries, grads,
                       key_t, query_t, grad_t, delta, grad_k, grad_v, grad_q_t):
    x = x_ref[0]
    lanes = lax.broadcasted_iota(jnp.int32, (BLOCK, PAIR), 1)
    for shift, (message, arrived) in enumerate(((m0, d0), (m1, d1), (m2, d2), (m3, d3))):
        source = lax.rem(x + RING - shift, RING)
        for part in range(4):
            at = pl.ds(pl.multiple_of(place_block(source, part) * BLOCK, BLOCK), BLOCK)
            inside = slice(part * BLOCK, (part + 1) * BLOCK)
            query, key, value = message[0, inside, :], message[1, inside, :], message[2, inside, :]
            grad = arrived[inside, :]
            zero = jnp.zeros_like(query)
            for both, block in ((keys, key), (values, value), (queries, query), (grads, grad)):
                both[0, at, :] = jnp.where(lanes < HD, block, zero)
                both[1, at, :] = jnp.where(lanes < HD, zero, block)
            key_t[:, at] = key.T
            query_t[:, at] = query.T
            turned_grad = grad.T
            grad_t[:, at] = turned_grad
            product = out_t[:, at] * turned_grad.astype(F32)
            delta[0:1, at] = jnp.sum(product[:HD], axis=0, keepdims=True)
            delta[1:2, at] = jnp.sum(product[HD:], axis=0, keepdims=True)
    grad_q_t[...] = jnp.zeros_like(grad_q_t)
    places = lax.broadcasted_iota(jnp.int32, (1, LEN), 1)
    start = first_visible(ends_ref, places)
    for low in range(0, LEN, BACK_KEYS):
        k_at, q_at = slice(low, low + BACK_KEYS), slice(low, LEN)
        key_places = low + lax.broadcasted_iota(jnp.int32, (BACK_KEYS, LEN - low), 0)
        visible = (key_places >= start[:, q_at]) & (key_places <= places[:, q_at])
        sum_k = sum_v = jnp.zeros((BACK_KEYS, PAIR), F32)
        for head in range(2):
            row, part = slice(head, head + 1), slice(head * HD, (head + 1) * HD)
            scores = jnp.dot(keys[head, k_at, :], query_t[:, q_at], preferred_element_type=F32)
            weight = jnp.exp(jnp.where(visible, scores, NEGATIVE) - lse_ref[row, q_at])
            grad_w = jnp.dot(values[head, k_at, :], grad_t[:, q_at], preferred_element_type=F32)
            grad_s = (weight * (grad_w - delta[row, q_at])).astype(BF)
            sum_v += jnp.dot(weight.astype(BF), grads[head, q_at, :], preferred_element_type=F32)
            sum_k += jnp.dot(grad_s, queries[head, q_at, :], preferred_element_type=F32)
            grad_q_t[part, q_at] += jnp.dot(key_t[part, k_at], grad_s, preferred_element_type=F32)
        grad_k[k_at, :] = sum_k
        grad_v[k_at, :] = sum_v
    for shift, out in enumerate((g0, g1, g2, g3)):
        source = lax.rem(x + RING - shift, RING)
        for part in range(4):
            at = pl.ds(pl.multiple_of(place_block(source, part) * BLOCK, BLOCK), BLOCK)
            inside = slice(part * BLOCK, (part + 1) * BLOCK)
            cosine, sine = cos_ref[at, :], sin_ref[at, :]
            grad_q = grad_q_t[:, at].T * HD ** (-0.5)
            out[0, inside, :] = turned(grad_q, cosine, sine, -1.0).astype(BF)
            out[1, inside, :] = turned(grad_k[at, :], cosine, sine, -1.0).astype(BF)
            grad_value = mix_ref[0] * grad_v[at, :] + mix_ref[1] * dv1_ref[shift, inside, :].astype(F32)
            out[2, inside, :] = grad_value.astype(BF)
            dv_ref[shift, inside, :] = grad_value.astype(BF)


def attend_back(x_index, ends, mix, messages, arrived, lse, out_t, dv1, cosine, sine, waits=(), us=18):
    rows = messages[0].shape[1]
    return on_core(
        attend_back_kernel,
        (x_index, ends, mix, *messages, *arrived, lse, out_t, dv1, cosine, sine),
        [shaped(3, rows, PAIR)] * 4 + [shaped(RING, rows, PAIR)],
        scratch=[pltpu.VMEM((2, LEN, PAIR), BF)] * 4
        + [pltpu.VMEM((PAIR, LEN), BF)] * 3
        + [
            pltpu.VMEM((2, LEN), F32),
            pltpu.VMEM((LEN, PAIR), F32),
            pltpu.VMEM((LEN, PAIR), F32),
            pltpu.VMEM((PAIR, LEN), F32),
        ],
        smem=3, waits=waits, limit=17, us=us, name="attend_back",
    )


def out_and_back(values, sign):
    return [values[0]] + [moved(values[shift], "x", sign * shift) for shift in range(1, RING)]


def groups(kinds):
    found = {}
    for index in range(32):
        place = {"y": index // 8, "z": index // 4 % 2, "x": index % 4}
        found.setdefault(tuple(place[k] for k in "yzx" if k not in kinds), []).append(index)
    return list(found.values())


def all_to_all(value, kinds):
    return lax.all_to_all(value, "dp", 0, 0, axis_index_groups=groups(kinds))


def per_device(tokens, cotangent, doc_lengths, gains, wqkv, wo, wgu, wd):
    first = lax.axis_index("section") == 0
    tensor = lax.axis_index("tensor")
    position = lax.axis_index("dp")
    y, z, x = position // 8, position // 4 % 2, position % 4
    x_index, z_index, t_index = [v.astype(jnp.int32).reshape(1) for v in (x, z, tensor)]
    width = tokens.shape[2]

    def in_order(keep, got):
        got = got.astype(keep.dtype)
        return jnp.where(z == 0, jnp.stack([keep, got]), jnp.stack([got, keep]))

    def regrouped(pair):
        keep = lax.dynamic_index_in_dim(pair, z, 0, keepdims=False)
        send = lax.dynamic_index_in_dim(pair, 1 - z, 0, keepdims=False)
        return in_order(keep, moved(send.astype(BF), "z", 1))

    lens = lax.dynamic_slice(doc_lengths, (z, y, 0), (1, 1, 4))
    ends = jnp.cumsum(lens.reshape(4), dtype=jnp.int32)
    cosine, sine = rotary_tables()
    w_qkv = jnp.transpose(wqkv[0], (1, 0, 2))
    w_out, w_down = wo[0], wd[0]
    gain_one, gain_two = gains[0, 0:1], gains[0, 1:2]
    mix = jnp.where(first, jnp.array([1.0, 0.0], F32), jnp.array([0.5, 0.5], F32))
    mix_back = jnp.where(first, jnp.array([1.0, 1.0], F32), jnp.array([0.5, 0.0], F32))

    def handed(value, pairs):
        return lax.ppermute(value, "section", pairs)

    def first_half(own, value_first):
        *messages, normed, value, hidden, zero = project(
            x_index, t_index, mix, own, swapped(own), gain_one, w_qkv, value_first, cosine, sine
        )
        return out_and_back(messages, 1), normed, value, hidden, zero

    def second_half(hidden, outs, value, save, waits=()):
        attended, part, value = branch(x_index, out_and_back(outs, -1), w_out, value, waits=waits)
        mine, keep, send, normed_two, *more = feed(
            t_index, hidden, part, swapped(part), gain_two, w_gu, w_down, save
        )
        return mine, keep, swapped(send), value, (attended, normed_two, *more)

    own_rows = regrouped(tokens).reshape(2 * BLOCK, width)
    no_value = jnp.zeros((RING, 4 * BLOCK, PAIR), BF)

    messages, _, value, hidden, zero = first_half(own_rows, no_value)
    w_gu = jnp.transpose(wgu[0] + zero[0, 0], (1, 0, 2))
    *outs, _, _ = attend(x_index, ends, messages, waits=(seen(w_gu),))
    cot_keep, cot_send = pick(z_index, cotangent, waits=(seen(outs[0]),))
    top_grad = in_order(cot_keep, moved(cot_send, "z", 1)).reshape(2 * BLOCK, width)
    mine, keep, got, value, _ = second_half(hidden, outs, value, False)
    v_in = handed(value, [(0, 1)])
    result = close(mine, keep, got, waits=(seen(v_in),))
    own = jnp.where(first, own_rows, handed(result, [(0, 1)]))

    messages, normed, value, hidden, _ = first_half(own, v_in)
    *outs, lse, out_t = attend(x_index, ends, messages)
    mine, keep, got, _, saved = second_half(hidden, outs, value, True, waits=(seen(top_grad),))
    attended, normed_two, middle, gate, up, act = saved
    def first_back(own_grad, us=7):
        return feed_back(t_index, own_grad, swapped(own_grad), w_gu, w_down, gate, up, us=us)

    def second_back(grad, part, waits=(), us=2.3):
        grad_middle, grad_branch, *sends, gain_sum = middle_back(
            x_index, t_index, grad, middle, part, swapped(part), gain_two, w_out, waits=waits, us=us
        )
        return grad_middle, grad_branch, out_and_back(sends, 1), gain_sum

    def third_back(arrived, grad_value, waits=(), us=20):
        return attend_back(
            x_index, ends, mix_back, messages, arrived, lse, out_t, grad_value, cosine, sine, waits=waits, us=us
        )

    def fourth_back(grads, grad_middle, waits=(), us=2):
        keep, send = project_back(
            x_index, t_index, out_and_back(grads, -1), w_qkv, waits=waits, us=us
        )
        return *input_back(
            t_index, own, grad_middle, keep, swapped(send), gain_one, normed, us=us
        ), keep

    _, _, part, grad = first_back(top_grad)
    grad_middle, _, arrived, _ = second_back(grad, part)
    *grads, grad_value = third_back(arrived, no_value)
    result = close(mine, keep, got, waits=(seen(grad_value),))
    acts = regrouped(result.reshape(2, BLOCK, width))[None]
    gv_in = handed(grad_value, [(1, 0)])
    _, grad_hidden, half, _ = fourth_back(
        grads, grad_middle, waits=(seen(gv_in), seen(acts[0, 0]))
    )
    near = lax.all_gather(half, "dp", axis_index_groups=groups("x"))
    own_grad = jnp.where(first, handed(grad_hidden, [(1, 0)]), top_grad)

    dgate, dup, part, grad_out = first_back(own_grad, us=BRIEF)
    grad_middle, grad_branch, arrived, gain_sum = second_back(grad_out, part, us=BRIEF)
    feed_term = feed_terms(normed_two, dgate, dup, waits=(seen(grad_branch),))
    feed_sum = lax.psum_scatter(
        feed_term, "dp", scatter_dimension=0, axis_index_groups=groups("y"), tiled=True
    )
    early, early_send = early_terms(z_index, act, grad_out, attended, grad_branch)
    early_got = moved(early_send, "z", 1)
    far = swapped(near)
    *grads, _ = third_back(arrived, gv_in, waits=(seen(far), seen(early), seen(feed_term)), us=BRIEF)
    late, late_send = qkv_terms(
        x_index, t_index, z_index, normed, near, far, grads, w_qkv, gain_one, gain_sum
    )
    late_got = moved(late_send, "z", 1)
    grad_hidden, _, _, last = fourth_back(grads, grad_middle, waits=(seen(late),), us=BRIEF)
    rest = rest_sum(early, early_got, late, late_got, waits=(seen(last),))
    dins = regrouped(grad_hidden.reshape(2, BLOCK, width))[None]
    feed_sum = summed([feed_sum], waits=(seen(rest), seen(dins[0, 0])))
    feed_share = jnp.sum(all_to_all(feed_sum, "zx").astype(F32), axis=0)
    feed_share = feed_share.reshape(2, width // 32, -1)
    down_share, out_share, qkv_share, gain_total = finish(all_to_all(rest, "yx"))
    return (
        acts,
        dins,
        jnp.transpose(qkv_share, (1, 0, 2))[None],
        out_share[None],
        jnp.transpose(feed_share, (1, 0, 2))[None],
        down_share[None],
        (gain_total + swapped(gain_total))[None],
    )


def solution(mesh):
    placed = (
        P(None, ("tensor", "dp"), None),
        P(None, ("tensor", "dp"), None),
        P(),
        P("section", None, None),
        P("section", None, None, "tensor"),
        P("section", "tensor", None),
        P("section", None, None, "tensor"),
        P("section", "tensor", None),
    )
    return jax.shard_map(
        per_device,
        mesh=mesh,
        in_specs=placed,
        out_specs=(
            P("section", None, ("tensor", "dp"), None),
            P("section", None, ("tensor", "dp"), None),
            P("section", "dp", None, "tensor"),
            P("section", ("tensor", "dp"), None),
            P("section", "dp", None, "tensor"),
            P("section", ("tensor", "dp"), None),
            P("section", None, None),
        ),
        check_vma=False,
    )
```

```python
import jax
import jax.numpy as jnp
import numpy as np
from jax import lax
from jax.experimental import pallas as pl
from jax.experimental.pallas import tpu as pltpu
from jax.sharding import PartitionSpec as P

HD = 64
LEN = 2048
RING = 4
BLOCK = 128
PAIR = 2 * HD
EPSILON = 1e-06
BRIEF = 0.001
NEGATIVE = -1e30
KEYS = 512
BACK_KEYS = 256
BF = jnp.bfloat16
F32 = jnp.float32


def along(kind, shift):
    pairs = []
    for index in range(32):
        y, z, x = index // 8, index // 4 % 2, index % 4
        if kind == "x":
            x = (x + shift) % 4
        elif kind == "y":
            y = (y + shift) % 4
        else:
            z = (z + shift) % 2
        pairs.append((index, y * 8 + z * 4 + x))
    return pairs


def moved(value, kind, shift):
    return lax.ppermute(value, "dp", along(kind, shift))


def swapped(value):
    return lax.ppermute(value, "tensor", [(0, 1), (1, 0)])


def rms_scale(hidden):
    return lax.rsqrt(jnp.mean(hidden * hidden, axis=-1, keepdims=True) + EPSILON)


def rotary_tables():
    half = HD // 2
    freqs = np.float32(10000.0) ** (-np.arange(half, dtype=np.float32) / np.float32(half))
    angles = np.arange(LEN, dtype=np.float32)[:, None] * freqs[None, :]
    return [jnp.asarray(np.tile(f(angles).astype(np.float32), (1, 4))) for f in (np.cos, np.sin)]


def low_lanes(shape):
    return lax.broadcasted_iota(jnp.int32, shape, 1) % HD < HD // 2


def turned(u, cosine, sine, sign):
    ahead = pltpu.roll(u, PAIR - HD // 2, 1)
    behind = pltpu.roll(u, HD // 2, 1)
    cross = jnp.where(low_lanes(u.shape), -sign * ahead, sign * behind)
    return u * cosine + cross * sine


def place_block(source, part):
    return (source, 4 + source, 15 - source, 11 - source)[part]


def lasting(us):
    return pl.CostEstimate(flops=int(us * 1.1e9), bytes_accessed=int(us * 3.6e6), transcendentals=0)


def on_core(kernel, ins, outs, *, scratch=(), smem=0, far=0, waits=(), limit=24, us, name):
    spots = [pl.BlockSpec(memory_space=pltpu.SMEM)] * smem
    spots += [pl.BlockSpec(memory_space=pltpu.VMEM)] * (len(ins) - smem - far)
    spots += [pl.BlockSpec(memory_space=pltpu.HBM)] * far
    spots += [pl.BlockSpec(memory_space=pl.ANY)] * len(waits)
    taken, given = len(ins), len(outs)

    def body(*refs):
        kernel(*refs[:taken], *refs[taken + len(waits) :])

    return pl.pallas_call(
        body,
        in_specs=spots,
        out_specs=[pl.BlockSpec(memory_space=pltpu.VMEM)] * given,
        out_shape=list(outs),
        scratch_shapes=list(scratch),
        compiler_params=pltpu.CompilerParams(vmem_limit_bytes=limit * 2**20),
        cost_estimate=lasting(us),
        name=name,
    )(*ins, *waits)


def seen(value):
    return value[(0,) * (value.ndim - 2)][:8, :PAIR]


def shaped(*shape, dtype=BF):
    return jax.ShapeDtypeStruct(shape, dtype)


def heads_at(x_ref, shift):
    return pl.ds(pl.multiple_of(lax.rem(x_ref[0] + shift, RING) * PAIR, PAIR), PAIR)


def halves(rows):
    return [slice(0, rows // 2), slice(rows // 2, rows)]


def across(left, right):
    return lax.dot_general(left, right, (((1,), (1,)), ((), ())), preferred_element_type=F32)


def down_rows(left, right):
    return lax.dot_general(left, right, (((0,), (0,)), ((), ())), preferred_element_type=F32)


def own_half(t_ref, rows):
    return pl.ds(pl.multiple_of(t_ref[0] * (rows // 2), rows // 2), rows // 2)


def far_half(t_ref, rows):
    return pl.ds(pl.multiple_of((1 - t_ref[0]) * (rows // 2), rows // 2), rows // 2)


def project_kernel(x_ref, t_ref, mix_ref, own_ref, other_ref, gain_ref, w_ref, v1_ref, cos_ref, sin_ref,
                   m0, m1, m2, m3, n_ref, v_ref, h_ref, zero_ref):
    zero_ref[...] = jnp.zeros_like(zero_ref)
    rows = h_ref.shape[0]
    h_ref[own_half(t_ref, rows), :] = own_ref[...]
    h_ref[far_half(t_ref, rows), :] = other_ref[...]
    for part in halves(rows):
        h = h_ref[part].astype(F32)
        n_ref[part] = (h * rms_scale(h) * gain_ref[...]).astype(BF)
    outs = (m0, m1, m2, m3)
    for pair in ((0, 1), (2, 3)):
        weight = jnp.concatenate(
            [w_ref[c, :, heads_at(x_ref, k)] for k in pair for c in range(3)], axis=1
        )
        for part in halves(rows):
            both = jnp.dot(n_ref[part], weight, preferred_element_type=F32)
            cosine, sine = cos_ref[part], sin_ref[part]
            for index, k in enumerate(pair):
                query, key, value = [
                    both[:, (3 * index + c) * PAIR : (3 * index + c + 1) * PAIR] for c in range(3)
                ]
                outs[k][0, part] = (turned(query, cosine, sine, 1.0) * HD ** (-0.5)).astype(BF)
                outs[k][1, part] = turned(key, cosine, sine, 1.0).astype(BF)
                value = mix_ref[0] * value + mix_ref[1] * v1_ref[k, part].astype(F32)
                outs[k][2, part] = value.astype(BF)
                v_ref[k, part] = value.astype(BF)


def project(x_index, t_index, mix, own, other, gain, w_qkv, value_first, cosine, sine, waits=()):
    rows, width = 2 * own.shape[0], own.shape[1]
    return on_core(
        project_kernel,
        (x_index, t_index, mix, own, other, gain, w_qkv, value_first, cosine, sine),
        [shaped(3, rows, PAIR)] * 4
        + [shaped(rows, width), shaped(RING, rows, PAIR), shaped(rows, width), shaped(8, PAIR)],
        smem=3, waits=waits, limit=5, us=3, name="project",
    )


def pick_kernel(z_ref, pair_ref, keep_ref, send_ref):
    keep_ref[...] = pair_ref[z_ref[0]]
    send_ref[...] = pair_ref[1 - z_ref[0]]


def pick(z_index, pair, waits=()):
    return on_core(
        pick_kernel, (z_index, pair), [shaped(*pair.shape[1:])] * 2, smem=1, waits=waits, limit=4, us=0.6, name="pick"
    )


def branch_kernel(x_ref, o0, o1, o2, o3, w_ref, v_ref, o_ref, part_ref, copy_ref):
    for k, arrived in enumerate((o0, o1, o2, o3)):
        o_ref[:, heads_at(x_ref, k)] = arrived[...]
    for part in halves(o_ref.shape[0]):
        part_ref[part] = jnp.dot(o_ref[part], w_ref[...], preferred_element_type=F32).astype(BF)
    copy_ref[...] = v_ref[...]


def branch(x_index, arrived, w_out, value, waits=()):
    rows, width = arrived[0].shape[0], w_out.shape[1]
    return on_core(
        branch_kernel,
        (x_index, *arrived, w_out, value),
        [shaped(rows, RING * PAIR), shaped(rows, width), jax.ShapeDtypeStruct(value.shape, BF)],
        smem=1, waits=waits, limit=4, us=1, name="branch",
    )


def put_halves(t_ref, which, keep_ref, send_ref, value):
    @pl.when(t_ref[0] == which)
    def _():
        keep_ref[...] = value

    @pl.when(t_ref[0] != which)
    def _():
        send_ref[...] = value


def pieces(units):
    cut = (units // PAIR + 1) // 2 * PAIR
    return [(0, cut), (cut, units)]


def weight_copies(wgu_ref, wd_ref, gu_buf, d_buf, sems):
    copies = []
    for index, (low, high) in enumerate(pieces(wd_ref.shape[0])):
        at = pl.ds(low, high - low)
        copies.append(
            [
                pltpu.make_async_copy(wgu_ref.at[:, :, at], gu_buf.at[:, :, at], sems.at[index, 0]),
                pltpu.make_async_copy(wd_ref.at[at, :], d_buf.at[at, :], sems.at[index, 1]),
            ]
        )
    return copies


def weight_scratch(width, units):
    return [
        pltpu.VMEM((2, width, units), BF),
        pltpu.VMEM((units, width), BF),
        pltpu.SemaphoreType.DMA((2, 2)),
    ]


def feed_kernel(t_ref, h_ref, p_ref, q_ref, gain_ref, wgu_ref, wd_ref,
                mine_ref, keep_ref, send_ref, n_ref, *rest):
    *saved, gu_buf, d_buf, sems, acc = rest
    copies = weight_copies(wgu_ref, wd_ref, gu_buf, d_buf, sems)
    for pair in copies:
        for copy in pair:
            copy.start()
    rows = halves(h_ref.shape[0])
    for which, part in enumerate(rows):
        middle = h_ref[part].astype(F32) + (p_ref[part].astype(F32) + q_ref[part].astype(F32))
        if saved:
            saved[0][part] = middle
        n_ref[part] = (middle * rms_scale(middle) * gain_ref[...]).astype(BF)

        @pl.when(t_ref[0] == which)
        def _():
            mine_ref[...] = middle

    for index, (low, high) in enumerate(pieces(d_buf.shape[0])):
        at = slice(low, high)
        for copy in copies[index]:
            copy.wait()
        for which, part in enumerate(rows):
            gate = jnp.dot(n_ref[part], gu_buf[0, :, at], preferred_element_type=F32)
            up = jnp.dot(n_ref[part], gu_buf[1, :, at], preferred_element_type=F32)
            act = (gate / (1.0 + jnp.exp(-gate)) * up).astype(BF)
            if saved:
                saved[1][part, at] = gate.astype(BF)
                saved[2][part, at] = up.astype(BF)
                saved[3][part, at] = act
            total = jnp.dot(act, d_buf[at, :], preferred_element_type=F32)
            if index == 0:
                acc[part] = total
            else:
                put_halves(t_ref, which, keep_ref, send_ref, (acc[part] + total).astype(BF))


def feed(t_index, hidden, own, other, gain, w_gu, w_down, save, waits=()):
    rows, width = hidden.shape
    units = w_down.shape[0]
    wide, half = shaped(rows, units), shaped(rows // 2, width)
    outs = [shaped(rows // 2, width, dtype=F32), half, half, shaped(rows, width)]
    if save:
        outs += [shaped(rows, width, dtype=F32), wide, wide, wide]
    return on_core(
        feed_kernel,
        (t_index, hidden, own, other, gain, w_gu, w_down),
        outs,
        scratch=weight_scratch(width, units) + [pltpu.VMEM((rows, width), F32)],
        smem=1, far=2, waits=waits, limit=14, us=7, name="feed",
    )


def feed_back_kernel(t_ref, own_ref, other_ref, gate_ref, up_ref, wgu_ref, wd_ref,
                     dgate_ref, dup_ref, part_ref, g_ref, gu_buf, d_buf, sems, acc):
    copies = weight_copies(wgu_ref, wd_ref, gu_buf, d_buf, sems)
    for which in (1, 0):
        for pair in copies:
            pair[which].start()
    g_ref[own_half(t_ref, g_ref.shape[0]), :] = own_ref[...]
    g_ref[far_half(t_ref, g_ref.shape[0]), :] = other_ref[...]
    for index, (low, high) in enumerate(pieces(d_buf.shape[0])):
        at = slice(low, high)
        copies[index][1].wait()
        for part in halves(g_ref.shape[0]):
            grad = across(g_ref[part], d_buf[at, :])
            gate = gate_ref[part, at].astype(F32)
            sigma = 1.0 / (1.0 + jnp.exp(-gate))
            up = up_ref[part, at].astype(F32)
            dgate_ref[part, at] = (grad * up * sigma * (1.0 + gate * (1.0 - sigma))).astype(BF)
            dup_ref[part, at] = (grad * gate * sigma).astype(BF)
        copies[index][0].wait()
        for part in halves(g_ref.shape[0]):
            total = across(dgate_ref[part, at], gu_buf[0, :, at]) + across(
                dup_ref[part, at], gu_buf[1, :, at]
            )
            if index == 0:
                acc[part] = total
            else:
                part_ref[part] = (acc[part] + total).astype(BF)


def feed_back(t_index, own, other, w_gu, w_down, gate, up, waits=(), us=7):
    rows, width = 2 * own.shape[0], own.shape[1]
    units = w_down.shape[0]
    wide = shaped(rows, units)
    return on_core(
        feed_back_kernel,
        (t_index, own, other, gate, up, w_gu, w_down),
        [wide, wide, shaped(rows, width), shaped(rows, width)],
        scratch=weight_scratch(width, units) + [pltpu.VMEM((rows, width), F32)],
        smem=1, far=2, waits=waits, limit=15, us=us, name="feed_back",
    )


def feed_terms_kernel(n_ref, g_ref, u_ref, out_ref):
    rows = n_ref.shape[1] // 32
    for low in range(0, n_ref.shape[1], 256):
        left = n_ref[:, low : low + 256]
        for spot, right in enumerate((g_ref, u_ref)):
            term = down_rows(left, right[...]).astype(BF)
            for index in range(256 // rows):
                out_ref[low // rows + index, spot * rows : (spot + 1) * rows, :] = term[
                    index * rows : (index + 1) * rows
                ]


def feed_terms(normed, dgate, dup, waits=()):
    width, units = normed.shape[1], dgate.shape[1]
    return on_core(
        feed_terms_kernel, (normed, dgate, dup), [shaped(32, width // 16, units)],
        waits=waits, limit=8, us=BRIEF, name="feed_terms",
    )[0]


def sum_kernel(*refs):
    total = refs[0][...].astype(F32)
    for ref in refs[1:-1]:
        total += ref[...].astype(F32)
    refs[-1][...] = total.astype(BF)


def summed(values, waits=()):
    shape = values[0].shape
    piece = pl.BlockSpec((shape[0] // 4, *shape[1:]), lambda i: (i, 0, 0))

    def body(*refs):
        sum_kernel(*refs[: len(values)], refs[-1])

    return pl.pallas_call(
        body,
        grid=(4,),
        in_specs=[piece] * len(values) + [pl.BlockSpec(memory_space=pl.ANY)] * len(waits),
        out_specs=piece,
        out_shape=shaped(*shape),
        compiler_params=pltpu.CompilerParams(vmem_limit_bytes=8 * 2**20),
        cost_estimate=lasting(BRIEF),
        name="summed",
    )(*values, *waits)


def middle_back_kernel(x_ref, t_ref, g_ref, m_ref, p_ref, q_ref, gain_ref, w_ref,
                       dm_ref, gm_ref, d0, d1, d2, d3, sum_ref, do_ref):
    rows = g_ref.shape[0]
    for which, part in enumerate(halves(rows)):
        grad = p_ref[part].astype(F32) + q_ref[part].astype(F32)
        inner, scale, unit = norm_back(m_ref[part], grad, gain_ref[...])
        middle = g_ref[part].astype(F32) + inner

        @pl.when(t_ref[0] == which)
        def _():
            dm_ref[...] = middle
            sum_ref[...] = jnp.sum(grad * unit, axis=0, keepdims=True)

        gm_ref[part] = middle.astype(BF)
        do_ref[part] = across(gm_ref[part], w_ref[...]).astype(BF)
    for k, out in enumerate((d0, d1, d2, d3)):
        out[...] = do_ref[:, heads_at(x_ref, k)]


def norm_back(hidden, grad, gain):
    scale = rms_scale(hidden)
    unit = hidden * scale
    weighted = grad * gain
    inner = scale * (weighted - unit * jnp.mean(weighted * unit, axis=-1, keepdims=True))
    return inner, scale, unit


def middle_back(x_index, t_index, grad, middle, own, other, gain, w_out, waits=(), us=2.3):
    rows, width = grad.shape
    return on_core(
        middle_back_kernel,
        (x_index, t_index, grad, middle, own, other, gain, w_out),
        [shaped(rows // 2, width, dtype=F32), shaped(rows, width)]
        + [shaped(rows, PAIR)] * 4
        + [shaped(1, width, dtype=F32)],
        scratch=[pltpu.VMEM((rows, RING * PAIR), BF)],
        smem=2, waits=waits, limit=8, us=us, name="middle_back",
    )


def project_back_kernel(x_ref, t_ref, g0, g1, g2, g3, w_ref, keep_ref, send_ref, d_ref):
    for k, grad in enumerate((g0, g1, g2, g3)):
        for c in range(3):
            d_ref[c, :, heads_at(x_ref, k)] = grad[c]
    for which, part in enumerate(halves(d_ref.shape[1])):
        total = sum(across(d_ref[c, part], w_ref[c]) for c in range(3)).astype(BF)
        put_halves(t_ref, which, keep_ref, send_ref, total)


def project_back(x_index, t_index, grads, w_qkv, waits=(), us=2.2):
    rows, width = grads[0].shape[1], w_qkv.shape[1]
    return on_core(
        project_back_kernel,
        (x_index, t_index, *grads, w_qkv),
        [shaped(rows // 2, width)] * 2,
        scratch=[pltpu.VMEM((3, rows, RING * PAIR), BF)],
        smem=2, waits=waits, limit=5, us=us, name="project_back",
    )


def input_back_kernel(t_ref, h_ref, dm_ref, p_ref, q_ref, gain_ref, n_ref, dh_ref, low_ref, half_ref):
    grad = p_ref[...].astype(F32) + q_ref[...].astype(F32)
    total = dm_ref[...] + norm_back(h_ref[...].astype(F32), grad, gain_ref[...])[0]
    dh_ref[...] = total
    low_ref[...] = total.astype(BF)
    half_ref[...] = n_ref[own_half(t_ref, n_ref.shape[0]), :]


def input_back(t_index, hidden, grad_middle, own, other, gain, normed, us=1.5):
    return on_core(
        input_back_kernel, (t_index, hidden, grad_middle, own, other, gain, normed),
        [shaped(*hidden.shape, dtype=F32), shaped(*hidden.shape), shaped(*hidden.shape)],
        smem=1, limit=5, us=us, name="input_back",
    )


def close_kernel(m_ref, p_ref, q_ref, out_ref):
    out_ref[...] = (m_ref[...] + (p_ref[...].astype(F32) + q_ref[...].astype(F32))).astype(BF)


def close(middle, own, other, waits=()):
    return on_core(
        close_kernel, (middle, own, other), [shaped(*own.shape)], waits=waits, limit=4, us=0.7, name="close"
    )[0]


DOWN_ROWS, OUT_AT, QKV_AT = 44, 48, 64


def put_by_z(z_ref, keep_ref, send_ref, device, rows, lanes, value):
    spot = device // 8 * 4 + device % 4
    put_halves(z_ref, device // 4 % 2, keep_ref.at[spot, rows, lanes], send_ref.at[spot, rows, lanes], value)


def early_terms_kernel(z_ref, act_ref, go_ref, o_ref, gm_ref, keep_ref, send_ref, down):
    width = go_ref.shape[1]
    units = act_ref.shape[1]
    for low in range(0, units, 256):
        high = min(low + 256, units)
        down[low:high, :] = down_rows(act_ref[:, low:high], go_ref[...])
    blank = jnp.zeros((OUT_AT - DOWN_ROWS, width), F32)
    everywhere = slice(0, width)
    for at in range(32):
        block = jnp.concatenate([down[at * DOWN_ROWS : (at + 1) * DOWN_ROWS, :], blank])
        put_by_z(z_ref, keep_ref, send_ref, at, slice(0, OUT_AT), everywhere, block.astype(BF))
    rows = o_ref.shape[1] // 32
    for low in range(0, o_ref.shape[1], 256):
        term = down_rows(o_ref[:, low : low + 256], gm_ref[...]).astype(BF)
        for index in range(256 // rows):
            put_by_z(
                z_ref, keep_ref, send_ref, low // rows + index, slice(OUT_AT, QKV_AT), everywhere,
                term[index * rows : (index + 1) * rows],
            )


def early_terms(z_index, act, grad_out, attended, grad_branch):
    width = grad_out.shape[1]
    return on_core(
        early_terms_kernel,
        (z_index, act, grad_out, attended, grad_branch),
        [shaped(16, QKV_AT, width)] * 2,
        scratch=[pltpu.VMEM((act.shape[1], width), F32)],
        smem=1, limit=9, us=BRIEF, name="early_terms",
    )


def qkv_terms_kernel(x_ref, t_ref, z_ref, n_ref, near_ref, far_ref, g0, g1, g2, g3,
                     w_ref, gain_ref, two_ref, keep_ref, send_ref, acc):
    half = near_ref.shape[1]
    rows, wide = n_ref.shape[1] // 32, 3 * PAIR

    def joined(grad, at):
        return jnp.concatenate([grad[c, at, :] for c in range(3)], axis=1)

    acc[...] = down_rows(joined(g0, slice(None)), n_ref[...])
    for shift, grad in ((1, g1), (2, g2), (3, g3)):
        source = lax.rem(x_ref[0] + RING - shift, RING)
        acc[...] += down_rows(joined(grad, own_half(t_ref, 2 * half)), near_ref[source]) + down_rows(
            joined(grad, far_half(t_ref, 2 * half)), far_ref[source]
        )
    sums = []
    for low in range(0, acc.shape[1], 256):
        term = acc[:, low : low + 256].T.astype(BF)
        for index in range(256 // rows):
            at = low // rows + index
            block = term[index * rows : (index + 1) * rows]
            both = jnp.concatenate([block[: rows // 2], block[rows // 2 :]], axis=1)
            put_by_z(z_ref, keep_ref, send_ref, at, slice(0, rows // 2), slice(0, 2 * wide), both)
        total = jnp.zeros((1, 256), F32)
        for c in range(3):
            weight = w_ref[c, low : low + 256, heads_at(x_ref, 0)].astype(F32).T
            total += jnp.sum(weight * acc[c * PAIR : (c + 1) * PAIR, low : low + 256], axis=0, keepdims=True)
        sums.append(total / gain_ref[:, low : low + 256])
    sums += [two_ref[:, low : low + 256] for low in range(0, acc.shape[1], 256)]
    sums = jnp.concatenate(sums)
    high = sums.astype(BF)
    sums = jnp.concatenate([high, (sums - high.astype(F32)).astype(BF)])
    for out in (keep_ref, send_ref):
        out[:, :, 2 * wide :] = jnp.broadcast_to(sums[None], (out.shape[0], *sums.shape))


def qkv_terms(x_index, t_index, z_index, normed, near, far, grads, w_qkv, gain, gain_sum):
    width = normed.shape[1]
    return on_core(
        qkv_terms_kernel,
        (x_index, t_index, z_index, normed, near, far, *grads, w_qkv, gain, gain_sum),
        [shaped(16, width // 64, width)] * 2,
        scratch=[pltpu.VMEM((3 * PAIR, width), F32)],
        smem=3, limit=6, us=BRIEF, name="qkv_terms",
    )


def rest_kernel(a_ref, b_ref, c_ref, d_ref, out_ref):
    rows, lanes = c_ref.shape[1] // 2, 6 * PAIR
    out_ref[:, :QKV_AT, :] = (a_ref[...].astype(F32) + b_ref[...].astype(F32)).astype(BF)
    late = c_ref[...].astype(F32) + d_ref[...].astype(F32)
    out_ref[:, QKV_AT:, :lanes] = late[:, :, :lanes].astype(BF)
    sums = late[:, :rows, lanes:] + late[:, rows:, lanes:]
    high = sums.astype(BF)
    out_ref[:, QKV_AT : QKV_AT + rows, lanes:] = high
    out_ref[:, QKV_AT + rows :, lanes:] = (sums - high.astype(F32)).astype(BF)


def finish_kernel(rest_ref, down_ref, out_ref, qkv_ref, gain_ref):
    count, total, width = rest_ref.shape
    wide, rows = 3 * PAIR, total - QKV_AT

    def added(low, high):
        value = rest_ref[0, low:high, :].astype(F32)
        for source in range(1, count):
            value += rest_ref[source, low:high, :].astype(F32)
        return value

    down_ref[...] = added(0, OUT_AT)[:DOWN_ROWS]
    out_ref[...] = added(OUT_AT, QKV_AT)
    gains = jnp.zeros((rows, width - 2 * wide), F32)
    for x in range(RING):
        value = rest_ref[x, QKV_AT:, :].astype(F32)
        for source in range(x + RING, count, RING):
            value += rest_ref[source, QKV_AT:, :].astype(F32)
        for half in range(2):
            for c in range(3):
                low = half * wide + c * PAIR
                qkv_ref[c, half * rows : (half + 1) * rows, x * PAIR : (x + 1) * PAIR] = value[
                    :, low : low + PAIR
                ]
        gains += value[:, 2 * wide :]
    gains = gains[: rows // 2] + gains[rows // 2 :]
    for index in range(rows // 2):
        low = index % 4 * 256
        gain_ref[index // 4 : index // 4 + 1, low : low + 256] = gains[index : index + 1]


def finish(rest):
    width = rest.shape[2]
    rows = 2 * (rest.shape[1] - QKV_AT)
    return on_core(
        finish_kernel,
        (rest,),
        [
            shaped(DOWN_ROWS, width, dtype=F32),
            shaped(QKV_AT - OUT_AT, width, dtype=F32),
            shaped(3, rows, RING * PAIR, dtype=F32),
            shaped(2, width, dtype=F32),
        ],
        limit=4, us=BRIEF, name="finish",
    )


def rest_sum(early, early_got, late, late_got, waits=()):
    count, _, width = early.shape
    first = pl.BlockSpec((count // 4, QKV_AT, width), lambda i: (i, 0, 0))
    second = pl.BlockSpec((count // 4, *late.shape[1:]), lambda i: (i, 0, 0))
    total = QKV_AT + late.shape[1]

    def body(*refs):
        rest_kernel(*refs[:4], refs[-1])

    return pl.pallas_call(
        body,
        grid=(4,),
        in_specs=[first, first, second, second] + [pl.BlockSpec(memory_space=pl.ANY)] * len(waits),
        out_specs=pl.BlockSpec((count // 4, total, width), lambda i: (i, 0, 0)),
        out_shape=shaped(count, total, width),
        compiler_params=pltpu.CompilerParams(vmem_limit_bytes=8 * 2**20),
        cost_estimate=lasting(BRIEF),
        name="rest_sum",
    )(early, early_got, late, late_got, *waits)


def first_visible(ends_ref, places):
    start = jnp.zeros_like(places)
    for index in range(4):
        start = jnp.where(places >= ends_ref[index], ends_ref[index], start)
    return start


def attend_kernel(x_ref, ends_ref, m0, m1, m2, m3, o0, o1, o2, o3, lse_ref, out_t, keys, query_t,
                  value_t, totals):
    x = x_ref[0]
    lanes = lax.broadcasted_iota(jnp.int32, (BLOCK, PAIR), 1)
    for shift, message in enumerate((m0, m1, m2, m3)):
        source = lax.rem(x + RING - shift, RING)
        for part in range(4):
            at = pl.ds(pl.multiple_of(place_block(source, part) * BLOCK, BLOCK), BLOCK)
            inside = slice(part * BLOCK, (part + 1) * BLOCK)
            block = message[1, inside, :]
            keys[0, at, :] = jnp.where(lanes < HD, block, jnp.zeros_like(block))
            keys[1, at, :] = jnp.where(lanes < HD, jnp.zeros_like(block), block)
            query_t[:, at] = message[0, inside, :].T
            value_t[:, at] = message[2, inside, :].T

    places = lax.broadcasted_iota(jnp.int32, (1, LEN), 1)
    start = first_visible(ends_ref, places)
    out_t[...] = jnp.zeros_like(out_t)
    lse_ref[...] = jnp.full_like(lse_ref, NEGATIVE)
    totals[...] = jnp.zeros_like(totals)
    for low in range(0, LEN, KEYS):
        k_at, q_at = slice(low, low + KEYS), slice(low, LEN)
        key_places = low + lax.broadcasted_iota(jnp.int32, (KEYS, LEN - low), 0)
        visible = (key_places >= start[:, q_at]) & (key_places <= places[:, q_at])
        for head in range(2):
            row, part = slice(head, head + 1), slice(head * HD, (head + 1) * HD)
            scores = jnp.dot(keys[head, k_at, :], query_t[:, q_at], preferred_element_type=F32)
            scores = jnp.where(visible, scores, NEGATIVE)
            highest = lse_ref[row, q_at]
            higher = jnp.maximum(highest, jnp.max(scores, axis=0, keepdims=True))
            shrink = jnp.exp(highest - higher)
            weight = jnp.exp(scores - higher)
            lse_ref[row, q_at] = higher
            totals[row, q_at] = totals[row, q_at] * shrink + jnp.sum(weight, axis=0, keepdims=True)
            out_t[part, q_at] = out_t[part, q_at] * shrink + jnp.dot(
                value_t[part, k_at], weight.astype(BF), preferred_element_type=F32
            )
    for head in range(2):
        row, part = slice(head, head + 1), slice(head * HD, (head + 1) * HD)
        out_t[part, :] = out_t[part, :] / totals[row, :]
        lse_ref[row, :] = lse_ref[row, :] + jnp.log(totals[row, :])
    for shift, out in enumerate((o0, o1, o2, o3)):
        source = lax.rem(x + RING - shift, RING)
        for part in range(4):
            at = pl.ds(pl.multiple_of(place_block(source, part) * BLOCK, BLOCK), BLOCK)
            out[part * BLOCK : (part + 1) * BLOCK, :] = out_t[:, at].T.astype(BF)


def attend(x_index, ends, messages, waits=()):
    rows = messages[0].shape[1]
    return on_core(
        attend_kernel,
        (x_index, ends, *messages),
        [shaped(rows, PAIR)] * 4 + [shaped(2, LEN, dtype=F32), shaped(PAIR, LEN, dtype=F32)],
        scratch=[
            pltpu.VMEM((2, LEN, PAIR), BF),
            pltpu.VMEM((PAIR, LEN), BF),
            pltpu.VMEM((PAIR, LEN), BF),
            pltpu.VMEM((2, LEN), F32),
        ],
        smem=2, waits=waits, limit=12, us=11, name="attend",
    )


def attend_back_kernel(x_ref, ends_ref, mix_ref, m0, m1, m2, m3, d0, d1, d2, d3, lse_ref, out_t,
                       dv1_ref, cos_ref, sin_ref, g0, g1, g2, g3, dv_ref, keys, values, queries, grads,
                       key_t, query_t, grad_t, delta, grad_k, grad_v, grad_q_t):
    x = x_ref[0]
    lanes = lax.broadcasted_iota(jnp.int32, (BLOCK, PAIR), 1)
    for shift, (message, arrived) in enumerate(((m0, d0), (m1, d1), (m2, d2), (m3, d3))):
        source = lax.rem(x + RING - shift, RING)
        for part in range(4):
            at = pl.ds(pl.multiple_of(place_block(source, part) * BLOCK, BLOCK), BLOCK)
            inside = slice(part * BLOCK, (part + 1) * BLOCK)
            query, key, value = message[0, inside, :], message[1, inside, :], message[2, inside, :]
            grad = arrived[inside, :]
            zero = jnp.zeros_like(query)
            for both, block in ((keys, key), (values, value), (queries, query), (grads, grad)):
                both[0, at, :] = jnp.where(lanes < HD, block, zero)
                both[1, at, :] = jnp.where(lanes < HD, zero, block)
            key_t[:, at] = key.T
            query_t[:, at] = query.T
            turned_grad = grad.T
            grad_t[:, at] = turned_grad
            product = out_t[:, at] * turned_grad.astype(F32)
            delta[0:1, at] = jnp.sum(product[:HD], axis=0, keepdims=True)
            delta[1:2, at] = jnp.sum(product[HD:], axis=0, keepdims=True)
    grad_q_t[...] = jnp.zeros_like(grad_q_t)
    places = lax.broadcasted_iota(jnp.int32, (1, LEN), 1)
    start = first_visible(ends_ref, places)
    for low in range(0, LEN, BACK_KEYS):
        k_at, q_at = slice(low, low + BACK_KEYS), slice(low, LEN)
        key_places = low + lax.broadcasted_iota(jnp.int32, (BACK_KEYS, LEN - low), 0)
        visible = (key_places >= start[:, q_at]) & (key_places <= places[:, q_at])
        sum_k = sum_v = jnp.zeros((BACK_KEYS, PAIR), F32)
        for head in range(2):
            row, part = slice(head, head + 1), slice(head * HD, (head + 1) * HD)
            scores = jnp.dot(keys[head, k_at, :], query_t[:, q_at], preferred_element_type=F32)
            weight = jnp.exp(jnp.where(visible, scores, NEGATIVE) - lse_ref[row, q_at])
            grad_w = jnp.dot(values[head, k_at, :], grad_t[:, q_at], preferred_element_type=F32)
            grad_s = (weight * (grad_w - delta[row, q_at])).astype(BF)
            sum_v += jnp.dot(weight.astype(BF), grads[head, q_at, :], preferred_element_type=F32)
            sum_k += jnp.dot(grad_s, queries[head, q_at, :], preferred_element_type=F32)
            grad_q_t[part, q_at] += jnp.dot(key_t[part, k_at], grad_s, preferred_element_type=F32)
        grad_k[k_at, :] = sum_k
        grad_v[k_at, :] = sum_v
    for shift, out in enumerate((g0, g1, g2, g3)):
        source = lax.rem(x + RING - shift, RING)
        for part in range(4):
            at = pl.ds(pl.multiple_of(place_block(source, part) * BLOCK, BLOCK), BLOCK)
            inside = slice(part * BLOCK, (part + 1) * BLOCK)
            cosine, sine = cos_ref[at, :], sin_ref[at, :]
            grad_q = grad_q_t[:, at].T * HD ** (-0.5)
            out[0, inside, :] = turned(grad_q, cosine, sine, -1.0).astype(BF)
            out[1, inside, :] = turned(grad_k[at, :], cosine, sine, -1.0).astype(BF)
            grad_value = mix_ref[0] * grad_v[at, :] + mix_ref[1] * dv1_ref[shift, inside, :].astype(F32)
            out[2, inside, :] = grad_value.astype(BF)
            dv_ref[shift, inside, :] = grad_value.astype(BF)


def attend_back(x_index, ends, mix, messages, arrived, lse, out_t, dv1, cosine, sine, waits=(), us=18):
    rows = messages[0].shape[1]
    return on_core(
        attend_back_kernel,
        (x_index, ends, mix, *messages, *arrived, lse, out_t, dv1, cosine, sine),
        [shaped(3, rows, PAIR)] * 4 + [shaped(RING, rows, PAIR)],
        scratch=[pltpu.VMEM((2, LEN, PAIR), BF)] * 4
        + [pltpu.VMEM((PAIR, LEN), BF)] * 3
        + [
            pltpu.VMEM((2, LEN), F32),
            pltpu.VMEM((LEN, PAIR), F32),
            pltpu.VMEM((LEN, PAIR), F32),
            pltpu.VMEM((PAIR, LEN), F32),
        ],
        smem=3, waits=waits, limit=17, us=us, name="attend_back",
    )


def out_and_back(values, sign):
    return [values[0]] + [moved(values[shift], "x", sign * shift) for shift in range(1, RING)]


def groups(kinds):
    found = {}
    for index in range(32):
        place = {"y": index // 8, "z": index // 4 % 2, "x": index % 4}
        found.setdefault(tuple(place[k] for k in "yzx" if k not in kinds), []).append(index)
    return list(found.values())


def all_to_all(value, kinds):
    return lax.all_to_all(value, "dp", 0, 0, axis_index_groups=groups(kinds))


def per_device(tokens, cotangent, doc_lengths, gains, wqkv, wo, wgu, wd):
    first = lax.axis_index("section") == 0
    tensor = lax.axis_index("tensor")
    position = lax.axis_index("dp")
    y, z, x = position // 8, position // 4 % 2, position % 4
    x_index, z_index, t_index = [v.astype(jnp.int32).reshape(1) for v in (x, z, tensor)]
    width = tokens.shape[2]

    def in_order(keep, got):
        got = got.astype(keep.dtype)
        return jnp.where(z == 0, jnp.stack([keep, got]), jnp.stack([got, keep]))

    def regrouped(pair):
        keep = lax.dynamic_index_in_dim(pair, z, 0, keepdims=False)
        send = lax.dynamic_index_in_dim(pair, 1 - z, 0, keepdims=False)
        return in_order(keep, moved(send.astype(BF), "z", 1))

    lens = lax.dynamic_slice(doc_lengths, (z, y, 0), (1, 1, 4))
    ends = jnp.cumsum(lens.reshape(4), dtype=jnp.int32)
    cosine, sine = rotary_tables()
    own_cosine, own_sine = [
        jnp.concatenate(
            [
                lax.dynamic_slice_in_dim(table, place_block(x, part) * BLOCK, BLOCK, 0)
                for part in range(4)
            ]
        )
        for table in (cosine, sine)
    ]
    w_qkv = jnp.transpose(wqkv[0], (1, 0, 2))
    w_out, w_down = wo[0], wd[0]
    gain_one, gain_two = gains[0, 0:1], gains[0, 1:2]
    mix = jnp.where(first, jnp.array([1.0, 0.0], F32), jnp.array([0.5, 0.5], F32))
    mix_back = jnp.where(first, jnp.array([1.0, 1.0], F32), jnp.array([0.5, 0.0], F32))

    def handed(value, pairs):
        return lax.ppermute(value, "section", pairs)

    def first_half(own, value_first):
        *messages, normed, value, hidden, zero = project(
            x_index, t_index, mix, own, swapped(own), gain_one, w_qkv, value_first, own_cosine, own_sine
        )
        return out_and_back(messages, 1), normed, value, hidden, zero

    def second_half(hidden, outs, value, save, waits=()):
        attended, part, value = branch(x_index, out_and_back(outs, -1), w_out, value, waits=waits)
        mine, keep, send, normed_two, *more = feed(
            t_index, hidden, part, swapped(part), gain_two, w_gu, w_down, save
        )
        return mine, keep, swapped(send), value, (attended, normed_two, *more)

    own_rows = regrouped(tokens).reshape(2 * BLOCK, width)
    no_value = jnp.zeros((RING, 4 * BLOCK, PAIR), BF)

    messages, _, value, hidden, zero = first_half(own_rows, no_value)
    w_gu = jnp.transpose(wgu[0] + zero[0, 0], (1, 0, 2))
    *outs, _, _ = attend(x_index, ends, messages, waits=(seen(w_gu),))
    cot_keep, cot_send = pick(z_index, cotangent, waits=(seen(outs[0]),))
    top_grad = in_order(cot_keep, moved(cot_send, "z", 1)).reshape(2 * BLOCK, width)
    mine, keep, got, value, _ = second_half(hidden, outs, value, False)
    v_in = handed(value, [(0, 1)])
    result = close(mine, keep, got, waits=(seen(v_in),))
    own = jnp.where(first, own_rows, handed(result, [(0, 1)]))

    messages, normed, value, hidden, _ = first_half(own, v_in)
    *outs, lse, out_t = attend(x_index, ends, messages)
    mine, keep, got, _, saved = second_half(hidden, outs, value, True, waits=(seen(top_grad),))
    attended, normed_two, middle, gate, up, act = saved
    def first_back(own_grad, us=7):
        return feed_back(t_index, own_grad, swapped(own_grad), w_gu, w_down, gate, up, us=us)

    def second_back(grad, part, waits=(), us=2.3):
        grad_middle, grad_branch, *sends, gain_sum = middle_back(
            x_index, t_index, grad, middle, part, swapped(part), gain_two, w_out, waits=waits, us=us
        )
        return grad_middle, grad_branch, out_and_back(sends, 1), gain_sum

    def third_back(arrived, grad_value, waits=(), us=20):
        return attend_back(
            x_index, ends, mix_back, messages, arrived, lse, out_t, grad_value, cosine, sine, waits=waits, us=us
        )

    def fourth_back(grads, grad_middle, waits=(), us=2):
        keep, send = project_back(
            x_index, t_index, out_and_back(grads, -1), w_qkv, waits=waits, us=us
        )
        return *input_back(
            t_index, own, grad_middle, keep, swapped(send), gain_one, normed, us=us
        ), keep

    _, _, part, grad = first_back(top_grad)
    grad_middle, _, arrived, _ = second_back(grad, part)
    *grads, grad_value = third_back(arrived, no_value)
    gv_in = handed(grad_value, [(1, 0)])
    _, grad_hidden, half, _ = fourth_back(
        grads, grad_middle, waits=(seen(gv_in),)
    )
    near = lax.all_gather(half, "dp", axis_index_groups=groups("x"))
    own_grad = jnp.where(first, handed(grad_hidden, [(1, 0)]), top_grad)

    dgate, dup, part, grad_out = first_back(own_grad, us=BRIEF)
    grad_middle, grad_branch, arrived, gain_sum = second_back(grad_out, part, us=BRIEF)
    feed_term = feed_terms(normed_two, dgate, dup, waits=(seen(grad_branch),))
    feed_sum = lax.psum_scatter(
        feed_term, "dp", scatter_dimension=0, axis_index_groups=groups("y"), tiled=True
    )
    early, early_send = early_terms(z_index, act, grad_out, attended, grad_branch)
    early_got = moved(early_send, "z", 1)
    far = swapped(near)
    *grads, _ = third_back(arrived, gv_in, waits=(seen(far), seen(early), seen(feed_term)), us=BRIEF)
    late, late_send = qkv_terms(
        x_index, t_index, z_index, normed, near, far, grads, w_qkv, gain_one, gain_sum
    )
    late_got = moved(late_send, "z", 1)
    grad_hidden, _, _, last = fourth_back(grads, grad_middle, waits=(seen(late),), us=BRIEF)
    rest = rest_sum(early, early_got, late, late_got, waits=(seen(last),))
    dins = regrouped(grad_hidden.reshape(2, BLOCK, width))[None]
    result = close(mine, keep, got, waits=(seen(last),))
    acts = regrouped(result.reshape(2, BLOCK, width))[None]
    feed_sum = summed([feed_sum], waits=(seen(rest), seen(dins[0, 0]), seen(acts[0, 0])))
    feed_share = jnp.sum(all_to_all(feed_sum, "zx").astype(F32), axis=0)
    feed_share = feed_share.reshape(2, width // 32, -1)
    down_share, out_share, qkv_share, gain_total = finish(all_to_all(rest, "yx"))
    return (
        acts,
        dins,
        jnp.transpose(qkv_share, (1, 0, 2))[None],
        out_share[None],
        jnp.transpose(feed_share, (1, 0, 2))[None],
        down_share[None],
        (gain_total + swapped(gain_total))[None],
    )


def solution(mesh):
    placed = (
        P(None, ("tensor", "dp"), None),
        P(None, ("tensor", "dp"), None),
        P(),
        P("section", None, None),
        P("section", None, None, "tensor"),
        P("section", "tensor", None),
        P("section", None, None, "tensor"),
        P("section", "tensor", None),
    )
    return jax.shard_map(
        per_device,
        mesh=mesh,
        in_specs=placed,
        out_specs=(
            P("section", None, ("tensor", "dp"), None),
            P("section", None, ("tensor", "dp"), None),
            P("section", "dp", None, "tensor"),
            P("section", ("tensor", "dp"), None),
            P("section", "dp", None, "tensor"),
            P("section", ("tensor", "dp"), None),
            P("section", None, None),
        ),
        check_vma=False,
    )
```
